256 devices in a mesh: group: 8 (over y, core), dev: 32 (over x, z).
Axes of the slice: x: 4, y: 4, z: 8, core: 2. Of those that a mesh axis runs over, the one named last changes fastest.
Arguments:
- embeddings: bfloat16 [262144, 768], P(('group', 'dev'))
- cluster_ids: int32 [262144], P(('group', 'dev')), may hold values from 0 to 1023, as said below
- sharpness: bfloat16 [1024], replicated, may hold values from 20 to 400
Outputs:
- soft_max: bfloat16 [262144], P(('group', 'dev'))
- neighbour: bfloat16 [262144, 768], P(('group', 'dev'))
The draws below stay inside these ranges and needn't reach their ends.
Inputs may be any that keep to these rules, and one draw needn't show every extreme that they name: `cluster_ids`: on every device, each cluster is named by at most 2 of that device's rows, and some cluster by exactly 2.
All inputs are finite; a program needn't handle non-finite values.
Results may differ from the reference program's by a relative error of at most 0.012.
Values may be sent and summed in bfloat16 or wider, within the bound.
A program may use at most 64 MiB of HBM per device.

```python
import math
import jax
import jax.numpy as jnp
from jax import lax

D = 768
SRC_CAP = 2
CLUSTERS = 1024
ROWS_DEV = 1024
ROWS = 262144


def cluster_layout(key):
    devices = ROWS // ROWS_DEV
    popular = jax.random.randint(jax.random.fold_in(key, 11), (CLUSTERS,), 0, 2 * CLUSTERS)

    def one_device(index):
        local = jax.random.fold_in(key, 1000 + index)
        noise = jax.random.randint(local, (CLUSTERS,), 0, CLUSTERS)
        score = (popular + noise) * CLUSTERS + jnp.arange(CLUSTERS).astype(jnp.int32)
        order = jnp.argsort(-score, stable=True).astype(jnp.int32)
        chosen = jnp.concatenate([order[:3 * CLUSTERS // 4], order[:CLUSTERS // 4]])
        shuffle = jax.random.permutation(jax.random.fold_in(local, 5), CLUSTERS)
        return chosen[shuffle]
    return jax.vmap(one_device)(jnp.arange(devices).astype(jnp.int32)).reshape(ROWS).astype(jnp.int32)


def draw_cluster_ids(key, part):
    return cluster_layout(key)


def draw_embeddings(key, part):
    member_ids = cluster_layout(key)
    key = jax.random.fold_in(key, 3)
    key_centre, key_pull, key_noise = jax.random.split(key, 3)
    centres = jax.random.normal(key_centre, (CLUSTERS, D), jnp.float32)
    pull = jnp.exp(jax.random.uniform(key_pull, (CLUSTERS,), jnp.float32, math.log(0.2), math.log(3.0)))
    noise = jax.random.normal(key_noise, (ROWS, D), jnp.float32)
    values = centres[member_ids] * pull[member_ids][:, None] + noise
    return values.astype(jnp.bfloat16)


def setup_inputs(seed: int = 0) -> dict:
    arg_keys = jax.random.split(jax.random.key(seed), 4)
    return {
        "embeddings": draw_embeddings(jax.random.fold_in(arg_keys[3], 71), 0),
        "cluster_ids": draw_cluster_ids(jax.random.fold_in(arg_keys[3], 71), 0),
        "sharpness": jnp.clip(jnp.exp(jax.random.uniform(arg_keys[2], (CLUSTERS,), jnp.float32, math.log(20.0), math.log(400.0))), 20.0, 400.0).astype(jnp.bfloat16),
    }


def local_slots(ids):
    count = ids.shape[0]
    position = jnp.arange(count).astype(jnp.int32)
    matching = ids[:, None] == ids[None, :]
    before = position[None, :] < position[:, None]
    return lax.optimization_barrier(jnp.sum((matching & before).astype(jnp.int32), axis=1)).astype(jnp.int32)

def cluster_stats(member_rows, sharp_rows):
    features = member_rows.shape[-1]
    span = member_rows.shape[1]
    widened = member_rows.astype(jnp.float32)
    cosine = jnp.einsum('csw,ctw->cst', widened, widened) / features
    present = sharp_rows > 0
    position = jnp.arange(span).astype(jnp.int32)
    diagonal_mask = position[:, None] == position[None, :]
    allowed = present[:, None, :] & (~diagonal_mask)[None]
    scores = sharp_rows[:, :, None] * cosine
    masked = jnp.where(allowed, scores, -jnp.inf)
    highest = jnp.maximum(lax.optimization_barrier(jnp.max(masked, axis=-1)), 0.0)
    exponent = jnp.exp(masked - highest[..., None])
    denominator = jnp.exp(-highest) + lax.optimization_barrier(jnp.sum(exponent, axis=-1))
    divisor = jnp.where(present, sharp_rows, 1.0)
    soft_max = ((highest + jnp.log(denominator)) / divisor).astype(jnp.bfloat16)
    weights = exponent.astype(jnp.bfloat16).astype(jnp.float32)
    summed = jnp.einsum('cst,ctw->csw', weights, widened)
    neighbour = (summed / denominator[..., None]).astype(jnp.bfloat16)
    return (soft_max, neighbour)

def reference(embeddings, cluster_ids, sharpness):
    widened = embeddings.astype(jnp.float32)
    normed = (widened * lax.rsqrt(lax.optimization_barrier(jnp.mean(widened * widened, axis=-1, keepdims=True)) + 1e-06)).astype(jnp.bfloat16)
    devices = ROWS // ROWS_DEV
    ordinal = lax.map(local_slots, cluster_ids.reshape(devices, ROWS_DEV)).reshape(ROWS)
    source = (jnp.arange(ROWS) // ROWS_DEV).astype(jnp.int32)
    span = devices * SRC_CAP
    destination = (cluster_ids * span + source * SRC_CAP + ordinal).astype(jnp.int32)
    padded = jnp.zeros((CLUSTERS * span, D), jnp.bfloat16).at[destination].set(normed).reshape(CLUSTERS, span, D)
    sharp_flat = jnp.zeros((CLUSTERS * span,), jnp.float32).at[destination].set(sharpness[cluster_ids].astype(jnp.float32))
    sharp_flat = sharp_flat.reshape(CLUSTERS, span)

    def settle(pair):
        soft_one, near_one = cluster_stats(pair[0][None], pair[1][None])
        return (soft_one[0], near_one[0])
    soft_all, near_all = lax.map(settle, (padded, sharp_flat))
    soft_max = soft_all.reshape(CLUSTERS * span)[destination]
    neighbour = near_all.reshape(CLUSTERS * span, D)[destination]
    return (soft_max, neighbour)
```

```python
import functools

import jax
import jax.numpy as jnp
from jax import lax
from jax.experimental import pallas as pl
from jax.experimental.pallas import tpu as pltpu
from jax.sharding import PartitionSpec as P

MESH = pl.DeviceIdType.MESH
SRC_CAP = 2
EMPTY = 1024.0
NEGATIVE = -1e30
F32 = jnp.float32
BF16 = jnp.bfloat16


def iota(shape, dim):
    return lax.broadcasted_iota(jnp.int32, shape, dim)


def as_column(row, lanes=128):
    return jnp.transpose(jnp.broadcast_to(row, (lanes, row.shape[1])))


def pack_kernel(ids_ref, x_ref, out_ref, dest_ref, normed):
    step = pl.program_id(0)
    count, features = x_ref.shape
    half = features // 2
    slots = out_ref.shape[0] // 2

    @pl.when(step == 0)
    def _():
        ids = ids_ref[...]
        columns = as_column(ids.astype(F32))
        ordinal = jnp.zeros((1, count), F32)
        for r in range(0, count, 128):
            block = jnp.concatenate([columns[r:r + 128]] * (count // 128), axis=1)
            same = block == ids.astype(F32)
            before = iota((128, count), 0) + r < iota((128, count), 1)
            ordinal += jnp.sum(jnp.where(same & before, 1.0, 0.0), axis=0, keepdims=True)
        dest_ref[...] = ids * SRC_CAP + ordinal.astype(jnp.int32)
        for r in range(0, count, 256):
            wide = x_ref[r:r + 256, :].astype(F32)
            scale = lax.rsqrt(jnp.mean(wide * wide, axis=-1, keepdims=True) + 1e-06)
            normed[r:r + 256, :] = (wide * scale).astype(BF16)

    dest = dest_ref[...]
    hit = jnp.where(iota((slots, count), 0) + step * slots == dest, 1.0, 0.0)
    filled = jnp.sum(hit, axis=1, keepdims=True)
    rows = jnp.dot(hit.astype(BF16), normed[...], preferred_element_type=F32)
    first = jnp.where((iota((slots, 128), 1) == 0) & (filled < 0.5), EMPTY, rows[:, :128])
    left = jnp.concatenate([first, rows[:, 128:half]], axis=1).reshape(slots // 8, 1, 8, half)
    right = rows[:, half:].reshape(slots // 8, 1, 8, half)
    both = jnp.concatenate([left, right], axis=1).reshape(slots * 2, half)
    out_ref[...] = both.astype(BF16)


def pack(ids, x, slots_all):
    count, features = x.shape
    steps = 8
    slots = slots_all // steps
    return pl.pallas_call(
        pack_kernel,
        grid=(steps,),
        in_specs=[
            pl.BlockSpec((1, count), lambda i: (0, 0)),
            pl.BlockSpec((count, features), lambda i: (0, 0)),
        ],
        out_specs=[
            pl.BlockSpec((slots * 2, features // 2), lambda i: (i, 0)),
            pl.BlockSpec((1, count), lambda i: (0, 0)),
        ],
        out_shape=[
            jax.ShapeDtypeStruct((slots_all * 2, features // 2), BF16),
            jax.ShapeDtypeStruct((1, count), jnp.int32),
        ],
        scratch_shapes=[pltpu.VMEM((count, features), BF16)],
        compiler_params=pltpu.CompilerParams(vmem_limit_bytes=32 * 2**20),
        name="pack",
    )(ids, x)


def partner(k, g, d):
    q = (k * 101) % 256
    z = (d % 8 + q % 8) % 8
    x = (d // 8 + (q // 8) % 4) % 4
    y = (g // 2 + (q // 32) % 4) % 4
    core = (g % 2 + q // 128) % 2
    return y * 2 + core, x * 8 + z


def exchange_kernel(n, *refs):
    count = (len(refs) - 3) // 2
    sources, targets = refs[:count], refs[count:2 * count]
    send_sem, recv_sem, own_sem = refs[2 * count:]
    g, d = lax.axis_index("group"), lax.axis_index("dev")
    me = g * 32 + d

    def part(ref, start, blocks):
        size = ref.shape[0] // n
        return ref.at[pl.ds(pl.multiple_of(start * size, size), blocks * size)]

    barrier = pltpu.get_barrier_semaphore()

    def greet(k, carry):
        tg, td = partner(k, g, d)
        pl.semaphore_signal(barrier, inc=1, device_id=(tg, td), device_id_type=MESH)
        return carry

    lax.fori_loop(1, n, greet, 0)
    own = [
        pltpu.make_async_copy(part(s, me, 1), part(t, me, 1), own_sem.at[i])
        for i, (s, t) in enumerate(zip(sources, targets))
    ]
    for copy in own:
        copy.start()
    pl.semaphore_wait(barrier, n - 1)

    def send(k, carry):
        tg, td = partner(k, g, d)
        for i, (s, t) in enumerate(zip(sources, targets)):
            pltpu.make_async_remote_copy(
                src_ref=part(s, tg * 32 + td, 1),
                dst_ref=part(t, me, 1),
                send_sem=send_sem.at[i],
                recv_sem=recv_sem.at[i],
                device_id=(tg, td),
                device_id_type=MESH,
            ).start()
        return carry

    lax.fori_loop(1, n, send, 0)
    for i, (s, t) in enumerate(zip(sources, targets)):
        pltpu.make_async_copy(part(s, 0, n - 1), part(s, 0, n - 1), send_sem.at[i]).wait()
        pltpu.make_async_copy(part(t, 0, n - 1), part(t, 0, n - 1), recv_sem.at[i]).wait()
    for copy in own:
        copy.wait()


def exchange(n, collective_id, *arrays):
    return pl.pallas_call(
        functools.partial(exchange_kernel, n),
        in_specs=[pl.BlockSpec(memory_space=pl.ANY)] * len(arrays),
        out_specs=[pl.BlockSpec(memory_space=pl.ANY)] * len(arrays),
        out_shape=[jax.ShapeDtypeStruct(a.shape, a.dtype) for a in arrays],
        scratch_shapes=[pltpu.SemaphoreType.DMA((len(arrays),))] * 3,
        compiler_params=pltpu.CompilerParams(collective_id=collective_id, has_side_effects=True),
        name="exchange",
    )(*arrays)


def settle_kernel(per_line, sharp_ref, in_ref, out_ref, soft_ref, members, results):
    me = lax.axis_index("group") * 32 + lax.axis_index("dev")
    owned, span, features = members.shape
    half = features // 2
    chunk = 16

    def source_row(o):
        return (o % 32) // 2 * 16 + o // 128 * 8 + (o % 128) // 32 * 2 + o % 2

    inward = jnp.where(source_row(iota((256, 256), 0)) == iota((256, 256), 1), 1.0, 0.0).astype(BF16)
    outward = jnp.where(source_row(iota((256, 256), 1)) == iota((256, 256), 0), 1.0, 0.0).astype(BF16)

    def gather(b, carry):
        arrived = in_ref[pl.ds(pl.multiple_of(b * 256, 256), 256), :]
        placed = jnp.dot(inward, arrived, preferred_element_type=F32).astype(BF16)
        rows = pl.ds(pl.multiple_of(b * 32, 32), 32)
        for c in range(owned):
            members[c, rows, :half] = placed[c * 32:(c + 1) * 32]
            members[c, rows, half:] = placed[128 + c * 32:128 + (c + 1) * 32]
        return carry

    lax.fori_loop(0, span // 32, gather, 0)

    off_diagonal = iota((span, span), 0) != iota((span, span), 1)

    def score(c, soft):
        sharp = sharp_ref[me * owned + c]
        rows = members[c]
        present = rows[:, 0:1].astype(F32) < EMPTY / 2
        dots = lax.dot_general(rows, rows, (((1,), (1,)), ((), ())), preferred_element_type=F32)
        masked = jnp.where(off_diagonal & present, dots * (sharp * (1.0 / features)), NEGATIVE)
        highest = jnp.maximum(jnp.max(masked, axis=0, keepdims=True), 0.0)
        weights = jnp.exp(masked - highest)
        total = jnp.exp(-highest) + jnp.sum(weights, axis=0, keepdims=True)
        soft_row = (highest + jnp.log(total)) / sharp
        scaled = (weights * (1.0 / total)).astype(BF16)
        summed = lax.dot_general(scaled, rows, (((0,), (0,)), ((), ())), preferred_element_type=F32)
        results[c] = summed.astype(BF16)
        source = iota((128, span), 1) // 2
        lane = source % per_line * 8 + 2 * c + iota((128, span), 1) % 2
        return jnp.where(iota((128, span), 0) == lane, soft_row, soft)

    soft = lax.fori_loop(0, owned, score, jnp.zeros((128, span), F32)).astype(BF16)
    lines = soft_ref.shape[0]
    pick = jnp.where(iota((lines, span), 1) // (2 * per_line) == iota((lines, span), 0), 1.0, 0.0).astype(BF16)
    spread = lax.dot_general(pick, soft, (((1,), (1,)), ((), ())), preferred_element_type=F32)
    soft_ref[...] = spread.reshape(soft_ref.shape)

    def scatter(b, carry):
        rows = pl.ds(pl.multiple_of(b * 32, 32), 32)
        placed = jnp.concatenate(
            [results[c, rows, :half] for c in range(owned)] + [results[c, rows, half:] for c in range(owned)],
            axis=0,
        )
        back = jnp.dot(outward, placed, preferred_element_type=F32)
        out_ref[pl.ds(pl.multiple_of(b * 256, 256), 256), :] = back.astype(BF16)
        return carry

    lax.fori_loop(0, span // 32, scatter, 0)


def settle(sharp, arrived, n, owned, per_line):
    rows, half = arrived.shape
    span = n * SRC_CAP
    return pl.pallas_call(
        functools.partial(settle_kernel, per_line),
        in_specs=[pl.BlockSpec(memory_space=pltpu.SMEM), pl.BlockSpec(memory_space=pltpu.VMEM)],
        out_specs=[pl.BlockSpec(memory_space=pltpu.VMEM)] * 2,
        out_shape=[
            jax.ShapeDtypeStruct((rows, half), BF16),
            jax.ShapeDtypeStruct((n // per_line, 1, 128), F32),
        ],
        scratch_shapes=[
            pltpu.VMEM((owned, span, half * 2), BF16),
            pltpu.VMEM((owned, span, half * 2), BF16),
        ],
        compiler_params=pltpu.CompilerParams(vmem_limit_bytes=40 * 2**20),
        name="settle",
    )(sharp, arrived)


def unpack_kernel(dest_ref, in_ref, soft_in_ref, soft_ref, out_ref, combined, soft_all):
    step = pl.program_id(0)
    slots, features = combined.shape
    half = features // 2
    n = soft_in_ref.shape[0]
    rows = out_ref.shape[0]

    @pl.when(step == 0)
    def _():
        def split(b, carry):
            block = in_ref[pl.ds(pl.multiple_of(b * 512, 512), 512), :].astype(F32).reshape(32, 2, 8, half)
            place = pl.ds(pl.multiple_of(b * 256, 256), 256)
            combined[place, :half] = block[:, 0].reshape(256, half).astype(BF16)
            combined[place, half:] = block[:, 1].reshape(256, half).astype(BF16)
            return carry

        lax.fori_loop(0, slots // 256, split, 0)
        soft_all[...] = jnp.transpose(soft_in_ref[...].reshape(n, 128)).astype(BF16)

    dest = dest_ref[...]
    column = as_column(dest.astype(F32))
    lane = iota((rows, 128), 1).astype(F32)
    hit = jnp.concatenate(
        [jnp.where(column == lane + float(s), 1.0, 0.0).astype(BF16) for s in range(0, slots, 128)], axis=1
    )
    out_ref[...] = jnp.dot(hit, combined[...], preferred_element_type=F32).astype(BF16)

    owner = jnp.where(iota((n, rows), 0) == dest // 8, 1.0, 0.0).astype(BF16)
    found = jnp.dot(soft_all[...], owner, preferred_element_type=F32)[:8]
    chosen = jnp.where(iota((8, rows), 0) == dest % 8, found, 0.0)
    soft_ref[...] = jnp.sum(chosen, axis=0, keepdims=True).astype(BF16)


def unpack(dest, returned, soft_returned):
    count = dest.shape[1]
    n = soft_returned.shape[0]
    blocks, half = returned.shape
    slots, features = blocks // 2, half * 2
    rows = 256
    return pl.pallas_call(
        unpack_kernel,
        grid=(count // rows,),
        in_specs=[
            pl.BlockSpec((1, rows), lambda i: (0, i)),
            pl.BlockSpec((blocks, half), lambda i: (0, 0)),
            pl.BlockSpec((n, 1, 128), lambda i: (0, 0, 0)),
        ],
        out_specs=[
            pl.BlockSpec((1, rows), lambda i: (0, i)),
            pl.BlockSpec((rows, features), lambda i: (i, 0)),
        ],
        out_shape=[
            jax.ShapeDtypeStruct((1, count), BF16),
            jax.ShapeDtypeStruct((count, features), BF16),
        ],
        scratch_shapes=[pltpu.VMEM((slots, features), BF16), pltpu.VMEM((128, n), BF16)],
        compiler_params=pltpu.CompilerParams(vmem_limit_bytes=40 * 2**20),
        name="unpack",
    )(dest, returned, soft_returned)


PLANES = 8
LINES = 32
CAP = 160
NT = (((1,), (1,)), ((), ()))
BLOCK = 16


def blocks(ref, start, count):
    return ref.at[pl.ds(pl.multiple_of(start * BLOCK, BLOCK), count * BLOCK)]


def along_z(k):
    near = k // 2 + 1
    return near + (k % 2) * (PLANES - 2 * near)


def place():
    g, d = lax.axis_index("group"), lax.axis_index("dev")
    return g, d // PLANES, d % PLANES


def on_line(j, g, x):
    q = (j * 11) % LINES
    core = (g % 2 + q % 2) % 2
    y = (g // 2 + (q // 2) % 4) % 4
    return y * 2 + core, (x + q // 8) % 4


def greet_all(g, x, z):
    barrier = pltpu.get_barrier_semaphore()

    def greet_z(k, carry):
        there = (g, x * PLANES + (z + k) % PLANES)
        pl.semaphore_signal(barrier, inc=1, device_id=there, device_id_type=MESH)
        return carry

    def greet_line(j, carry):
        tg, tx = on_line(j, g, x)
        pl.semaphore_signal(barrier, inc=1, device_id=(tg, tx * PLANES + z), device_id_type=MESH)
        return carry

    lax.fori_loop(1, PLANES, greet_z, 0)
    lax.fori_loop(1, LINES, greet_line, 0)
    return barrier


def collect_kernel(ids_ref, x_ref, inbox, where_ref, slots_in, normed, hits, rows_out, rows_in, slots_out, line_out,
                   z_send, z_recv, line_send, line_recv, own_sem):
    g, x, z = place()
    count, features = x_ref.shape
    half = features // 2
    barrier = greet_all(g, x, z)

    ids = ids_ref[...]
    columns = as_column(ids.astype(F32)).astype(jnp.int32)
    plane = ids // 4 % PLANES
    ordinal = jnp.zeros((1, count), F32)
    position = jnp.zeros((1, count), F32)
    for r in range(0, count, 128):
        block = jnp.concatenate([columns[r:r + 128]] * (count // 128), axis=1)
        before = iota((128, count), 0) + r < iota((128, count), 1)
        same = (block == ids) & before
        beside = (block // 4 % PLANES == plane) & before
        ordinal += jnp.sum(jnp.where(same, 1.0, 0.0), axis=0, keepdims=True)
        position += jnp.sum(jnp.where(beside, 1.0, 0.0), axis=0, keepdims=True)
    where_ref[...] = jnp.concatenate([plane.astype(F32), position, jnp.zeros((6, count), F32)], axis=0)
    flag = jnp.where(jnp.max(position) > CAP - 0.5, 1.0, 0.0)
    slot = (ids // LINES * 8 + ids % 4 * SRC_CAP).astype(F32) + ordinal + 1.0
    slot = jnp.broadcast_to(slot, (16, count)).astype(BF16)
    for r in range(0, count, 256):
        wide = x_ref[r:r + 256, :].astype(F32)
        scale = lax.rsqrt(jnp.mean(wide * wide, axis=-1, keepdims=True) + 1e-06)
        normed[r:r + 256, :] = (wide * scale).astype(BF16)
    hits[CAP:, :] = jnp.zeros((256 - CAP, count), BF16)
    key = jnp.where(position < CAP - 0.5, position.astype(jnp.int32) * PLANES + plane, -1)

    def compact(there):
        hits[:CAP, :] = jnp.where(iota((CAP, count), 0) * PLANES + there == key, 1.0, 0.0).astype(BF16)
        rows = jnp.dot(hits[:CAP, :], normed[...], preferred_element_type=F32).astype(BF16)
        names = lax.dot_general(slot, hits[...], NT, preferred_element_type=F32)[:1]
        return rows, jnp.where(iota((1, 256), 1) == 255, flag, names)

    def z_copies(there):
        peer = (g, x * PLANES + there)
        return [
            pltpu.make_async_remote_copy(
                src_ref=out.at[there], dst_ref=into.at[z], send_sem=z_send.at[i], recv_sem=z_recv.at[i, z],
                device_id=peer, device_id_type=MESH)
            for i, (out, into) in enumerate([(rows_out, rows_in), (slots_out, slots_in)])
        ]

    def send_z(k, carry):
        there = (z + along_z(k)) % PLANES
        rows, names = compact(there)
        rows_out[there] = rows
        slots_out[there] = names

        @pl.when(k == 0)
        def _():
            pl.semaphore_wait(barrier, PLANES + LINES - 2)

        for copy in z_copies(there):
            copy.start()
        return carry

    lax.fori_loop(0, PLANES - 1, send_z, 0)
    rows, names = compact(z)
    rows_in[z] = rows
    slots_in[z] = names

    def own_copy(source):
        return pltpu.make_async_copy(
            blocks(line_out, source * LINES + g * 4 + x, 1), blocks(inbox, (g * 4 + x) * PLANES + source, 1),
            own_sem.at[source])

    def forward(source):
        names = slots_in[source][:, :CAP].astype(jnp.int32) - 1
        hit = jnp.where(iota((256, CAP), 0) == names, 1.0, 0.0)
        filled = jnp.sum(hit, axis=1, keepdims=True)
        rows = jnp.dot(hit.astype(BF16), rows_in[source], preferred_element_type=F32)
        first = jnp.where((iota((256, 128), 1) == 0) & (filled < 0.5), EMPTY, rows[:, :128])
        left = jnp.concatenate([first, rows[:, 128:half]], axis=1).reshape(LINES, 1, 8, half)
        right = rows[:, half:].reshape(LINES, 1, 8, half)
        both = jnp.concatenate([left, right], axis=1).reshape(512, half)
        line_out[pl.ds(pl.multiple_of(source * 512, 512), 512), :] = both.astype(BF16)
        own_copy(source).start()

        def send(j, carry):
            tg, tx = on_line(j, g, x)
            pltpu.make_async_remote_copy(
                src_ref=blocks(line_out, source * LINES + tg * 4 + tx, 1),
                dst_ref=blocks(inbox, (g * 4 + x) * PLANES + source, 1),
                send_sem=line_send, recv_sem=line_recv,
                device_id=(tg, tx * PLANES + z), device_id_type=MESH).start()
            return carry

        lax.fori_loop(1, LINES, send, 0)

    forward(z)

    def arrive(k, carry):
        source = (z + PLANES - along_z(k)) % PLANES
        pltpu.make_async_copy(rows_in.at[source], rows_in.at[source], z_recv.at[0, source]).wait()
        pltpu.make_async_copy(slots_in.at[source], slots_in.at[source], z_recv.at[1, source]).wait()
        forward(source)
        return carry

    lax.fori_loop(0, PLANES - 1, arrive, 0)
    others = PLANES * (LINES - 1)
    for i, out in enumerate((rows_out, slots_out)):
        sent = out.at[pl.ds(0, PLANES - 1)]
        pltpu.make_async_copy(sent, sent, z_send.at[i]).wait()
    pltpu.make_async_copy(blocks(line_out, 0, others), blocks(line_out, 0, others), line_send).wait()
    pltpu.make_async_copy(blocks(inbox, 0, others), blocks(inbox, 0, others), line_recv).wait()

    def finish(source, carry):
        own_copy(source).wait()
        return carry

    lax.fori_loop(0, PLANES, finish, 0)


def collect(ids, x):
    count, features = x.shape
    half = features // 2
    slots = PLANES * LINES * BLOCK
    vmem = pl.BlockSpec(memory_space=pltpu.VMEM)
    return pl.pallas_call(
        collect_kernel,
        in_specs=[vmem] * 2,
        out_specs=[vmem] * 3,
        out_shape=[
            jax.ShapeDtypeStruct((slots, half), BF16),
            jax.ShapeDtypeStruct((8, count), F32),
            jax.ShapeDtypeStruct((PLANES, 1, 256), F32),
        ],
        scratch_shapes=[
            pltpu.VMEM((count, features), BF16),
            pltpu.VMEM((256, count), BF16),
            pltpu.VMEM((PLANES, CAP, features), BF16),
            pltpu.VMEM((PLANES, CAP, features), BF16),
            pltpu.VMEM((PLANES, 1, 256), F32),
            pltpu.VMEM((slots, half), BF16),
            pltpu.SemaphoreType.DMA((2,)),
            pltpu.SemaphoreType.DMA((2, PLANES)),
            pltpu.SemaphoreType.DMA,
            pltpu.SemaphoreType.DMA,
            pltpu.SemaphoreType.DMA((PLANES,)),
        ],
        compiler_params=pltpu.CompilerParams(
            collective_id=2, has_side_effects=True, vmem_limit_bytes=40 * 2**20),
        name="collect",
    )(ids, x)


def restore_kernel(results, soft_ref, slots_ref, rows_back, soft_back, flag_ref, line_in, soft_out, soft_in, rows_out,
                   names_out, z_send, z_recv, line_send, line_recv, soft_sem, own_sem):
    g, x, z = place()
    me = g * 4 + x
    half = results.shape[1]
    barrier = greet_all(g, x, z)
    flag = jnp.max(jnp.where(iota((PLANES, 1, 256), 2) == 255, slots_ref[...], 0.0))
    soft_out[...] = jnp.where(iota(soft_out.shape, 2) < 64, soft_ref[...], flag)
    soft_in[me] = soft_out[me]
    pl.semaphore_wait(barrier, PLANES + LINES - 2)

    def send_soft(j, carry):
        tg, tx = on_line(j, g, x)
        pltpu.make_async_remote_copy(
            src_ref=soft_out.at[tg * 4 + tx], dst_ref=soft_in.at[me], send_sem=soft_sem.at[0],
            recv_sem=soft_sem.at[1], device_id=(tg, tx * PLANES + z), device_id_type=MESH).start()
        return carry

    lax.fori_loop(1, LINES, send_soft, 0)

    def own_copy(home):
        return pltpu.make_async_copy(
            blocks(results, me * PLANES + home, 1), blocks(line_in, home * LINES + me, 1), own_sem.at[home])

    def home_of(k):
        return (z + along_z(k) * (1 - k // (PLANES - 1))) % PLANES

    def send_line(k, carry):
        home = home_of(k)
        own_copy(home).start()

        def send(j, inner):
            tg, tx = on_line(j, g, x)
            pltpu.make_async_remote_copy(
                src_ref=blocks(results, (tg * 4 + tx) * PLANES + home, 1),
                dst_ref=blocks(line_in, home * LINES + me, 1),
                send_sem=line_send, recv_sem=line_recv.at[home],
                device_id=(tg, tx * PLANES + z), device_id_type=MESH).start()
            return inner

        return lax.fori_loop(1, LINES, send, carry)

    lax.fori_loop(0, PLANES, send_line, 0)
    first = soft_in.at[pl.ds(0, LINES - 1)]
    pltpu.make_async_copy(first, first, soft_sem.at[1]).wait()
    all_soft = soft_in[...].reshape(LINES, 128)
    flag_ref[...] = jnp.broadcast_to(jnp.max(all_soft[:, 64:], axis=(0, 1), keepdims=True), flag_ref.shape)
    spread = jnp.where(iota((256, LINES), 0) // 8 == iota((256, LINES), 1), 1.0, 0.0).astype(BF16)
    all_soft = jnp.dot(spread, all_soft.astype(BF16), preferred_element_type=F32)

    def settle_home(home):
        arrived = blocks(line_in, home * LINES, LINES - 1)
        pltpu.make_async_copy(arrived, arrived, line_recv.at[home]).wait()
        own_copy(home).wait()
        both = line_in[pl.ds(pl.multiple_of(home * 512, 512), 512), :].astype(F32).reshape(LINES, 2, 8, half)
        left, right = both[:, 0].reshape(256, half).astype(BF16), both[:, 1].reshape(256, half).astype(BF16)
        names = slots_ref[home]
        column = as_column(names)[:CAP] - 1.0
        lane = iota((CAP, 128), 1).astype(F32)
        hit = jnp.concatenate(
            [jnp.where(column == lane + float(s), 1.0, 0.0).astype(BF16) for s in (0, 128)], axis=1)
        mine = jnp.where(iota((256, 128), 1) == home * 8 + iota((256, 128), 0) % 8, all_soft, 0.0).astype(BF16)
        values = lax.dot_general(jnp.ones((16, 128), BF16), mine, NT, preferred_element_type=F32)
        picked = jnp.where(iota((256, 256), 0) == names.astype(jnp.int32) - 1, 1.0, 0.0).astype(BF16)
        picked = jnp.dot(values.astype(BF16), picked, preferred_element_type=F32)[:1]
        left = jnp.dot(hit, left, preferred_element_type=F32).astype(BF16)
        right = jnp.dot(hit, right, preferred_element_type=F32).astype(BF16)
        return left, right, picked

    def send_z(k, carry):
        home = home_of(k)
        left, right, picked = settle_home(home)
        rows_out[home, :, :half] = left
        rows_out[home, :, half:] = right
        names_out[home] = picked
        for i, (out, into) in enumerate([(rows_out, rows_back), (names_out, soft_back)]):
            pltpu.make_async_remote_copy(
                src_ref=out.at[home], dst_ref=into.at[z], send_sem=z_send.at[i], recv_sem=z_recv.at[i],
                device_id=(g, x * PLANES + home), device_id_type=MESH).start()
        return carry

    lax.fori_loop(0, PLANES - 1, send_z, 0)
    left, right, picked = settle_home(z)
    rows_back[z, :, :half] = left
    rows_back[z, :, half:] = right
    soft_back[z] = picked

    others = PLANES * (LINES - 1)
    sent = soft_out.at[pl.ds(0, LINES - 1)]
    pltpu.make_async_copy(sent, sent, soft_sem.at[0]).wait()
    pltpu.make_async_copy(blocks(results, 0, others), blocks(results, 0, others), line_send).wait()
    for i, (out, into) in enumerate([(rows_out, rows_back), (names_out, soft_back)]):
        sent, came = out.at[pl.ds(0, PLANES - 1)], into.at[pl.ds(0, PLANES - 1)]
        pltpu.make_async_copy(sent, sent, z_send.at[i]).wait()
        pltpu.make_async_copy(came, came, z_recv.at[i]).wait()


def restore(results, soft, slots):
    rows, half = results.shape
    vmem = pl.BlockSpec(memory_space=pltpu.VMEM)
    return pl.pallas_call(
        restore_kernel,
        in_specs=[vmem] * 3,
        out_specs=[vmem] * 3,
        out_shape=[
            jax.ShapeDtypeStruct((PLANES, CAP, half * 2), BF16),
            jax.ShapeDtypeStruct((PLANES, 1, 256), F32),
            jax.ShapeDtypeStruct((8, 128), F32),
        ],
        scratch_shapes=[
            pltpu.VMEM((rows, half), BF16),
            pltpu.VMEM((LINES, 1, 128), F32),
            pltpu.VMEM((LINES, 1, 128), F32),
            pltpu.VMEM((PLANES, CAP, half * 2), BF16),
            pltpu.VMEM((PLANES, 1, 256), F32),
            pltpu.SemaphoreType.DMA((2,)),
            pltpu.SemaphoreType.DMA((2,)),
            pltpu.SemaphoreType.DMA,
            pltpu.SemaphoreType.DMA((PLANES,)),
            pltpu.SemaphoreType.DMA((2,)),
            pltpu.SemaphoreType.DMA((PLANES,)),
        ],
        compiler_params=pltpu.CompilerParams(
            collective_id=3, has_side_effects=True, vmem_limit_bytes=40 * 2**20),
        name="restore",
    )(results, soft, slots)


def place_kernel(where_ref, in_ref, soft_in_ref, soft_ref, out_ref):
    rows = out_ref.shape[0]
    plane, position = where_ref[0:1, :], where_ref[1:2, :]
    column = as_column(plane * CAP + position)
    lane = iota((rows, 128), 1).astype(F32)
    hit = jnp.concatenate(
        [jnp.where(column == lane + float(s), 1.0, 0.0).astype(BF16) for s in range(0, PLANES * CAP, 128)], axis=1)
    combined = in_ref[...].reshape(PLANES * CAP, in_ref.shape[2])
    out_ref[...] = jnp.dot(hit, combined, preferred_element_type=F32).astype(BF16)

    spot = jnp.where(iota((256, rows), 0).astype(F32) == position, 1.0, 0.0).astype(BF16)
    soft = soft_in_ref[...].reshape(PLANES, 256)
    soft = jnp.concatenate([soft, jnp.zeros((8, 256), F32)], axis=0).astype(BF16)
    found = jnp.dot(soft, spot, preferred_element_type=F32)[:PLANES]
    chosen = jnp.where(iota((PLANES, rows), 0).astype(F32) == plane, found, 0.0)
    soft_ref[...] = jnp.sum(chosen, axis=0, keepdims=True).astype(BF16)


def put_in_place(where, returned, soft_returned):
    count = where.shape[1]
    planes, cap, features = returned.shape
    rows = 256
    return pl.pallas_call(
        place_kernel,
        grid=(count // rows,),
        in_specs=[
            pl.BlockSpec((8, rows), lambda i: (0, i)),
            pl.BlockSpec((planes, cap, features), lambda i: (0, 0, 0)),
            pl.BlockSpec((planes, 1, 256), lambda i: (0, 0, 0)),
        ],
        out_specs=[
            pl.BlockSpec((1, rows), lambda i: (0, i)),
            pl.BlockSpec((rows, features), lambda i: (i, 0)),
        ],
        out_shape=[
            jax.ShapeDtypeStruct((1, count), BF16),
            jax.ShapeDtypeStruct((count, features), BF16),
        ],
        compiler_params=pltpu.CompilerParams(vmem_limit_bytes=32 * 2**20),
        name="put_in_place",
    )(where, returned, soft_returned)


def by_all_slots(n, embeddings, cluster_ids, sharp):
    clusters = sharp.shape[0]
    outbox, dest = pack(cluster_ids[None, :], embeddings, clusters * SRC_CAP)
    (arrived,) = exchange(n, 0, outbox)
    results, soft = settle(sharp, arrived, n, clusters // n, 1)
    returned, soft_returned = exchange(n, 1, results, soft)
    return unpack(dest, returned, soft_returned)


def body(n, embeddings, cluster_ids, sharpness):
    sharp = sharpness.astype(F32)
    arrived, where, slots = collect(cluster_ids[None, :], embeddings)
    results, soft = settle(sharp, arrived, n, sharp.shape[0] // n, PLANES)
    returned, soft_returned, flag = restore(results, soft, slots)
    soft_max, neighbour = put_in_place(where, returned, soft_returned)
    soft_max, neighbour = lax.cond(
        flag[0, 0] > 0.5,
        lambda: tuple(by_all_slots(n, embeddings, cluster_ids, sharp)),
        lambda: (soft_max, neighbour),
    )
    return (soft_max[0], neighbour)


def solution(mesh):
    n = mesh.size
    return jax.shard_map(
        functools.partial(body, n),
        mesh=mesh,
        in_specs=(P(("group", "dev"), None), P(("group", "dev")), P()),
        out_specs=(P(("group", "dev")), P(("group", "dev"), None)),
        check_vma=False,
    )
```

```python
import functools

import jax
import jax.numpy as jnp
from jax import lax
from jax.experimental import pallas as pl
from jax.experimental.pallas import tpu as pltpu
from jax.sharding import PartitionSpec as P

MESH = pl.DeviceIdType.MESH
SRC_CAP = 2
EMPTY = 1024.0
NEGATIVE = -1e30
NT = (((1,), (1,)), ((), ()))
F32 = jnp.float32
BF16 = jnp.bfloat16


def iota(shape, dim):
    return lax.broadcasted_iota(jnp.int32, shape, dim)


def as_column(row, lanes=128):
    return jnp.transpose(jnp.broadcast_to(row, (lanes, row.shape[1])))


def pack_kernel(ids_ref, x_ref, out_ref, dest_ref, normed):
    step = pl.program_id(0)
    count, features = x_ref.shape
    half = features // 2
    slots = out_ref.shape[0] // 2

    @pl.when(step == 0)
    def _():
        ids = ids_ref[...]
        columns = as_column(ids.astype(F32))
        ordinal = jnp.zeros((1, count), F32)
        for r in range(0, count, 128):
            block = jnp.concatenate([columns[r:r + 128]] * (count // 128), axis=1)
            same = block == ids.astype(F32)
            before = iota((128, count), 0) + r < iota((128, count), 1)
            ordinal += jnp.sum(jnp.where(same & before, 1.0, 0.0), axis=0, keepdims=True)
        dest_ref[...] = ids * SRC_CAP + ordinal.astype(jnp.int32)
        for r in range(0, count, 256):
            wide = x_ref[r:r + 256, :].astype(F32)
            scale = lax.rsqrt(jnp.mean(wide * wide, axis=-1, keepdims=True) + 1e-06)
            normed[r:r + 256, :] = (wide * scale).astype(BF16)

    dest = dest_ref[...]
    hit = jnp.where(iota((slots, count), 0) + step * slots == dest, 1.0, 0.0)
    filled = jnp.sum(hit, axis=1, keepdims=True)
    rows = jnp.dot(hit.astype(BF16), normed[...], preferred_element_type=F32)
    first = jnp.where((iota((slots, 128), 1) == 0) & (filled < 0.5), EMPTY, rows[:, :128])
    left = jnp.concatenate([first, rows[:, 128:half]], axis=1).reshape(slots // 8, 1, 8, half)
    right = rows[:, half:].reshape(slots // 8, 1, 8, half)
    both = jnp.concatenate([left, right], axis=1).reshape(slots * 2, half)
    out_ref[...] = both.astype(BF16)


def pack(ids, x, slots_all):
    count, features = x.shape
    steps = 8
    slots = slots_all // steps
    return pl.pallas_call(
        pack_kernel,
        grid=(steps,),
        in_specs=[
            pl.BlockSpec((1, count), lambda i: (0, 0)),
            pl.BlockSpec((count, features), lambda i: (0, 0)),
        ],
        out_specs=[
            pl.BlockSpec((slots * 2, features // 2), lambda i: (i, 0)),
            pl.BlockSpec((1, count), lambda i: (0, 0)),
        ],
        out_shape=[
            jax.ShapeDtypeStruct((slots_all * 2, features // 2), BF16),
            jax.ShapeDtypeStruct((1, count), jnp.int32),
        ],
        scratch_shapes=[pltpu.VMEM((count, features), BF16)],
        compiler_params=pltpu.CompilerParams(vmem_limit_bytes=32 * 2**20),
        name="pack",
    )(ids, x)


def partner(k, g, d):
    q = (k * 101) % 256
    z = (d % 8 + q % 8) % 8
    x = (d // 8 + (q // 8) % 4) % 4
    y = (g // 2 + (q // 32) % 4) % 4
    core = (g % 2 + q // 128) % 2
    return y * 2 + core, x * 8 + z


def exchange_kernel(n, *refs):
    count = (len(refs) - 3) // 2
    sources, targets = refs[:count], refs[count:2 * count]
    send_sem, recv_sem, own_sem = refs[2 * count:]
    g, d = lax.axis_index("group"), lax.axis_index("dev")
    me = g * 32 + d

    def part(ref, start, blocks):
        size = ref.shape[0] // n
        return ref.at[pl.ds(pl.multiple_of(start * size, size), blocks * size)]

    barrier = pltpu.get_barrier_semaphore()

    def greet(k, carry):
        tg, td = partner(k, g, d)
        pl.semaphore_signal(barrier, inc=1, device_id=(tg, td), device_id_type=MESH)
        return carry

    lax.fori_loop(1, n, greet, 0)
    own = [
        pltpu.make_async_copy(part(s, me, 1), part(t, me, 1), own_sem.at[i])
        for i, (s, t) in enumerate(zip(sources, targets))
    ]
    for copy in own:
        copy.start()
    pl.semaphore_wait(barrier, n - 1)

    def send(k, carry):
        tg, td = partner(k, g, d)
        for i, (s, t) in enumerate(zip(sources, targets)):
            pltpu.make_async_remote_copy(
                src_ref=part(s, tg * 32 + td, 1),
                dst_ref=part(t, me, 1),
                send_sem=send_sem.at[i],
                recv_sem=recv_sem.at[i],
                device_id=(tg, td),
                device_id_type=MESH,
            ).start()
        return carry

    lax.fori_loop(1, n, send, 0)
    for i, (s, t) in enumerate(zip(sources, targets)):
        pltpu.make_async_copy(part(s, 0, n - 1), part(s, 0, n - 1), send_sem.at[i]).wait()
        pltpu.make_async_copy(part(t, 0, n - 1), part(t, 0, n - 1), recv_sem.at[i]).wait()
    for copy in own:
        copy.wait()


def exchange(n, collective_id, *arrays):
    return pl.pallas_call(
        functools.partial(exchange_kernel, n),
        in_specs=[pl.BlockSpec(memory_space=pl.ANY)] * len(arrays),
        out_specs=[pl.BlockSpec(memory_space=pl.ANY)] * len(arrays),
        out_shape=[jax.ShapeDtypeStruct(a.shape, a.dtype) for a in arrays],
        scratch_shapes=[pltpu.SemaphoreType.DMA((len(arrays),))] * 3,
        compiler_params=pltpu.CompilerParams(collective_id=collective_id, has_side_effects=True),
        name="exchange",
    )(*arrays)


def settle_kernel(per_line, sharp_ref, in_ref, out_ref, soft_ref, members, results):
    me = lax.axis_index("group") * 32 + lax.axis_index("dev")
    owned, span, features = members.shape
    half = features // 2
    chunk = 16

    def source_row(o):
        return (o % 32) // 2 * 16 + o // 128 * 8 + (o % 128) // 32 * 2 + o % 2

    inward = jnp.where(source_row(iota((256, 256), 0)) == iota((256, 256), 1), 1.0, 0.0).astype(BF16)
    outward = jnp.where(source_row(iota((256, 256), 1)) == iota((256, 256), 0), 1.0, 0.0).astype(BF16)

    def gather(b, carry):
        arrived = in_ref[pl.ds(pl.multiple_of(b * 256, 256), 256), :]
        placed = jnp.dot(inward, arrived, preferred_element_type=F32).astype(BF16)
        rows = pl.ds(pl.multiple_of(b * 32, 32), 32)
        for c in range(owned):
            members[c, rows, :half] = placed[c * 32:(c + 1) * 32]
            members[c, rows, half:] = placed[128 + c * 32:128 + (c + 1) * 32]
        return carry

    lax.fori_loop(0, span // 32, gather, 0, unroll=4)

    off_diagonal = iota((span, span), 0) != iota((span, span), 1)
    first = jnp.where(iota((16, 128), 1) == 0, 1.0, 0.0).astype(BF16)
    source = iota((span, 128), 0) // 2
    lane = iota((span, 128), 1) - source % per_line * 8 - iota((span, 128), 0) % 2
    soft = jnp.zeros((span, 128), F32)
    for c in range(owned):
        sharp = sharp_ref[me * owned + c]
        rows = members[c]
        marks = lax.dot_general(first, rows[:, :128], NT, preferred_element_type=F32)[:1]
        dots = lax.dot_general(rows, rows, NT, preferred_element_type=F32)
        masked = jnp.where(off_diagonal & (marks < EMPTY / 2), dots * (sharp * (1.0 / features)), NEGATIVE)
        highest = jnp.maximum(jnp.max(masked, axis=1, keepdims=True), 0.0)
        weights = jnp.exp(masked - highest)
        total = jnp.exp(-highest) + jnp.sum(weights, axis=1, keepdims=True)
        soft = jnp.where(lane == 2 * c, (highest + jnp.log(total)) / sharp, soft)
        summed = jnp.dot(weights.astype(BF16), rows, preferred_element_type=F32)
        results[c] = (summed * (1.0 / total)).astype(BF16)

    lines = soft_ref.shape[0]
    pick = jnp.where(iota((lines, span), 1) // (2 * per_line) == iota((lines, span), 0), 1.0, 0.0).astype(BF16)
    spread = jnp.dot(pick, soft.astype(BF16), preferred_element_type=F32)
    soft_ref[...] = spread.reshape(soft_ref.shape)

    def scatter(b, carry):
        rows = pl.ds(pl.multiple_of(b * 32, 32), 32)
        placed = jnp.concatenate(
            [results[c, rows, :half] for c in range(owned)] + [results[c, rows, half:] for c in range(owned)],
            axis=0,
        )
        back = jnp.dot(outward, placed, preferred_element_type=F32)
        out_ref[pl.ds(pl.multiple_of(b * 256, 256), 256), :] = back.astype(BF16)
        return carry

    lax.fori_loop(0, span // 32, scatter, 0, unroll=4)


def settle(sharp, arrived, n, owned, per_line):
    rows, half = arrived.shape
    span = n * SRC_CAP
    return pl.pallas_call(
        functools.partial(settle_kernel, per_line),
        in_specs=[pl.BlockSpec(memory_space=pltpu.SMEM), pl.BlockSpec(memory_space=pltpu.VMEM)],
        out_specs=[pl.BlockSpec(memory_space=pltpu.VMEM)] * 2,
        out_shape=[
            jax.ShapeDtypeStruct((rows, half), BF16),
            jax.ShapeDtypeStruct((n // per_line, 1, 128), F32),
        ],
        scratch_shapes=[
            pltpu.VMEM((owned, span, half * 2), BF16),
            pltpu.VMEM((owned, span, half * 2), BF16),
        ],
        compiler_params=pltpu.CompilerParams(vmem_limit_bytes=40 * 2**20),
        name="settle",
    )(sharp, arrived)


def unpack_kernel(dest_ref, in_ref, soft_in_ref, soft_ref, out_ref, combined, soft_all):
    step = pl.program_id(0)
    slots, features = combined.shape
    half = features // 2
    n = soft_in_ref.shape[0]
    rows = out_ref.shape[0]

    @pl.when(step == 0)
    def _():
        def split(b, carry):
            block = in_ref[pl.ds(pl.multiple_of(b * 512, 512), 512), :].astype(F32).reshape(32, 2, 8, half)
            place = pl.ds(pl.multiple_of(b * 256, 256), 256)
            combined[place, :half] = block[:, 0].reshape(256, half).astype(BF16)
            combined[place, half:] = block[:, 1].reshape(256, half).astype(BF16)
            return carry

        lax.fori_loop(0, slots // 256, split, 0)
        soft_all[...] = jnp.transpose(soft_in_ref[...].reshape(n, 128)).astype(BF16)

    dest = dest_ref[...]
    column = as_column(dest.astype(F32))
    lane = iota((rows, 128), 1).astype(F32)
    hit = jnp.concatenate(
        [jnp.where(column == lane + float(s), 1.0, 0.0).astype(BF16) for s in range(0, slots, 128)], axis=1
    )
    out_ref[...] = jnp.dot(hit, combined[...], preferred_element_type=F32).astype(BF16)

    owner = jnp.where(iota((n, rows), 0) == dest // 8, 1.0, 0.0).astype(BF16)
    found = jnp.dot(soft_all[...], owner, preferred_element_type=F32)[:8]
    chosen = jnp.where(iota((8, rows), 0) == dest % 8, found, 0.0)
    soft_ref[...] = jnp.sum(chosen, axis=0, keepdims=True).astype(BF16)


def unpack(dest, returned, soft_returned):
    count = dest.shape[1]
    n = soft_returned.shape[0]
    blocks, half = returned.shape
    slots, features = blocks // 2, half * 2
    rows = 256
    return pl.pallas_call(
        unpack_kernel,
        grid=(count // rows,),
        in_specs=[
            pl.BlockSpec((1, rows), lambda i: (0, i)),
            pl.BlockSpec((blocks, half), lambda i: (0, 0)),
            pl.BlockSpec((n, 1, 128), lambda i: (0, 0, 0)),
        ],
        out_specs=[
            pl.BlockSpec((1, rows), lambda i: (0, i)),
            pl.BlockSpec((rows, features), lambda i: (i, 0)),
        ],
        out_shape=[
            jax.ShapeDtypeStruct((1, count), BF16),
            jax.ShapeDtypeStruct((count, features), BF16),
        ],
        scratch_shapes=[pltpu.VMEM((slots, features), BF16), pltpu.VMEM((128, n), BF16)],
        compiler_params=pltpu.CompilerParams(vmem_limit_bytes=40 * 2**20),
        name="unpack",
    )(dest, returned, soft_returned)


PLANES = 8
LINES = 32
CAP = 160
BLOCK = 16


def blocks(ref, start, count):
    return ref.at[pl.ds(pl.multiple_of(start * BLOCK, BLOCK), count * BLOCK)]


def near_first(k):
    near = k // 2 + 1
    return near + (k % 2) * (PLANES - 2 * near)


def far_first(k):
    near = 4 - (k + 1) // 2
    return near + ((k + 1) % 2) * (PLANES - 2 * near)


def place():
    g, d = lax.axis_index("group"), lax.axis_index("dev")
    return g, d // PLANES, d % PLANES


def on_line(j, g, x):
    q = (j * 11) % LINES
    core = (g % 2 + q % 2) % 2
    y = (g // 2 + (q // 2) % 4) % 4
    return y * 2 + core, (x + q // 8) % 4


def greet_all(g, x, z):
    barrier = pltpu.get_barrier_semaphore()

    def greet_z(k, carry):
        there = (g, x * PLANES + (z + k) % PLANES)
        pl.semaphore_signal(barrier, inc=1, device_id=there, device_id_type=MESH)
        return carry

    def greet_line(j, carry):
        tg, tx = on_line(j, g, x)
        pl.semaphore_signal(barrier, inc=1, device_id=(tg, tx * PLANES + z), device_id_type=MESH)
        return carry

    lax.fori_loop(1, PLANES, greet_z, 0)
    lax.fori_loop(1, LINES, greet_line, 0)
    return barrier


def relay_copies(rows_out, relay_in, rows_in, send_sems, recv_sems, g, x, z, source_at):
    def first_leg():
        copies = []
        for way, hop in enumerate((2, PLANES - 2)):
            half = pl.ds(way * (CAP // 2), CAP // 2)
            copies.append(pltpu.make_async_remote_copy(
                src_ref=rows_out.at[(z + 4) % PLANES, half], dst_ref=relay_in.at[way],
                send_sem=send_sems.at[way], recv_sem=recv_sems.at[way],
                device_id=(g, x * PLANES + (z + hop) % PLANES), device_id_type=MESH))
        return copies

    def second_leg():
        copies = []
        for way, hop in enumerate((2, PLANES - 2)):
            half = pl.ds(way * (CAP // 2), CAP // 2)
            source = (z + PLANES - hop) % PLANES
            copies.append(pltpu.make_async_remote_copy(
                src_ref=relay_in.at[way], dst_ref=rows_in.at[source, half],
                send_sem=send_sems.at[2 + way], recv_sem=source_at(source),
                device_id=(g, x * PLANES + (z + hop) % PLANES), device_id_type=MESH))
        return copies

    def pass_on():
        for way, copy in enumerate(second_leg()):
            came = relay_in.at[way]
            pltpu.make_async_copy(came, came, recv_sems.at[way]).wait()
            copy.start()

    def finish():
        for copy in first_leg() + second_leg():
            copy.wait_send()

    return first_leg, pass_on, finish


def collect_kernel(ids_ref, x_ref, inbox, where_ref, slots_in, hits, rows_out, rows_in, relay_in, slots_out, line_out,
                   z_send, z_recv, relay_send, relay_recv, line_send, line_recv, own_sem):
    g, x, z = place()
    count, features = x_ref.shape
    half = features // 2
    barrier = greet_all(g, x, z)

    ids = ids_ref[...]
    columns = as_column(ids.astype(F32)).astype(jnp.int32)
    plane = jnp.right_shift(ids, 2) & (PLANES - 1)
    plane_columns = jnp.right_shift(columns, 2) & (PLANES - 1)
    before = iota((128, 128), 0) < iota((128, 128), 1)
    ordinal, position = [], []
    for t in range(0, count, 128):
        same = jnp.zeros((128, 128), F32)
        beside = jnp.zeros((128, 128), F32)
        for r in range(0, t + 128, 128):
            alike = columns[r:r + 128] == ids[:, t:t + 128]
            near = plane_columns[r:r + 128] == plane[:, t:t + 128]
            if r == t:
                alike, near = alike & before, near & before
            same += jnp.where(alike, 1.0, 0.0)
            beside += jnp.where(near, 1.0, 0.0)
        ordinal.append(jnp.sum(same, axis=0, keepdims=True))
        position.append(jnp.sum(beside, axis=0, keepdims=True))
    ordinal, position = jnp.concatenate(ordinal, axis=1), jnp.concatenate(position, axis=1)
    where_ref[...] = jnp.concatenate([plane.astype(F32), position, jnp.zeros((6, count), F32)], axis=0)
    flag = jnp.where(jnp.max(position) > CAP - 0.5, 1.0, 0.0)
    slot = (jnp.right_shift(ids, 5) * 8 + (ids & 3) * SRC_CAP).astype(F32) + ordinal + 1.0
    slot = jnp.broadcast_to(slot, (16, count)).astype(BF16)
    hits[CAP:, :] = jnp.zeros((256 - CAP, count), BF16)
    key = jnp.where(position < CAP - 0.5, position.astype(jnp.int32) * PLANES + plane, -1)

    def compact(there):
        hits[:CAP, :] = jnp.where(iota((CAP, count), 0) * PLANES + there == key, 1.0, 0.0).astype(BF16)
        rows = jnp.dot(hits[:CAP, :], x_ref[...], preferred_element_type=F32).astype(BF16)
        names = lax.dot_general(slot, hits[...], NT, preferred_element_type=F32)[:1]
        return rows, jnp.where(iota((1, 256), 1) == 255, flag, names)

    def z_copy(out, into, i, there):
        return pltpu.make_async_remote_copy(
            src_ref=out.at[there], dst_ref=into.at[z], send_sem=z_send.at[i], recv_sem=z_recv.at[i, z],
            device_id=(g, x * PLANES + there), device_id_type=MESH)

    first_leg, pass_on, finish_relay = relay_copies(
        rows_out, relay_in, rows_in, relay_send, relay_recv, g, x, z, lambda source: z_recv.at[0, source])

    def prepare(there):
        rows, names = compact(there)
        rows_out[there] = rows
        slots_out[there] = names

    def send_z(k, carry):
        there = (z + near_first(k)) % PLANES
        prepare(there)
        z_copy(rows_out, rows_in, 0, there).start()
        z_copy(slots_out, slots_in, 1, there).start()
        return carry

    pl.semaphore_wait(barrier, PLANES + LINES - 2)
    lax.fori_loop(0, 4, send_z, 0)
    opposite = (z + 4) % PLANES
    prepare(opposite)
    for copy in first_leg():
        copy.start()
    z_copy(slots_out, slots_in, 1, opposite).start()
    lax.fori_loop(4, 6, send_z, 0)
    rows, names = compact(z)
    rows_in[z] = rows
    slots_in[z] = names

    def own_copy(source):
        return pltpu.make_async_copy(
            blocks(line_out, source * LINES + g * 4 + x, 1), blocks(inbox, (g * 4 + x) * PLANES + source, 1),
            own_sem.at[source])

    def forward(source):
        wide = rows_in[source].astype(F32)
        scale = lax.rsqrt(jnp.mean(wide * wide, axis=-1, keepdims=True) + 1e-06)
        names = slots_in[source][:, :CAP].astype(jnp.int32) - 1
        hit = jnp.where(iota((256, CAP), 0) == names, 1.0, 0.0)
        filled = jnp.sum(hit, axis=1, keepdims=True)
        rows = jnp.dot(hit.astype(BF16), (wide * scale).astype(BF16), preferred_element_type=F32)
        first = jnp.where((iota((256, 128), 1) == 0) & (filled < 0.5), EMPTY, rows[:, :128])
        left = jnp.concatenate([first, rows[:, 128:half]], axis=1).reshape(LINES, 1, 8, half)
        right = rows[:, half:].reshape(LINES, 1, 8, half)
        both = jnp.concatenate([left, right], axis=1).reshape(512, half)
        line_out[pl.ds(pl.multiple_of(source * 512, 512), 512), :] = both.astype(BF16)
        own_copy(source).start()

        def send(j, carry):
            tg, tx = on_line(j, g, x)
            pltpu.make_async_remote_copy(
                src_ref=blocks(line_out, source * LINES + tg * 4 + tx, 1),
                dst_ref=blocks(inbox, (g * 4 + x) * PLANES + source, 1),
                send_sem=line_send, recv_sem=line_recv,
                device_id=(tg, tx * PLANES + z), device_id_type=MESH).start()
            return carry

        lax.fori_loop(1, LINES, send, 0)

    forward(z)

    def arrive(k, carry):
        source = (z + PLANES - near_first(k)) % PLANES

        @pl.when(k == 4)
        def _():
            pass_on()

        pltpu.make_async_copy(rows_in.at[source], rows_in.at[source], z_recv.at[0, source]).wait()
        pltpu.make_async_copy(slots_in.at[source], slots_in.at[source], z_recv.at[1, source]).wait()
        forward(source)
        return carry

    lax.fori_loop(0, PLANES - 1, arrive, 0)
    others = PLANES * (LINES - 1)
    sent = rows_out.at[pl.ds(0, PLANES - 2)]
    pltpu.make_async_copy(sent, sent, z_send.at[0]).wait()
    sent = slots_out.at[pl.ds(0, PLANES - 1)]
    pltpu.make_async_copy(sent, sent, z_send.at[1]).wait()
    finish_relay()
    pltpu.make_async_copy(blocks(line_out, 0, others), blocks(line_out, 0, others), line_send).wait()
    pltpu.make_async_copy(blocks(inbox, 0, others), blocks(inbox, 0, others), line_recv).wait()

    def finish(source, carry):
        own_copy(source).wait()
        return carry

    lax.fori_loop(0, PLANES, finish, 0)


def collect(ids, x):
    count, features = x.shape
    half = features // 2
    slots = PLANES * LINES * BLOCK
    vmem = pl.BlockSpec(memory_space=pltpu.VMEM)
    return pl.pallas_call(
        collect_kernel,
        in_specs=[vmem] * 2,
        out_specs=[vmem] * 3,
        out_shape=[
            jax.ShapeDtypeStruct((slots, half), BF16),
            jax.ShapeDtypeStruct((8, count), F32),
            jax.ShapeDtypeStruct((PLANES, 1, 256), F32),
        ],
        scratch_shapes=[
            pltpu.VMEM((256, count), BF16),
            pltpu.VMEM((PLANES, CAP, features), BF16),
            pltpu.VMEM((PLANES, CAP, features), BF16),
            pltpu.VMEM((2, CAP // 2, features), BF16),
            pltpu.VMEM((PLANES, 1, 256), F32),
            pltpu.VMEM((slots, half), BF16),
            pltpu.SemaphoreType.DMA((2,)),
            pltpu.SemaphoreType.DMA((2, PLANES)),
            pltpu.SemaphoreType.DMA((4,)),
            pltpu.SemaphoreType.DMA((2,)),
            pltpu.SemaphoreType.DMA,
            pltpu.SemaphoreType.DMA,
            pltpu.SemaphoreType.DMA((PLANES,)),
        ],
        compiler_params=pltpu.CompilerParams(
            collective_id=2, has_side_effects=True, vmem_limit_bytes=40 * 2**20),
        name="collect",
    )(ids, x)


def restore_kernel(results, soft_ref, slots_ref, rows_back, soft_back, flag_ref, line_in, soft_out, soft_in, rows_out,
                   relay_in, names_out, z_send, z_recv, relay_send, relay_recv, line_send, line_recv, soft_sem, own_sem):
    g, x, z = place()
    me = g * 4 + x
    half = results.shape[1]
    barrier = greet_all(g, x, z)
    flag = jnp.max(jnp.where(iota((PLANES, 1, 256), 2) == 255, slots_ref[...], 0.0))
    soft_out[...] = jnp.where(iota(soft_out.shape, 2) < 64, soft_ref[...], flag)
    soft_in[me] = soft_out[me]
    pl.semaphore_wait(barrier, PLANES + LINES - 2)

    def send_soft(j, carry):
        tg, tx = on_line(j, g, x)
        pltpu.make_async_remote_copy(
            src_ref=soft_out.at[tg * 4 + tx], dst_ref=soft_in.at[me], send_sem=soft_sem.at[0],
            recv_sem=soft_sem.at[1], device_id=(tg, tx * PLANES + z), device_id_type=MESH).start()
        return carry

    lax.fori_loop(1, LINES, send_soft, 0)

    def own_copy(home):
        return pltpu.make_async_copy(
            blocks(results, me * PLANES + home, 1), blocks(line_in, home * LINES + me, 1), own_sem.at[home])

    def home_of(k):
        return (z + far_first(k)) % PLANES

    def send_line(k, carry):
        home = home_of(k)
        own_copy(home).start()

        def send(j, inner):
            tg, tx = on_line(j, g, x)
            pltpu.make_async_remote_copy(
                src_ref=blocks(results, (tg * 4 + tx) * PLANES + home, 1),
                dst_ref=blocks(line_in, home * LINES + me, 1),
                send_sem=line_send, recv_sem=line_recv.at[home],
                device_id=(tg, tx * PLANES + z), device_id_type=MESH).start()
            return inner

        return lax.fori_loop(1, LINES, send, carry)

    lax.fori_loop(0, 3, send_line, 0)
    first = soft_in.at[pl.ds(0, LINES - 1)]
    pltpu.make_async_copy(first, first, soft_sem.at[1]).wait()
    all_soft = soft_in[...].reshape(LINES, 128)
    flag_ref[...] = jnp.broadcast_to(jnp.max(all_soft[:, 64:], axis=(0, 1), keepdims=True), flag_ref.shape)
    spread = jnp.where(iota((256, LINES), 0) // 8 == iota((256, LINES), 1), 1.0, 0.0).astype(BF16)
    all_soft = jnp.dot(spread, all_soft.astype(BF16), preferred_element_type=F32)

    def settle_home(home):
        arrived = blocks(line_in, home * LINES, LINES - 1)
        pltpu.make_async_copy(arrived, arrived, line_recv.at[home]).wait()
        own_copy(home).wait()
        both = line_in[pl.ds(pl.multiple_of(home * 512, 512), 512), :].astype(F32).reshape(LINES, 2, 8, half)
        left, right = both[:, 0].reshape(256, half).astype(BF16), both[:, 1].reshape(256, half).astype(BF16)
        names = slots_ref[home]
        column = as_column(names)[:CAP] - 1.0
        lane = iota((CAP, 128), 1).astype(F32)
        hit = jnp.concatenate(
            [jnp.where(column == lane + float(s), 1.0, 0.0).astype(BF16) for s in (0, 128)], axis=1)
        mine = jnp.where(iota((256, 128), 1) == home * 8 + iota((256, 128), 0) % 8, all_soft, 0.0).astype(BF16)
        values = lax.dot_general(jnp.ones((16, 128), BF16), mine, NT, preferred_element_type=F32)
        picked = jnp.where(iota((256, 256), 0) == names.astype(jnp.int32) - 1, 1.0, 0.0).astype(BF16)
        picked = jnp.dot(values.astype(BF16), picked, preferred_element_type=F32)[:1]
        left = jnp.dot(hit, left, preferred_element_type=F32).astype(BF16)
        right = jnp.dot(hit, right, preferred_element_type=F32).astype(BF16)
        return left, right, picked

    first_leg, pass_on, finish_relay = relay_copies(
        rows_out, relay_in, rows_back, relay_send, relay_recv, g, x, z, lambda source: z_recv.at[0])

    def z_copy(out, into, i, home):
        return pltpu.make_async_remote_copy(
            src_ref=out.at[home], dst_ref=into.at[z], send_sem=z_send.at[i], recv_sem=z_recv.at[i],
            device_id=(g, x * PLANES + home), device_id_type=MESH)

    def send_z(k, carry):
        home = home_of(k)
        left, right, picked = settle_home(home)
        rows_out[home, :, :half] = left
        rows_out[home, :, half:] = right
        names_out[home] = picked
        z_copy(names_out, soft_back, 1, home).start()

        @pl.when(k == 0)
        def _():
            for copy in first_leg():
                copy.start()

        @pl.when(k > 0)
        def _():
            z_copy(rows_out, rows_back, 0, home).start()

        @pl.when(k == 3)
        def _():
            pass_on()

        @pl.when(k < PLANES - 3)
        def _():
            send_line(k + 3, 0)

        return carry

    lax.fori_loop(0, PLANES - 1, send_z, 0)
    left, right, picked = settle_home(z)
    rows_back[z, :, :half] = left
    rows_back[z, :, half:] = right
    soft_back[z] = picked

    others = PLANES * (LINES - 1)
    sent = soft_out.at[pl.ds(0, LINES - 1)]
    pltpu.make_async_copy(sent, sent, soft_sem.at[0]).wait()
    pltpu.make_async_copy(blocks(results, 0, others), blocks(results, 0, others), line_send).wait()
    sent = rows_out.at[pl.ds(0, PLANES - 2)]
    pltpu.make_async_copy(sent, sent, z_send.at[0]).wait()
    sent = names_out.at[pl.ds(0, PLANES - 1)]
    pltpu.make_async_copy(sent, sent, z_send.at[1]).wait()
    finish_relay()
    for i, into in enumerate((rows_back, soft_back)):
        came = into.at[pl.ds(0, PLANES - 1)]
        pltpu.make_async_copy(came, came, z_recv.at[i]).wait()


def restore(results, soft, slots):
    rows, half = results.shape
    vmem = pl.BlockSpec(memory_space=pltpu.VMEM)
    return pl.pallas_call(
        restore_kernel,
        in_specs=[vmem] * 3,
        out_specs=[vmem] * 3,
        out_shape=[
            jax.ShapeDtypeStruct((PLANES, CAP, half * 2), BF16),
            jax.ShapeDtypeStruct((PLANES, 1, 256), F32),
            jax.ShapeDtypeStruct((8, 128), F32),
        ],
        scratch_shapes=[
            pltpu.VMEM((rows, half), BF16),
            pltpu.VMEM((LINES, 1, 128), F32),
            pltpu.VMEM((LINES, 1, 128), F32),
            pltpu.VMEM((PLANES, CAP, half * 2), BF16),
            pltpu.VMEM((2, CAP // 2, half * 2), BF16),
            pltpu.VMEM((PLANES, 1, 256), F32),
            pltpu.SemaphoreType.DMA((2,)),
            pltpu.SemaphoreType.DMA((2,)),
            pltpu.SemaphoreType.DMA((4,)),
            pltpu.SemaphoreType.DMA((2,)),
            pltpu.SemaphoreType.DMA,
            pltpu.SemaphoreType.DMA((PLANES,)),
            pltpu.SemaphoreType.DMA((2,)),
            pltpu.SemaphoreType.DMA((PLANES,)),
        ],
        compiler_params=pltpu.CompilerParams(
            collective_id=3, has_side_effects=True, vmem_limit_bytes=40 * 2**20),
        name="restore",
    )(results, soft, slots)


def place_kernel(where_ref, in_ref, soft_in_ref, soft_ref, out_ref):
    rows = out_ref.shape[0]
    plane, position = where_ref[0:1, :], where_ref[1:2, :]
    column = as_column(plane * CAP + position)
    lane = iota((rows, 128), 1).astype(F32)
    hit = jnp.concatenate(
        [jnp.where(column == lane + float(s), 1.0, 0.0).astype(BF16) for s in range(0, PLANES * CAP, 128)], axis=1)
    combined = in_ref[...].reshape(PLANES * CAP, in_ref.shape[2])
    out_ref[...] = jnp.dot(hit, combined, preferred_element_type=F32).astype(BF16)

    spot = jnp.where(iota((256, rows), 0).astype(F32) == position, 1.0, 0.0).astype(BF16)
    soft = soft_in_ref[...].reshape(PLANES, 256)
    soft = jnp.concatenate([soft, jnp.zeros((8, 256), F32)], axis=0).astype(BF16)
    found = jnp.dot(soft, spot, preferred_element_type=F32)[:PLANES]
    chosen = jnp.where(iota((PLANES, rows), 0).astype(F32) == plane, found, 0.0)
    soft_ref[...] = jnp.sum(chosen, axis=0, keepdims=True).astype(BF16)


def put_in_place(where, returned, soft_returned):
    count = where.shape[1]
    planes, cap, features = returned.shape
    rows = 256
    return pl.pallas_call(
        place_kernel,
        grid=(count // rows,),
        in_specs=[
            pl.BlockSpec((8, rows), lambda i: (0, i)),
            pl.BlockSpec((planes, cap, features), lambda i: (0, 0, 0)),
            pl.BlockSpec((planes, 1, 256), lambda i: (0, 0, 0)),
        ],
        out_specs=[
            pl.BlockSpec((1, rows), lambda i: (0, i)),
            pl.BlockSpec((rows, features), lambda i: (i, 0)),
        ],
        out_shape=[
            jax.ShapeDtypeStruct((1, count), BF16),
            jax.ShapeDtypeStruct((count, features), BF16),
        ],
        compiler_params=pltpu.CompilerParams(vmem_limit_bytes=32 * 2**20),
        name="put_in_place",
    )(where, returned, soft_returned)


def by_all_slots(n, embeddings, cluster_ids, sharp):
    clusters = sharp.shape[0]
    outbox, dest = pack(cluster_ids[None, :], embeddings, clusters * SRC_CAP)
    (arrived,) = exchange(n, 0, outbox)
    results, soft = settle(sharp, arrived, n, clusters // n, 1)
    returned, soft_returned = exchange(n, 1, results, soft)
    return unpack(dest, returned, soft_returned)


def body(n, embeddings, cluster_ids, sharpness):
    sharp = sharpness.astype(F32)
    arrived, where, slots = collect(cluster_ids[None, :], embeddings)
    results, soft = settle(sharp, arrived, n, sharp.shape[0] // n, PLANES)
    returned, soft_returned, flag = restore(results, soft, slots)
    soft_max, neighbour = put_in_place(where, returned, soft_returned)
    soft_max, neighbour = lax.cond(
        flag[0, 0] > 0.5,
        lambda: tuple(by_all_slots(n, embeddings, cluster_ids, sharp)),
        lambda: (soft_max, neighbour),
    )
    return (soft_max[0], neighbour)


def solution(mesh):
    n = mesh.size
    return jax.shard_map(
        functools.partial(body, n),
        mesh=mesh,
        in_specs=(P(("group", "dev"), None), P(("group", "dev")), P()),
        out_specs=(P(("group", "dev")), P(("group", "dev"), None)),
        check_vma=False,
    )
```

```python
import functools

import jax
import jax.numpy as jnp
from jax import lax
from jax.experimental import pallas as pl
from jax.experimental.pallas import tpu as pltpu
from jax.sharding import PartitionSpec as P

MESH = pl.DeviceIdType.MESH
SRC_CAP = 2
EMPTY = 1024.0
NEGATIVE = -1e30
NT = (((1,), (1,)), ((), ()))
F32 = jnp.float32
BF16 = jnp.bfloat16


def iota(shape, dim):
    return lax.broadcasted_iota(jnp.int32, shape, dim)


def as_column(row, lanes=128):
    return jnp.transpose(jnp.broadcast_to(row, (lanes, row.shape[1])))


def pack_kernel(ids_ref, x_ref, out_ref, dest_ref, normed):
    step = pl.program_id(0)
    count, features = x_ref.shape
    half = features // 2
    slots = out_ref.shape[0] // 2

    @pl.when(step == 0)
    def _():
        ids = ids_ref[...]
        columns = as_column(ids.astype(F32))
        ordinal = jnp.zeros((1, count), F32)
        for r in range(0, count, 128):
            block = jnp.concatenate([columns[r:r + 128]] * (count // 128), axis=1)
            same = block == ids.astype(F32)
            before = iota((128, count), 0) + r < iota((128, count), 1)
            ordinal += jnp.sum(jnp.where(same & before, 1.0, 0.0), axis=0, keepdims=True)
        dest_ref[...] = ids * SRC_CAP + ordinal.astype(jnp.int32)
        for r in range(0, count, 256):
            wide = x_ref[r:r + 256, :].astype(F32)
            scale = lax.rsqrt(jnp.mean(wide * wide, axis=-1, keepdims=True) + 1e-06)
            normed[r:r + 256, :] = (wide * scale).astype(BF16)

    dest = dest_ref[...]
    hit = jnp.where(iota((slots, count), 0) + step * slots == dest, 1.0, 0.0)
    filled = jnp.sum(hit, axis=1, keepdims=True)
    rows = jnp.dot(hit.astype(BF16), normed[...], preferred_element_type=F32)
    first = jnp.where((iota((slots, 128), 1) == 0) & (filled < 0.5), EMPTY, rows[:, :128])
    left = jnp.concatenate([first, rows[:, 128:half]], axis=1).reshape(slots // 8, 1, 8, half)
    right = rows[:, half:].reshape(slots // 8, 1, 8, half)
    both = jnp.concatenate([left, right], axis=1).reshape(slots * 2, half)
    out_ref[...] = both.astype(BF16)


def pack(ids, x, slots_all):
    count, features = x.shape
    steps = 8
    slots = slots_all // steps
    return pl.pallas_call(
        pack_kernel,
        grid=(steps,),
        in_specs=[
            pl.BlockSpec((1, count), lambda i: (0, 0)),
            pl.BlockSpec((count, features), lambda i: (0, 0)),
        ],
        out_specs=[
            pl.BlockSpec((slots * 2, features // 2), lambda i: (i, 0)),
            pl.BlockSpec((1, count), lambda i: (0, 0)),
        ],
        out_shape=[
            jax.ShapeDtypeStruct((slots_all * 2, features // 2), BF16),
            jax.ShapeDtypeStruct((1, count), jnp.int32),
        ],
        scratch_shapes=[pltpu.VMEM((count, features), BF16)],
        compiler_params=pltpu.CompilerParams(vmem_limit_bytes=32 * 2**20),
        name="pack",
    )(ids, x)


def partner(k, g, d):
    q = (k * 101) % 256
    z = (d % 8 + q % 8) % 8
    x = (d // 8 + (q // 8) % 4) % 4
    y = (g // 2 + (q // 32) % 4) % 4
    core = (g % 2 + q // 128) % 2
    return y * 2 + core, x * 8 + z


def exchange_kernel(n, *refs):
    count = (len(refs) - 3) // 2
    sources, targets = refs[:count], refs[count:2 * count]
    send_sem, recv_sem, own_sem = refs[2 * count:]
    g, d = lax.axis_index("group"), lax.axis_index("dev")
    me = g * 32 + d

    def part(ref, start, blocks):
        size = ref.shape[0] // n
        return ref.at[pl.ds(pl.multiple_of(start * size, size), blocks * size)]

    barrier = pltpu.get_barrier_semaphore()

    def greet(k, carry):
        tg, td = partner(k, g, d)
        pl.semaphore_signal(barrier, inc=1, device_id=(tg, td), device_id_type=MESH)
        return carry

    lax.fori_loop(1, n, greet, 0)
    own = [
        pltpu.make_async_copy(part(s, me, 1), part(t, me, 1), own_sem.at[i])
        for i, (s, t) in enumerate(zip(sources, targets))
    ]
    for copy in own:
        copy.start()
    pl.semaphore_wait(barrier, n - 1)

    def send(k, carry):
        tg, td = partner(k, g, d)
        for i, (s, t) in enumerate(zip(sources, targets)):
            pltpu.make_async_remote_copy(
                src_ref=part(s, tg * 32 + td, 1),
                dst_ref=part(t, me, 1),
                send_sem=send_sem.at[i],
                recv_sem=recv_sem.at[i],
                device_id=(tg, td),
                device_id_type=MESH,
            ).start()
        return carry

    lax.fori_loop(1, n, send, 0)
    for i, (s, t) in enumerate(zip(sources, targets)):
        pltpu.make_async_copy(part(s, 0, n - 1), part(s, 0, n - 1), send_sem.at[i]).wait()
        pltpu.make_async_copy(part(t, 0, n - 1), part(t, 0, n - 1), recv_sem.at[i]).wait()
    for copy in own:
        copy.wait()


def exchange(n, collective_id, *arrays):
    return pl.pallas_call(
        functools.partial(exchange_kernel, n),
        in_specs=[pl.BlockSpec(memory_space=pl.ANY)] * len(arrays),
        out_specs=[pl.BlockSpec(memory_space=pl.ANY)] * len(arrays),
        out_shape=[jax.ShapeDtypeStruct(a.shape, a.dtype) for a in arrays],
        scratch_shapes=[pltpu.SemaphoreType.DMA((len(arrays),))] * 3,
        compiler_params=pltpu.CompilerParams(collective_id=collective_id, has_side_effects=True),
        name="exchange",
    )(*arrays)


def settle_kernel(per_line, sharp_ref, in_ref, out_ref, soft_ref, members, results):
    me = lax.axis_index("group") * 32 + lax.axis_index("dev")
    owned, span, features = members.shape
    half = features // 2
    chunk = 16

    def source_row(o):
        return (o % 32) // 2 * 16 + o // 128 * 8 + (o % 128) // 32 * 2 + o % 2

    inward = jnp.where(source_row(iota((256, 256), 0)) == iota((256, 256), 1), 1.0, 0.0).astype(BF16)
    outward = jnp.where(source_row(iota((256, 256), 1)) == iota((256, 256), 0), 1.0, 0.0).astype(BF16)

    def gather(b, carry):
        arrived = in_ref[pl.ds(pl.multiple_of(b * 256, 256), 256), :]
        placed = jnp.dot(inward, arrived, preferred_element_type=F32).astype(BF16)
        rows = pl.ds(pl.multiple_of(b * 32, 32), 32)
        for c in range(owned):
            members[c, rows, :half] = placed[c * 32:(c + 1) * 32]
            members[c, rows, half:] = placed[128 + c * 32:128 + (c + 1) * 32]
        return carry

    lax.fori_loop(0, span // 32, gather, 0, unroll=4)

    off_diagonal = iota((span, span), 0) != iota((span, span), 1)
    first = jnp.where(iota((16, 128), 1) == 0, 1.0, 0.0).astype(BF16)
    source = iota((span, 128), 0) // 2
    lane = iota((span, 128), 1) - source % per_line * 8 - iota((span, 128), 0) % 2
    soft = jnp.zeros((span, 128), F32)
    for c in range(owned):
        sharp = sharp_ref[me * owned + c]
        rows = members[c]
        marks = lax.dot_general(first, rows[:, :128], NT, preferred_element_type=F32)[:1]
        dots = lax.dot_general(rows, rows, NT, preferred_element_type=F32)
        masked = jnp.where(off_diagonal & (marks < EMPTY / 2), dots * (sharp * (1.0 / features)), NEGATIVE)
        highest = jnp.maximum(jnp.max(masked, axis=1, keepdims=True), 0.0)
        weights = jnp.exp(masked - highest)
        total = jnp.exp(-highest) + jnp.sum(weights, axis=1, keepdims=True)
        soft = jnp.where(lane == 2 * c, (highest + jnp.log(total)) / sharp, soft)
        summed = jnp.dot(weights.astype(BF16), rows, preferred_element_type=F32)
        results[c] = (summed * (1.0 / total)).astype(BF16)

    lines = soft_ref.shape[0]
    pick = jnp.where(iota((lines, span), 1) // (2 * per_line) == iota((lines, span), 0), 1.0, 0.0).astype(BF16)
    spread = jnp.dot(pick, soft.astype(BF16), preferred_element_type=F32)
    soft_ref[...] = spread.reshape(soft_ref.shape)

    def scatter(b, carry):
        rows = pl.ds(pl.multiple_of(b * 32, 32), 32)
        placed = jnp.concatenate(
            [results[c, rows, :half] for c in range(owned)] + [results[c, rows, half:] for c in range(owned)],
            axis=0,
        )
        back = jnp.dot(outward, placed, preferred_element_type=F32)
        out_ref[pl.ds(pl.multiple_of(b * 256, 256), 256), :] = back.astype(BF16)
        return carry

    lax.fori_loop(0, span // 32, scatter, 0, unroll=4)


def settle(sharp, arrived, n, owned, per_line):
    rows, half = arrived.shape
    span = n * SRC_CAP
    return pl.pallas_call(
        functools.partial(settle_kernel, per_line),
        in_specs=[pl.BlockSpec(memory_space=pltpu.SMEM), pl.BlockSpec(memory_space=pltpu.VMEM)],
        out_specs=[pl.BlockSpec(memory_space=pltpu.VMEM)] * 2,
        out_shape=[
            jax.ShapeDtypeStruct((rows, half), BF16),
            jax.ShapeDtypeStruct((n // per_line, 1, 128), F32),
        ],
        scratch_shapes=[
            pltpu.VMEM((owned, span, half * 2), BF16),
            pltpu.VMEM((owned, span, half * 2), BF16),
        ],
        compiler_params=pltpu.CompilerParams(vmem_limit_bytes=40 * 2**20),
        name="settle",
    )(sharp, arrived)


def unpack_kernel(dest_ref, in_ref, soft_in_ref, soft_ref, out_ref, combined, soft_all):
    step = pl.program_id(0)
    slots, features = combined.shape
    half = features // 2
    n = soft_in_ref.shape[0]
    rows = out_ref.shape[0]

    @pl.when(step == 0)
    def _():
        def split(b, carry):
            block = in_ref[pl.ds(pl.multiple_of(b * 512, 512), 512), :].astype(F32).reshape(32, 2, 8, half)
            place = pl.ds(pl.multiple_of(b * 256, 256), 256)
            combined[place, :half] = block[:, 0].reshape(256, half).astype(BF16)
            combined[place, half:] = block[:, 1].reshape(256, half).astype(BF16)
            return carry

        lax.fori_loop(0, slots // 256, split, 0)
        soft_all[...] = jnp.transpose(soft_in_ref[...].reshape(n, 128)).astype(BF16)

    dest = dest_ref[...]
    column = as_column(dest.astype(F32))
    lane = iota((rows, 128), 1).astype(F32)
    hit = jnp.concatenate(
        [jnp.where(column == lane + float(s), 1.0, 0.0).astype(BF16) for s in range(0, slots, 128)], axis=1
    )
    out_ref[...] = jnp.dot(hit, combined[...], preferred_element_type=F32).astype(BF16)

    owner = jnp.where(iota((n, rows), 0) == dest // 8, 1.0, 0.0).astype(BF16)
    found = jnp.dot(soft_all[...], owner, preferred_element_type=F32)[:8]
    chosen = jnp.where(iota((8, rows), 0) == dest % 8, found, 0.0)
    soft_ref[...] = jnp.sum(chosen, axis=0, keepdims=True).astype(BF16)


def unpack(dest, returned, soft_returned):
    count = dest.shape[1]
    n = soft_returned.shape[0]
    blocks, half = returned.shape
    slots, features = blocks // 2, half * 2
    rows = 256
    return pl.pallas_call(
        unpack_kernel,
        grid=(count // rows,),
        in_specs=[
            pl.BlockSpec((1, rows), lambda i: (0, i)),
            pl.BlockSpec((blocks, half), lambda i: (0, 0)),
            pl.BlockSpec((n, 1, 128), lambda i: (0, 0, 0)),
        ],
        out_specs=[
            pl.BlockSpec((1, rows), lambda i: (0, i)),
            pl.BlockSpec((rows, features), lambda i: (i, 0)),
        ],
        out_shape=[
            jax.ShapeDtypeStruct((1, count), BF16),
            jax.ShapeDtypeStruct((count, features), BF16),
        ],
        scratch_shapes=[pltpu.VMEM((slots, features), BF16), pltpu.VMEM((128, n), BF16)],
        compiler_params=pltpu.CompilerParams(vmem_limit_bytes=40 * 2**20),
        name="unpack",
    )(dest, returned, soft_returned)


PLANES = 8
LINES = 32
CAP = 160
BLOCK = 16


def blocks(ref, start, count):
    return ref.at[pl.ds(pl.multiple_of(start * BLOCK, BLOCK), count * BLOCK)]


def near_first(k):
    near = k // 2 + 1
    return near + (k % 2) * (PLANES - 2 * near)


def far_first(k):
    near = 4 - (k + 1) // 2
    return near + ((k + 1) % 2) * (PLANES - 2 * near)


def place():
    g, d = lax.axis_index("group"), lax.axis_index("dev")
    return g, d // PLANES, d % PLANES


def on_line(j, g, x):
    q = (j * 11) % LINES
    core = (g % 2 + q % 2) % 2
    y = (g // 2 + (q // 2) % 4) % 4
    return y * 2 + core, (x + q // 8) % 4


def greet_all(g, x, z):
    barrier = pltpu.get_barrier_semaphore()

    def greet_z(k, carry):
        there = (g, x * PLANES + (z + k) % PLANES)
        pl.semaphore_signal(barrier, inc=1, device_id=there, device_id_type=MESH)
        return carry

    def greet_line(j, carry):
        tg, tx = on_line(j, g, x)
        pl.semaphore_signal(barrier, inc=1, device_id=(tg, tx * PLANES + z), device_id_type=MESH)
        return carry

    lax.fori_loop(1, PLANES, greet_z, 0)
    lax.fori_loop(1, LINES, greet_line, 0)
    return barrier


def relay_copies(rows_out, relay_in, rows_in, send_sems, recv_sems, g, x, z, source_at):
    def first_leg():
        copies = []
        for way, hop in enumerate((2, PLANES - 2)):
            half = pl.ds(way * (CAP // 2), CAP // 2)
            copies.append(pltpu.make_async_remote_copy(
                src_ref=rows_out.at[(z + 4) % PLANES, half], dst_ref=relay_in.at[way],
                send_sem=send_sems.at[way], recv_sem=recv_sems.at[way],
                device_id=(g, x * PLANES + (z + hop) % PLANES), device_id_type=MESH))
        return copies

    def second_leg():
        copies = []
        for way, hop in enumerate((2, PLANES - 2)):
            half = pl.ds(way * (CAP // 2), CAP // 2)
            source = (z + PLANES - hop) % PLANES
            copies.append(pltpu.make_async_remote_copy(
                src_ref=relay_in.at[way], dst_ref=rows_in.at[source, half],
                send_sem=send_sems.at[2 + way], recv_sem=source_at(source),
                device_id=(g, x * PLANES + (z + hop) % PLANES), device_id_type=MESH))
        return copies

    def pass_on():
        for way, copy in enumerate(second_leg()):
            came = relay_in.at[way]
            pltpu.make_async_copy(came, came, recv_sems.at[way]).wait()
            copy.start()

    def finish():
        for copy in first_leg() + second_leg():
            copy.wait_send()

    return first_leg, pass_on, finish


def collect_kernel(ids_ref, x_ref, inbox, where_ref, slots_in, hits, rows_out, rows_in, relay_in, slots_out, line_out,
                   z_send, z_recv, relay_send, relay_recv, line_send, line_recv, own_sem):
    g, x, z = place()
    count, features = x_ref.shape
    half = features // 2
    barrier = greet_all(g, x, z)

    ids = ids_ref[...]
    columns = as_column(ids.astype(F32)).astype(jnp.int32)
    plane = jnp.right_shift(ids, 2) & (PLANES - 1)
    plane_columns = jnp.right_shift(columns, 2) & (PLANES - 1)
    before = iota((128, 128), 0) < iota((128, 128), 1)
    ordinal, position = [], []
    for t in range(0, count, 128):
        same = jnp.zeros((128, 128), F32)
        beside = jnp.zeros((128, 128), F32)
        for r in range(0, t + 128, 128):
            alike = columns[r:r + 128] == ids[:, t:t + 128]
            near = plane_columns[r:r + 128] == plane[:, t:t + 128]
            if r == t:
                alike, near = alike & before, near & before
            same += jnp.where(alike, 1.0, 0.0)
            beside += jnp.where(near, 1.0, 0.0)
        ordinal.append(jnp.sum(same, axis=0, keepdims=True))
        position.append(jnp.sum(beside, axis=0, keepdims=True))
    ordinal, position = jnp.concatenate(ordinal, axis=1), jnp.concatenate(position, axis=1)
    where_ref[...] = jnp.concatenate([plane.astype(F32), position, jnp.zeros((6, count), F32)], axis=0)
    flag = jnp.where(jnp.max(position) > CAP - 0.5, 1.0, 0.0)
    slot = (jnp.right_shift(ids, 5) * 8 + (ids & 3) * SRC_CAP).astype(F32) + ordinal + 1.0
    slot = jnp.broadcast_to(slot, (16, count)).astype(BF16)
    hits[CAP:, :] = jnp.zeros((256 - CAP, count), BF16)
    key = jnp.where(position < CAP - 0.5, position.astype(jnp.int32) * PLANES + plane, -1)

    def compact(there):
        hits[:CAP, :] = jnp.where(iota((CAP, count), 0) * PLANES + there == key, 1.0, 0.0).astype(BF16)
        rows = jnp.dot(hits[:CAP, :], x_ref[...], preferred_element_type=F32).astype(BF16)
        names = lax.dot_general(slot, hits[...], NT, preferred_element_type=F32)[:1]
        return rows, jnp.where(iota((1, 256), 1) == 255, flag, names)

    def z_copy(out, into, i, there):
        return pltpu.make_async_remote_copy(
            src_ref=out.at[there], dst_ref=into.at[z], send_sem=z_send.at[i], recv_sem=z_recv.at[i, z],
            device_id=(g, x * PLANES + there), device_id_type=MESH)

    first_leg, pass_on, finish_relay = relay_copies(
        rows_out, relay_in, rows_in, relay_send, relay_recv, g, x, z, lambda source: z_recv.at[0, source])

    def prepare(there):
        rows, names = compact(there)
        rows_out[there] = rows
        slots_out[there] = names

    def send_z(k, carry):
        there = (z + near_first(k)) % PLANES
        prepare(there)
        z_copy(rows_out, rows_in, 0, there).start()
        z_copy(slots_out, slots_in, 1, there).start()
        return carry

    pl.semaphore_wait(barrier, PLANES + LINES - 2)
    lax.fori_loop(0, 4, send_z, 0)
    opposite = (z + 4) % PLANES
    prepare(opposite)
    for copy in first_leg():
        copy.start()
    z_copy(slots_out, slots_in, 1, opposite).start()
    lax.fori_loop(4, 6, send_z, 0)
    rows, names = compact(z)
    rows_in[z] = rows
    slots_in[z] = names

    def own_copy(source):
        return pltpu.make_async_copy(
            blocks(line_out, source * LINES + g * 4 + x, 1), blocks(inbox, (g * 4 + x) * PLANES + source, 1),
            own_sem.at[source])

    def forward(source):
        wide = rows_in[source].astype(F32)
        scale = lax.rsqrt(jnp.mean(wide * wide, axis=-1, keepdims=True) + 1e-06)
        names = slots_in[source][:, :CAP].astype(jnp.int32) - 1
        hit = jnp.where(iota((256, CAP), 0) == names, 1.0, 0.0)
        filled = jnp.sum(hit, axis=1, keepdims=True)
        rows = jnp.dot(hit.astype(BF16), (wide * scale).astype(BF16), preferred_element_type=F32)
        first = jnp.where((iota((256, 128), 1) == 0) & (filled < 0.5), EMPTY, rows[:, :128])
        left = jnp.concatenate([first, rows[:, 128:half]], axis=1).reshape(LINES, 1, 8, half)
        right = rows[:, half:].reshape(LINES, 1, 8, half)
        both = jnp.concatenate([left, right], axis=1).reshape(512, half)
        line_out[pl.ds(pl.multiple_of(source * 512, 512), 512), :] = both.astype(BF16)
        own_copy(source).start()

        def send(j, carry):
            tg, tx = on_line(j, g, x)
            pltpu.make_async_remote_copy(
                src_ref=blocks(line_out, source * LINES + tg * 4 + tx, 1),
                dst_ref=blocks(inbox, (g * 4 + x) * PLANES + source, 1),
                send_sem=line_send, recv_sem=line_recv,
                device_id=(tg, tx * PLANES + z), device_id_type=MESH).start()
            return carry

        lax.fori_loop(1, LINES, send, 0)

    forward(z)

    def arrive(k, carry):
        source = (z + PLANES - near_first(k)) % PLANES

        @pl.when(k == 4)
        def _():
            pass_on()

        pltpu.make_async_copy(rows_in.at[source], rows_in.at[source], z_recv.at[0, source]).wait()
        pltpu.make_async_copy(slots_in.at[source], slots_in.at[source], z_recv.at[1, source]).wait()
        forward(source)
        return carry

    lax.fori_loop(0, PLANES - 1, arrive, 0)
    others = PLANES * (LINES - 1)
    sent = rows_out.at[pl.ds(0, PLANES - 2)]
    pltpu.make_async_copy(sent, sent, z_send.at[0]).wait()
    sent = slots_out.at[pl.ds(0, PLANES - 1)]
    pltpu.make_async_copy(sent, sent, z_send.at[1]).wait()
    finish_relay()
    pltpu.make_async_copy(blocks(line_out, 0, others), blocks(line_out, 0, others), line_send).wait()
    pltpu.make_async_copy(blocks(inbox, 0, others), blocks(inbox, 0, others), line_recv).wait()

    def finish(source, carry):
        own_copy(source).wait()
        return carry

    lax.fori_loop(0, PLANES, finish, 0)


def restore_kernel(results, soft_ref, slots_ref, rows_back, soft_back, flag_ref, line_in, soft_out, soft_in, rows_out,
                   relay_in, names_out, z_send, z_recv, relay_send, relay_recv, line_send, line_recv, soft_sem, own_sem):
    g, x, z = place()
    me = g * 4 + x
    half = results.shape[1]
    flag = jnp.max(jnp.where(iota((PLANES, 1, 256), 2) == 255, slots_ref[...], 0.0))
    soft_out[...] = jnp.where(iota(soft_out.shape, 2) < 64, soft_ref[...], flag)
    soft_in[me] = soft_out[me]

    def send_soft(j, carry):
        tg, tx = on_line(j, g, x)
        pltpu.make_async_remote_copy(
            src_ref=soft_out.at[tg * 4 + tx], dst_ref=soft_in.at[me], send_sem=soft_sem.at[0],
            recv_sem=soft_sem.at[1], device_id=(tg, tx * PLANES + z), device_id_type=MESH).start()
        return carry

    lax.fori_loop(1, LINES, send_soft, 0)

    def own_copy(home):
        return pltpu.make_async_copy(
            blocks(results, me * PLANES + home, 1), blocks(line_in, home * LINES + me, 1), own_sem.at[home])

    def home_of(k):
        return (z + far_first(k)) % PLANES

    def send_line(k, carry):
        home = home_of(k)
        own_copy(home).start()

        def send(j, inner):
            tg, tx = on_line(j, g, x)
            pltpu.make_async_remote_copy(
                src_ref=blocks(results, (tg * 4 + tx) * PLANES + home, 1),
                dst_ref=blocks(line_in, home * LINES + me, 1),
                send_sem=line_send, recv_sem=line_recv.at[home],
                device_id=(tg, tx * PLANES + z), device_id_type=MESH).start()
            return inner

        return lax.fori_loop(1, LINES, send, carry)

    lax.fori_loop(0, 3, send_line, 0)
    first = soft_in.at[pl.ds(0, LINES - 1)]
    pltpu.make_async_copy(first, first, soft_sem.at[1]).wait()
    all_soft = soft_in[...].reshape(LINES, 128)
    flag_ref[...] = jnp.broadcast_to(jnp.max(all_soft[:, 64:], axis=(0, 1), keepdims=True), flag_ref.shape)
    spread = jnp.where(iota((256, LINES), 0) // 8 == iota((256, LINES), 1), 1.0, 0.0).astype(BF16)
    all_soft = jnp.dot(spread, all_soft.astype(BF16), preferred_element_type=F32)

    def settle_home(home):
        arrived = blocks(line_in, home * LINES, LINES - 1)
        pltpu.make_async_copy(arrived, arrived, line_recv.at[home]).wait()
        own_copy(home).wait()
        both = line_in[pl.ds(pl.multiple_of(home * 512, 512), 512), :].astype(F32).reshape(LINES, 2, 8, half)
        left, right = both[:, 0].reshape(256, half).astype(BF16), both[:, 1].reshape(256, half).astype(BF16)
        names = slots_ref[home]
        column = as_column(names)[:CAP] - 1.0
        lane = iota((CAP, 128), 1).astype(F32)
        hit = jnp.concatenate(
            [jnp.where(column == lane + float(s), 1.0, 0.0).astype(BF16) for s in (0, 128)], axis=1)
        mine = jnp.where(iota((256, 128), 1) == home * 8 + iota((256, 128), 0) % 8, all_soft, 0.0).astype(BF16)
        values = lax.dot_general(jnp.ones((16, 128), BF16), mine, NT, preferred_element_type=F32)
        picked = jnp.where(iota((256, 256), 0) == names.astype(jnp.int32) - 1, 1.0, 0.0).astype(BF16)
        picked = jnp.dot(values.astype(BF16), picked, preferred_element_type=F32)[:1]
        left = jnp.dot(hit, left, preferred_element_type=F32).astype(BF16)
        right = jnp.dot(hit, right, preferred_element_type=F32).astype(BF16)
        return left, right, picked

    first_leg, pass_on, finish_relay = relay_copies(
        rows_out, relay_in, rows_back, relay_send, relay_recv, g, x, z, lambda source: z_recv.at[0])

    def z_copy(out, into, i, home):
        return pltpu.make_async_remote_copy(
            src_ref=out.at[home], dst_ref=into.at[z], send_sem=z_send.at[i], recv_sem=z_recv.at[i],
            device_id=(g, x * PLANES + home), device_id_type=MESH)

    def send_z(k, carry):
        home = home_of(k)
        left, right, picked = settle_home(home)
        rows_out[home, :, :half] = left
        rows_out[home, :, half:] = right
        names_out[home] = picked
        z_copy(names_out, soft_back, 1, home).start()

        @pl.when(k == 0)
        def _():
            for copy in first_leg():
                copy.start()

        @pl.when(k > 0)
        def _():
            z_copy(rows_out, rows_back, 0, home).start()

        @pl.when(k == 3)
        def _():
            pass_on()

        @pl.when(k < PLANES - 3)
        def _():
            send_line(k + 3, 0)

        return carry

    lax.fori_loop(0, PLANES - 1, send_z, 0)
    left, right, picked = settle_home(z)
    rows_back[z, :, :half] = left
    rows_back[z, :, half:] = right
    soft_back[z] = picked

    others = PLANES * (LINES - 1)
    sent = soft_out.at[pl.ds(0, LINES - 1)]
    pltpu.make_async_copy(sent, sent, soft_sem.at[0]).wait()
    pltpu.make_async_copy(blocks(results, 0, others), blocks(results, 0, others), line_send).wait()
    sent = rows_out.at[pl.ds(0, PLANES - 2)]
    pltpu.make_async_copy(sent, sent, z_send.at[0]).wait()
    sent = names_out.at[pl.ds(0, PLANES - 1)]
    pltpu.make_async_copy(sent, sent, z_send.at[1]).wait()
    finish_relay()
    for i, into in enumerate((rows_back, soft_back)):
        came = into.at[pl.ds(0, PLANES - 1)]
        pltpu.make_async_copy(came, came, z_recv.at[i]).wait()


def place_kernel(where_ref, in_ref, soft_in_ref, soft_ref, out_ref):
    rows = out_ref.shape[0]
    plane, position = where_ref[0:1, :], where_ref[1:2, :]
    column = as_column(plane * CAP + position)
    lane = iota((rows, 128), 1).astype(F32)
    hit = jnp.concatenate(
        [jnp.where(column == lane + float(s), 1.0, 0.0).astype(BF16) for s in range(0, PLANES * CAP, 128)], axis=1)
    combined = in_ref[...].reshape(PLANES * CAP, in_ref.shape[2])
    out_ref[...] = jnp.dot(hit, combined, preferred_element_type=F32).astype(BF16)

    spot = jnp.where(iota((256, rows), 0).astype(F32) == position, 1.0, 0.0).astype(BF16)
    soft = soft_in_ref[...].reshape(PLANES, 256)
    soft = jnp.concatenate([soft, jnp.zeros((8, 256), F32)], axis=0).astype(BF16)
    found = jnp.dot(soft, spot, preferred_element_type=F32)[:PLANES]
    chosen = jnp.where(iota((PLANES, rows), 0).astype(F32) == plane, found, 0.0)
    soft_ref[...] = jnp.sum(chosen, axis=0, keepdims=True).astype(BF16)


def whole_kernel(sharp_ref, ids_ref, x_ref, soft_max, neighbour, flag_ref, inbox, where_ref, slots_in, hits,
                 rows_out, rows_in, relay_in, slots_out, line_out, members, results, soft, line_in, soft_out, soft_in,
                 back_out, back_in, relay_back, names_out, names_in, z_send, z_recv, relay_send, relay_recv, line_send,
                 line_recv, own_sem, z_send_b, z_recv_b, relay_send_b, relay_recv_b, line_send_b, line_recv_b, soft_sem,
                 own_sem_b):
    collect_kernel(ids_ref, x_ref, inbox, where_ref, slots_in, hits, rows_out, rows_in, relay_in, slots_out, line_out,
                   z_send, z_recv, relay_send, relay_recv, line_send, line_recv, own_sem)
    settle_kernel(PLANES, sharp_ref, inbox, line_out, soft, members, results)
    restore_kernel(line_out, soft, slots_in, back_in, names_in, flag_ref, line_in, soft_out, soft_in, back_out,
                   relay_back, names_out, z_send_b, z_recv_b, relay_send_b, relay_recv_b, line_send_b, line_recv_b,
                   soft_sem, own_sem_b)
    for r in range(0, neighbour.shape[0], 256):
        rows = pl.ds(r, 256)
        place_kernel(where_ref.at[:, rows], back_in, names_in, soft_max.at[:, rows], neighbour.at[rows])


def whole(sharp, ids, x):
    count, features = x.shape
    half = features // 2
    slots = PLANES * LINES * BLOCK
    vmem = pl.BlockSpec(memory_space=pltpu.VMEM)
    lines = pltpu.VMEM((slots, half), BF16)
    rows = pltpu.VMEM((PLANES, CAP, features), BF16)
    halves = pltpu.VMEM((2, CAP // 2, features), BF16)
    names = pltpu.VMEM((PLANES, 1, 256), F32)
    soft = pltpu.VMEM((LINES, 1, 128), F32)
    members = pltpu.VMEM((4, slots // 8, features), BF16)
    dma = pltpu.SemaphoreType.DMA
    return pl.pallas_call(
        whole_kernel,
        in_specs=[pl.BlockSpec(memory_space=pltpu.SMEM), vmem, vmem],
        out_specs=[vmem] * 3,
        out_shape=[
            jax.ShapeDtypeStruct((1, count), BF16),
            jax.ShapeDtypeStruct((count, features), BF16),
            jax.ShapeDtypeStruct((8, 128), F32),
        ],
        scratch_shapes=[
            lines, pltpu.VMEM((8, count), F32), names, pltpu.VMEM((256, count), BF16),
            rows, rows, halves, names, lines, members, members, soft, lines, soft, soft,
            rows, rows, halves, names, names,
            dma((2,)), dma((2, PLANES)), dma((4,)), dma((2,)), dma, dma, dma((PLANES,)),
            dma((2,)), dma((2,)), dma((4,)), dma((2,)), dma, dma((PLANES,)), dma((2,)), dma((PLANES,)),
        ],
        compiler_params=pltpu.CompilerParams(
            collective_id=2, has_side_effects=True, vmem_limit_bytes=48 * 2**20),
        name="whole",
    )(sharp, ids, x)


def by_all_slots(n, embeddings, cluster_ids, sharp):
    clusters = sharp.shape[0]
    outbox, dest = pack(cluster_ids[None, :], embeddings, clusters * SRC_CAP)
    (arrived,) = exchange(n, 0, outbox)
    results, soft = settle(sharp, arrived, n, clusters // n, 1)
    returned, soft_returned = exchange(n, 1, results, soft)
    return unpack(dest, returned, soft_returned)


def body(n, embeddings, cluster_ids, sharpness):
    sharp = sharpness.astype(F32)
    soft_max, neighbour, flag = whole(sharp, cluster_ids[None, :], embeddings)
    soft_max, neighbour = lax.cond(
        flag[0, 0] > 0.5,
        lambda: tuple(by_all_slots(n, embeddings, cluster_ids, sharp)),
        lambda: (soft_max, neighbour),
    )
    return (soft_max[0], neighbour)


def solution(mesh):
    n = mesh.size
    return jax.shard_map(
        functools.partial(body, n),
        mesh=mesh,
        in_specs=(P(("group", "dev"), None), P(("group", "dev")), P()),
        out_specs=(P(("group", "dev")), P(("group", "dev"), None)),
        check_vma=False,
    )
```

```python
import functools

import jax
import jax.numpy as jnp
from jax import lax
from jax.experimental import pallas as pl
from jax.experimental.pallas import tpu as pltpu
from jax.sharding import PartitionSpec as P

MESH = pl.DeviceIdType.MESH
SRC_CAP = 2
EMPTY = 1024.0
NEGATIVE = -1e30
NT = (((1,), (1,)), ((), ()))
F32 = jnp.float32
BF16 = jnp.bfloat16


def iota(shape, dim):
    return lax.broadcasted_iota(jnp.int32, shape, dim)


def as_column(row, lanes=128):
    return jnp.transpose(jnp.broadcast_to(row, (lanes, row.shape[1])))


def pack_kernel(ids_ref, x_ref, out_ref, dest_ref, normed):
    step = pl.program_id(0)
    count, features = x_ref.shape
    half = features // 2
    slots = out_ref.shape[0] // 2

    @pl.when(step == 0)
    def _():
        ids = ids_ref[...]
        columns = as_column(ids.astype(F32))
        ordinal = jnp.zeros((1, count), F32)
        for r in range(0, count, 128):
            block = jnp.concatenate([columns[r:r + 128]] * (count // 128), axis=1)
            same = block == ids.astype(F32)
            before = iota((128, count), 0) + r < iota((128, count), 1)
            ordinal += jnp.sum(jnp.where(same & before, 1.0, 0.0), axis=0, keepdims=True)
        dest_ref[...] = ids * SRC_CAP + ordinal.astype(jnp.int32)
        for r in range(0, count, 256):
            wide = x_ref[r:r + 256, :].astype(F32)
            scale = lax.rsqrt(jnp.mean(wide * wide, axis=-1, keepdims=True) + 1e-06)
            normed[r:r + 256, :] = (wide * scale).astype(BF16)

    dest = dest_ref[...]
    hit = jnp.where(iota((slots, count), 0) + step * slots == dest, 1.0, 0.0)
    filled = jnp.sum(hit, axis=1, keepdims=True)
    rows = jnp.dot(hit.astype(BF16), normed[...], preferred_element_type=F32)
    first = jnp.where((iota((slots, 128), 1) == 0) & (filled < 0.5), EMPTY, rows[:, :128])
    left = jnp.concatenate([first, rows[:, 128:half]], axis=1).reshape(slots // 8, 1, 8, half)
    right = rows[:, half:].reshape(slots // 8, 1, 8, half)
    both = jnp.concatenate([left, right], axis=1).reshape(slots * 2, half)
    out_ref[...] = both.astype(BF16)


def pack(ids, x, slots_all):
    count, features = x.shape
    steps = 8
    slots = slots_all // steps
    return pl.pallas_call(
        pack_kernel,
        grid=(steps,),
        in_specs=[
            pl.BlockSpec((1, count), lambda i: (0, 0)),
            pl.BlockSpec((count, features), lambda i: (0, 0)),
        ],
        out_specs=[
            pl.BlockSpec((slots * 2, features // 2), lambda i: (i, 0)),
            pl.BlockSpec((1, count), lambda i: (0, 0)),
        ],
        out_shape=[
            jax.ShapeDtypeStruct((slots_all * 2, features // 2), BF16),
            jax.ShapeDtypeStruct((1, count), jnp.int32),
        ],
        scratch_shapes=[pltpu.VMEM((count, features), BF16)],
        compiler_params=pltpu.CompilerParams(vmem_limit_bytes=32 * 2**20),
        name="pack",
    )(ids, x)


def partner(k, g, d):
    q = (k * 101) % 256
    z = (d % 8 + q % 8) % 8
    x = (d // 8 + (q // 8) % 4) % 4
    y = (g // 2 + (q // 32) % 4) % 4
    core = (g % 2 + q // 128) % 2
    return y * 2 + core, x * 8 + z


def exchange_kernel(n, *refs):
    count = (len(refs) - 3) // 2
    sources, targets = refs[:count], refs[count:2 * count]
    send_sem, recv_sem, own_sem = refs[2 * count:]
    g, d = lax.axis_index("group"), lax.axis_index("dev")
    me = g * 32 + d

    def part(ref, start, blocks):
        size = ref.shape[0] // n
        return ref.at[pl.ds(pl.multiple_of(start * size, size), blocks * size)]

    barrier = pltpu.get_barrier_semaphore()

    def greet(k, carry):
        tg, td = partner(k, g, d)
        pl.semaphore_signal(barrier, inc=1, device_id=(tg, td), device_id_type=MESH)
        return carry

    lax.fori_loop(1, n, greet, 0)
    own = [
        pltpu.make_async_copy(part(s, me, 1), part(t, me, 1), own_sem.at[i])
        for i, (s, t) in enumerate(zip(sources, targets))
    ]
    for copy in own:
        copy.start()
    pl.semaphore_wait(barrier, n - 1)

    def send(k, carry):
        tg, td = partner(k, g, d)
        for i, (s, t) in enumerate(zip(sources, targets)):
            pltpu.make_async_remote_copy(
                src_ref=part(s, tg * 32 + td, 1),
                dst_ref=part(t, me, 1),
                send_sem=send_sem.at[i],
                recv_sem=recv_sem.at[i],
                device_id=(tg, td),
                device_id_type=MESH,
            ).start()
        return carry

    lax.fori_loop(1, n, send, 0)
    for i, (s, t) in enumerate(zip(sources, targets)):
        pltpu.make_async_copy(part(s, 0, n - 1), part(s, 0, n - 1), send_sem.at[i]).wait()
        pltpu.make_async_copy(part(t, 0, n - 1), part(t, 0, n - 1), recv_sem.at[i]).wait()
    for copy in own:
        copy.wait()


def exchange(n, collective_id, *arrays):
    return pl.pallas_call(
        functools.partial(exchange_kernel, n),
        in_specs=[pl.BlockSpec(memory_space=pl.ANY)] * len(arrays),
        out_specs=[pl.BlockSpec(memory_space=pl.ANY)] * len(arrays),
        out_shape=[jax.ShapeDtypeStruct(a.shape, a.dtype) for a in arrays],
        scratch_shapes=[pltpu.SemaphoreType.DMA((len(arrays),))] * 3,
        compiler_params=pltpu.CompilerParams(collective_id=collective_id, has_side_effects=True),
        name="exchange",
    )(*arrays)


def settle_kernel(per_line, sharp_ref, in_ref, out_ref, soft_ref, members, results):
    me = lax.axis_index("group") * 32 + lax.axis_index("dev")
    owned, span, features = members.shape
    half = features // 2
    chunk = 16

    def source_row(o):
        return (o % 32) // 2 * 16 + o // 128 * 8 + (o % 128) // 32 * 2 + o % 2

    inward = jnp.where(source_row(iota((256, 256), 0)) == iota((256, 256), 1), 1.0, 0.0).astype(BF16)
    outward = jnp.where(source_row(iota((256, 256), 1)) == iota((256, 256), 0), 1.0, 0.0).astype(BF16)

    def gather(b, carry):
        arrived = in_ref[pl.ds(pl.multiple_of(b * 256, 256), 256), :]
        placed = jnp.dot(inward, arrived, preferred_element_type=F32).astype(BF16)
        rows = pl.ds(pl.multiple_of(b * 32, 32), 32)
        for c in range(owned):
            members[c, rows, :half] = placed[c * 32:(c + 1) * 32]
            members[c, rows, half:] = placed[128 + c * 32:128 + (c + 1) * 32]
        return carry

    lax.fori_loop(0, span // 32, gather, 0, unroll=4)

    off_diagonal = iota((span, span), 0) != iota((span, span), 1)
    first = jnp.where(iota((16, 128), 1) == 0, 1.0, 0.0).astype(BF16)
    source = iota((span, 128), 0) // 2
    lane = iota((span, 128), 1) - source % per_line * 8 - iota((span, 128), 0) % 2
    soft = jnp.zeros((span, 128), F32)
    for c in range(owned):
        sharp = sharp_ref[me * owned + c]
        rows = members[c]
        marks = lax.dot_general(first, rows[:, :128], NT, preferred_element_type=F32)[:1]
        dots = lax.dot_general(rows, rows, NT, preferred_element_type=F32)
        masked = jnp.where(off_diagonal & (marks < EMPTY / 2), dots * (sharp * (1.0 / features)), NEGATIVE)
        highest = jnp.maximum(jnp.max(masked, axis=1, keepdims=True), 0.0)
        weights = jnp.exp(masked - highest)
        total = jnp.exp(-highest) + jnp.sum(weights, axis=1, keepdims=True)
        soft = jnp.where(lane == 2 * c, (highest + jnp.log(total)) / sharp, soft)
        summed = jnp.dot(weights.astype(BF16), rows, preferred_element_type=F32)
        results[c] = (summed * (1.0 / total)).astype(BF16)

    lines = soft_ref.shape[0]
    pick = jnp.where(iota((lines, span), 1) // (2 * per_line) == iota((lines, span), 0), 1.0, 0.0).astype(BF16)
    spread = jnp.dot(pick, soft.astype(BF16), preferred_element_type=F32)
    soft_ref[...] = spread.reshape(soft_ref.shape)

    def scatter(b, carry):
        rows = pl.ds(pl.multiple_of(b * 32, 32), 32)
        placed = jnp.concatenate(
            [results[c, rows, :half] for c in range(owned)] + [results[c, rows, half:] for c in range(owned)],
            axis=0,
        )
        back = jnp.dot(outward, placed, preferred_element_type=F32)
        out_ref[pl.ds(pl.multiple_of(b * 256, 256), 256), :] = back.astype(BF16)
        return carry

    lax.fori_loop(0, span // 32, scatter, 0, unroll=4)


def settle(sharp, arrived, n, owned, per_line):
    rows, half = arrived.shape
    span = n * SRC_CAP
    return pl.pallas_call(
        functools.partial(settle_kernel, per_line),
        in_specs=[pl.BlockSpec(memory_space=pltpu.SMEM), pl.BlockSpec(memory_space=pltpu.VMEM)],
        out_specs=[pl.BlockSpec(memory_space=pltpu.VMEM)] * 2,
        out_shape=[
            jax.ShapeDtypeStruct((rows, half), BF16),
            jax.ShapeDtypeStruct((n // per_line, 1, 128), F32),
        ],
        scratch_shapes=[
            pltpu.VMEM((owned, span, half * 2), BF16),
            pltpu.VMEM((owned, span, half * 2), BF16),
        ],
        compiler_params=pltpu.CompilerParams(vmem_limit_bytes=40 * 2**20),
        name="settle",
    )(sharp, arrived)


def unpack_kernel(dest_ref, in_ref, soft_in_ref, soft_ref, out_ref, combined, soft_all):
    step = pl.program_id(0)
    slots, features = combined.shape
    half = features // 2
    n = soft_in_ref.shape[0]
    rows = out_ref.shape[0]

    @pl.when(step == 0)
    def _():
        def split(b, carry):
            block = in_ref[pl.ds(pl.multiple_of(b * 512, 512), 512), :].astype(F32).reshape(32, 2, 8, half)
            place = pl.ds(pl.multiple_of(b * 256, 256), 256)
            combined[place, :half] = block[:, 0].reshape(256, half).astype(BF16)
            combined[place, half:] = block[:, 1].reshape(256, half).astype(BF16)
            return carry

        lax.fori_loop(0, slots // 256, split, 0)
        soft_all[...] = jnp.transpose(soft_in_ref[...].reshape(n, 128)).astype(BF16)

    dest = dest_ref[...]
    column = as_column(dest.astype(F32))
    lane = iota((rows, 128), 1).astype(F32)
    hit = jnp.concatenate(
        [jnp.where(column == lane + float(s), 1.0, 0.0).astype(BF16) for s in range(0, slots, 128)], axis=1
    )
    out_ref[...] = jnp.dot(hit, combined[...], preferred_element_type=F32).astype(BF16)

    owner = jnp.where(iota((n, rows), 0) == dest // 8, 1.0, 0.0).astype(BF16)
    found = jnp.dot(soft_all[...], owner, preferred_element_type=F32)[:8]
    chosen = jnp.where(iota((8, rows), 0) == dest % 8, found, 0.0)
    soft_ref[...] = jnp.sum(chosen, axis=0, keepdims=True).astype(BF16)


def unpack(dest, returned, soft_returned):
    count = dest.shape[1]
    n = soft_returned.shape[0]
    blocks, half = returned.shape
    slots, features = blocks // 2, half * 2
    rows = 256
    return pl.pallas_call(
        unpack_kernel,
        grid=(count // rows,),
        in_specs=[
            pl.BlockSpec((1, rows), lambda i: (0, i)),
            pl.BlockSpec((blocks, half), lambda i: (0, 0)),
            pl.BlockSpec((n, 1, 128), lambda i: (0, 0, 0)),
        ],
        out_specs=[
            pl.BlockSpec((1, rows), lambda i: (0, i)),
            pl.BlockSpec((rows, features), lambda i: (i, 0)),
        ],
        out_shape=[
            jax.ShapeDtypeStruct((1, count), BF16),
            jax.ShapeDtypeStruct((count, features), BF16),
        ],
        scratch_shapes=[pltpu.VMEM((slots, features), BF16), pltpu.VMEM((128, n), BF16)],
        compiler_params=pltpu.CompilerParams(vmem_limit_bytes=40 * 2**20),
        name="unpack",
    )(dest, returned, soft_returned)


PLANES = 8
LINES = 32
CAP = 160
FRONT = 96
BACK = 88
BLOCK = 16


def blocks(ref, h, start, count):
    return ref.at[h, pl.ds(pl.multiple_of(start * BLOCK, BLOCK), count * BLOCK)]


def pair(m):
    return (m + 1) % 4, 7 - m


def place():
    g, d = lax.axis_index("group"), lax.axis_index("dev")
    return g, d // PLANES, d % PLANES


def other_lines(g, x):
    ys = [(g // 2 + i) % 4 for i in range(4)]
    cores = [(g % 2 + i) % 2 for i in range(2)]
    xs = [(x + i) % 4 for i in range(4)]
    mixed = [(j * 11) % LINES for j in range(1, LINES)]
    return [(ys[q // 2 % 4] * 2 + cores[q % 2], xs[q // 8]) for q in mixed]


def greet_all(g, x, z):
    barrier = pltpu.get_barrier_semaphore()

    def greet_z(k, carry):
        there = (g, x * PLANES + (z + k) % PLANES)
        pl.semaphore_signal(barrier, inc=1, device_id=there, device_id_type=MESH)
        return carry

    lax.fori_loop(1, PLANES, greet_z, 0)
    for tg, tx in other_lines(g, x):
        pl.semaphore_signal(barrier, inc=1, device_id=(tg, tx * PLANES + z), device_id_type=MESH)
    return barrier


def relay(out_at, relay_at, into_at, send_sems, recv_sems, arrive_sem, g, x, z):
    hops = (2, PLANES - 2)

    def there(hop):
        return (g, x * PLANES + (z + hop) % PLANES)

    def first(way):
        return pltpu.make_async_remote_copy(
            src_ref=out_at(way), dst_ref=relay_at(way), send_sem=send_sems.at[way], recv_sem=recv_sems.at[way],
            device_id=there(hops[way]), device_id_type=MESH)

    def second(way):
        source = (z + PLANES - hops[way]) % PLANES
        return pltpu.make_async_remote_copy(
            src_ref=relay_at(way), dst_ref=into_at(source, way), send_sem=send_sems.at[2 + way],
            recv_sem=arrive_sem(source), device_id=there(hops[way]), device_id_type=MESH)

    def start():
        for way in range(2):
            first(way).start()

    def pass_on():
        for way in range(2):
            pltpu.make_async_copy(relay_at(way), relay_at(way), recv_sems.at[way]).wait()
            second(way).start()

    def finish():
        for way in range(2):
            first(way).wait_send()
            second(way).wait_send()

    return start, pass_on, finish


def target(shape, dim, h, sel):
    o = iota(shape, dim)
    return jnp.where(o // 4 % 2 == sel, h * 128 + o // 8 * 4 + o % 4 + 1, -5)


def source_row(o):
    return o % 64 // 4 * 16 + o // 128 * 8 + o % 4 // 2 * 4 + o % 128 // 64 * 2 + o % 2


def score_half(h, sharp_ref, owner, inbox, outbox, soft_ref, members, results):
    owned, span, features = members.shape
    half = features // 2
    inward = jnp.where(source_row(iota((256, 256), 0)) == iota((256, 256), 1), 1.0, 0.0).astype(BF16)
    outward = jnp.where(source_row(iota((256, 256), 1)) == iota((256, 256), 0), 1.0, 0.0).astype(BF16)

    def gather(b, carry):
        arrived = inbox[h, pl.ds(pl.multiple_of(b * 256, 256), 256), :]
        placed = jnp.dot(inward, arrived, preferred_element_type=F32).astype(BF16)
        rows = pl.ds(pl.multiple_of(b * 64, 64), 64)
        for c in range(owned):
            members[c, rows, :half] = placed[c * 64:(c + 1) * 64]
            members[c, rows, half:] = placed[128 + c * 64:128 + (c + 1) * 64]
        return carry

    lax.fori_loop(0, span // 64, gather, 0, unroll=4)

    off_diagonal = iota((span, span), 0) != iota((span, span), 1)
    first = jnp.where(iota((16, 128), 1) == 0, 1.0, 0.0).astype(BF16)
    row = iota((span, 128), 0)
    lane = iota((span, 128), 1) - (row // 4 % 4 * 8 + row // 2 % 2 * 4 + row % 2)
    soft = jnp.zeros((span, 128), F32)
    for c in range(owned):
        sharp = sharp_ref[owner * 4 + 2 * h + c]
        rows = members[c]
        marks = lax.dot_general(first, rows[:, :128], NT, preferred_element_type=F32)[:1]
        dots = lax.dot_general(rows, rows, NT, preferred_element_type=F32)
        masked = jnp.where(off_diagonal & (marks < EMPTY / 2), dots * (sharp * (1.0 / features)), NEGATIVE)
        highest = jnp.maximum(jnp.max(masked, axis=1, keepdims=True), 0.0)
        weights = jnp.exp(masked - highest)
        total = jnp.exp(-highest) + jnp.sum(weights, axis=1, keepdims=True)
        soft = jnp.where(lane == 2 * c, (highest + jnp.log(total)) / sharp, soft)
        summed = jnp.dot(weights.astype(BF16), rows, preferred_element_type=F32)
        results[c] = (summed * (1.0 / total)).astype(BF16)

    pick = jnp.where(iota((LINES, span), 1) // 16 == iota((LINES, span), 0), 1.0, 0.0).astype(BF16)
    spread = jnp.dot(pick, soft.astype(BF16), preferred_element_type=F32)
    soft_ref[h] = spread.reshape(soft_ref.shape[1:])

    def scatter(b, carry):
        rows = pl.ds(pl.multiple_of(b * 64, 64), 64)
        placed = jnp.concatenate(
            [results[c, rows, :half] for c in range(owned)] + [results[c, rows, half:] for c in range(owned)],
            axis=0,
        )
        back = jnp.dot(outward, placed, preferred_element_type=F32)
        outbox[h, pl.ds(pl.multiple_of(b * 256, 256), 256), :] = back.astype(BF16)
        return carry

    lax.fori_loop(0, span // 64, scatter, 0, unroll=4)


def whole_kernel(sharp_ref, ids_ref, x_ref, soft_max, neighbour, flag_ref,
                 where_ref, hits, rows_out, rows_in, relay_a, relay_b, slots_out, slots_in, line_out, inbox,
                 members, results, outbox, line_in, soft_out, soft_in, back_out, back_in, back_relay, names_out,
                 names_in, combined, spots,
                 z_send, z_recv, slot_send, slot_recv, relay_send, relay_recv, line_send, line_recv, own_sem,
                 soft_send, soft_recv, back_line_send, back_line_recv, back_own_sem, back_send, back_recv,
                 name_send, name_recv, back_relay_send, back_relay_recv):
    g, x, z = place()
    lines = other_lines(g, x)
    me = g * 4 + x
    count, features = x_ref.shape
    half = features // 2
    barrier = greet_all(g, x, z)

    ids = ids_ref[...]
    columns = as_column(ids.astype(F32)).astype(jnp.int32)
    plane = jnp.right_shift(ids, 2) & (PLANES - 1)
    second = jnp.right_shift(ids, 1) & 1
    group = jnp.right_shift(ids, 1) & 15
    group_columns = jnp.right_shift(columns, 1) & 15
    before = iota((128, 128), 0) < iota((128, 128), 1)
    ordinal, rank = [], []
    for t in range(0, count, 128):
        same = jnp.zeros((128, 128), F32)
        beside = jnp.zeros((128, 128), F32)
        for r in range(0, t + 128, 128):
            alike = columns[r:r + 128] == ids[:, t:t + 128]
            near = group_columns[r:r + 128] == group[:, t:t + 128]
            if r == t:
                alike, near = alike & before, near & before
            same += jnp.where(alike, 1.0, 0.0)
            beside += jnp.where(near, 1.0, 0.0)
        ordinal.append(jnp.sum(same, axis=0, keepdims=True))
        rank.append(jnp.sum(beside, axis=0, keepdims=True))
    ordinal, rank = jnp.concatenate(ordinal, axis=1), jnp.concatenate(rank, axis=1)
    in_back = second == 1
    spot = ((second * PLANES + plane) * BACK).astype(F32) + jnp.where(in_back, BACK - 1 - rank, rank)
    soft_lane = jnp.where(in_back, 128 + CAP - 1 - (CAP - FRONT) - rank, rank)
    where_ref[...] = jnp.concatenate(
        [spot, soft_lane, plane.astype(F32), jnp.zeros((5, count), F32)], axis=0)
    loads = jnp.sum(jnp.where(iota((PLANES, count), 0) == plane, 1.0, 0.0), axis=1, keepdims=True)
    flag = jnp.where((jnp.max(rank) > BACK - 0.5) | (jnp.max(loads) > CAP + 0.5), 1.0, 0.0)
    slot = (second * 128 + jnp.right_shift(ids, 5) * 4 + (ids & 1) * SRC_CAP).astype(F32) + ordinal + 1.0
    slot = jnp.broadcast_to(slot, (16, count)).astype(BF16)
    position = jnp.where(in_back, CAP - 1 - rank, rank)
    key = jnp.where(rank < BACK - 0.5, position.astype(jnp.int32) * PLANES + plane, -1)
    hits[FRONT:128, :] = jnp.zeros((128 - FRONT, count), BF16)
    hits[128 + FRONT:, :] = jnp.zeros((128 - FRONT, count), BF16)

    def compact(there):
        line = iota((FRONT, count), 0)
        hits[:FRONT, :] = jnp.where(line * PLANES + there == key, 1.0, 0.0).astype(BF16)
        later = (line + (CAP - FRONT)) * PLANES + there
        hits[128:128 + FRONT, :] = jnp.where(later == key, 1.0, 0.0).astype(BF16)
        names = lax.dot_general(slot, hits[...], NT, preferred_element_type=F32)[:1]
        ahead = jnp.dot(hits[:FRONT, :], x_ref[...], preferred_element_type=F32).astype(BF16)
        behind = jnp.dot(hits[256 - (CAP - FRONT) - 32:224, :], x_ref[...], preferred_element_type=F32).astype(BF16)
        return ahead, behind, jnp.where(iota((1, 256), 1) == 255, flag, names)

    def z_copy(c, there):
        part = pl.ds(0, FRONT) if c == 0 else pl.ds(FRONT, CAP - FRONT)
        return pltpu.make_async_remote_copy(
            src_ref=rows_out.at[there, part], dst_ref=rows_in.at[z, part], send_sem=z_send.at[c],
            recv_sem=z_recv.at[c, z], device_id=(g, x * PLANES + there), device_id_type=MESH)

    def slot_copy(there):
        return pltpu.make_async_remote_copy(
            src_ref=slots_out.at[there], dst_ref=slots_in.at[z], send_sem=slot_send, recv_sem=slot_recv.at[z],
            device_id=(g, x * PLANES + there), device_id_type=MESH)

    opposite = (z + 4) % PLANES

    def forward_relay(c):
        size = (FRONT if c == 0 else CAP - FRONT) // 2
        start = 0 if c == 0 else FRONT
        held = relay_a if c == 0 else relay_b
        return relay(
            lambda way: rows_out.at[opposite, pl.ds(start + way * size, size)],
            lambda way: held.at[way],
            lambda source, way: rows_in.at[source, pl.ds(start + way * size, size)],
            relay_send.at[c], relay_recv.at[c], lambda source: z_recv.at[c, source], g, x, z)

    relays = [forward_relay(0), forward_relay(1)]

    def prepare(there):
        ahead, behind, names = compact(there)
        rows_out[there, :FRONT] = ahead
        rows_out[there, FRONT:] = behind
        slots_out[there] = names

    def send_front(k, carry):
        near = k // 2 + 1
        there = (z + near + (k % 2) * (PLANES - 2 * near)) % PLANES
        prepare(there)
        slot_copy(there).start()
        z_copy(0, there).start()
        return carry

    pl.semaphore_wait(barrier, PLANES + LINES - 2)
    lax.fori_loop(0, 4, send_front, 0)
    prepare(opposite)
    slot_copy(opposite).start()
    relays[0][0]()
    lax.fori_loop(4, 6, send_front, 0)
    ahead, behind, names = compact(z)
    rows_in[z, :FRONT] = ahead
    rows_in[z, FRONT:] = behind
    slots_in[z] = names

    def own_copy(h, m):
        return pltpu.make_async_copy(
            blocks(line_out, h, m * LINES + me, 1), blocks(inbox, h, me * 4 + m, 1), own_sem.at[h, m])

    def forward(h, m):
        rows = jnp.zeros((256, features), F32)
        filled = jnp.zeros((256, 1), F32)
        for sel, offset in enumerate(pair(m)):
            source = (z + PLANES - offset) % PLANES
            wide = rows_in[source, pl.ds(h * (CAP - FRONT), FRONT)].astype(F32)
            scale = lax.rsqrt(jnp.mean(wide * wide, axis=-1, keepdims=True) + 1e-06)
            names = slots_in[source][:, h * 128:h * 128 + FRONT].astype(jnp.int32)
            hit = jnp.where(target((256, FRONT), 0, h, sel) == names, 1.0, 0.0)
            filled += jnp.sum(hit, axis=1, keepdims=True)
            rows += jnp.dot(hit.astype(BF16), (wide * scale).astype(BF16), preferred_element_type=F32)
        first = jnp.where((iota((256, 128), 1) == 0) & (filled < 0.5), EMPTY, rows[:, :128])
        left = jnp.concatenate([first, rows[:, 128:half]], axis=1).reshape(LINES, 1, 8, half)
        right = rows[:, half:].reshape(LINES, 1, 8, half)
        both = jnp.concatenate([left, right], axis=1).reshape(512, half)
        line_out[h, pl.ds(pl.multiple_of(m * 512, 512), 512), :] = both.astype(BF16)
        own_copy(h, m).start()

        for tg, tx in lines:
            pltpu.make_async_remote_copy(
                src_ref=blocks(line_out, h, m * LINES + tg * 4 + tx, 1),
                dst_ref=blocks(inbox, h, me * 4 + m, 1),
                send_sem=line_send.at[h], recv_sem=line_recv.at[h],
                device_id=(tg, tx * PLANES + z), device_id_type=MESH).start()

    def await_rows(c, source):
        part = rows_in.at[source, pl.ds(0, FRONT) if c == 0 else pl.ds(FRONT, CAP - FRONT)]
        pltpu.make_async_copy(part, part, z_recv.at[c, source]).wait()
        if c == 0:
            pltpu.make_async_copy(slots_in.at[source], slots_in.at[source], slot_recv.at[source]).wait()

    def take(h, m):
        @pl.when(m == 2)
        def _():
            relays[h][1]()

        near, far = pair(m)

        @pl.when(m < 3)
        def _():
            await_rows(h, (z + PLANES - near) % PLANES)

        await_rows(h, (z + PLANES - far) % PLANES)

    def forward_first(m, carry):
        take(0, m)

        @pl.when(m < 3)
        def _():
            for offset in pair(m):
                z_copy(1, (z + offset) % PLANES).start()

        @pl.when(m == 1)
        def _():
            relays[1][0]()

        forward(0, m)
        return carry

    lax.fori_loop(0, 4, forward_first, 0)

    def await_lines(h):
        others = blocks(inbox, h, 0, 4 * (LINES - 1))
        pltpu.make_async_copy(others, others, line_recv.at[h]).wait()

        def finish(m, carry):
            own_copy(h, m).wait()
            return carry

        lax.fori_loop(0, 4, finish, 0)

    def back_own_copy(h, m):
        return pltpu.make_async_copy(
            blocks(outbox, h, me * 4 + m, 1), blocks(line_in, h, m * LINES + me, 1), back_own_sem.at[h, m])

    def order(t):
        return (t + 2) * (1 - t // 2) + (3 - t) * (t // 2)

    def send_lines(h):
        line_flag = jnp.max(jnp.where(iota((PLANES, 1, 256), 2) == 255, slots_in[...], 0.0))
        soft_out[h] = jnp.where(iota((LINES, 1, 128), 2) < 64, soft_out[h], line_flag)
        soft_in[h, me] = soft_out[h, me]

        for tg, tx in lines:
            pltpu.make_async_remote_copy(
                src_ref=soft_out.at[h, tg * 4 + tx], dst_ref=soft_in.at[h, me], send_sem=soft_send.at[h],
                recv_sem=soft_recv.at[h], device_id=(tg, tx * PLANES + z), device_id_type=MESH).start()

        def send_pair(t, carry):
            m = order(t)
            back_own_copy(h, m).start()

            for tg, tx in lines:
                pltpu.make_async_remote_copy(
                    src_ref=blocks(outbox, h, (tg * 4 + tx) * 4 + m, 1),
                    dst_ref=blocks(line_in, h, m * LINES + me, 1),
                    send_sem=back_line_send.at[h], recv_sem=back_line_recv.at[h, m],
                    device_id=(tg, tx * PLANES + z), device_id_type=MESH).start()
            return carry

        lax.fori_loop(0, 4, send_pair, 0)

    def back_relay_for(h):
        parts = (pl.ds(0, FRONT), pl.ds(FRONT, 2 * BACK - FRONT))
        return relay(
            lambda way: back_out.at[h, opposite, parts[way]],
            lambda way: back_relay.at[h, parts[way]],
            lambda source, way: back_in.at[h, source, parts[way]],
            back_relay_send.at[h], back_relay_recv.at[h], lambda source: back_recv.at[h], g, x, z)

    back_relays = [back_relay_for(0), back_relay_for(1)]

    def back_copy(h, home):
        return pltpu.make_async_remote_copy(
            src_ref=back_out.at[h, home], dst_ref=back_in.at[h, z], send_sem=back_send.at[h],
            recv_sem=back_recv.at[h], device_id=(g, x * PLANES + home), device_id_type=MESH)

    def name_copy(home):
        return pltpu.make_async_remote_copy(
            src_ref=names_out.at[home], dst_ref=names_in.at[z], send_sem=name_send, recv_sem=name_recv,
            device_id=(g, x * PLANES + home), device_id_type=MESH)

    def await_soft(h):
        others = soft_in.at[h, pl.ds(0, LINES - 1)]
        pltpu.make_async_copy(others, others, soft_recv.at[h]).wait()
        return soft_in[h].reshape(LINES, 128)

    def home_pair(h, m, all_soft):
        arrived = blocks(line_in, h, m * LINES, LINES - 1)
        pltpu.make_async_copy(arrived, arrived, back_line_recv.at[h, m]).wait()
        back_own_copy(h, m).wait()
        both = line_in[h, pl.ds(pl.multiple_of(m * 512, 512), 512), :].astype(F32).reshape(LINES, 2, 8, half)
        left, right = both[:, 0].reshape(256, half).astype(BF16), both[:, 1].reshape(256, half).astype(BF16)
        mine = jnp.where(iota((256, 128), 1) == m * 8 + iota((256, 128), 0) % 8, all_soft, 0.0).astype(BF16)
        values = lax.dot_general(jnp.ones((16, 128), BF16), mine, NT, preferred_element_type=F32).astype(BF16)
        for sel, offset in enumerate(pair(m)):
            home = (z + PLANES - offset) % PLANES
            names = slots_in[home]
            start = 0 if h == 0 else 128 + FRONT - BACK
            column = as_column(names)[start:start + BACK].astype(jnp.int32)
            hit = jnp.concatenate(
                [jnp.where(target((BACK, 256), 1, h, sel)[:, s:s + 128] == column, 1.0, 0.0) for s in (0, 128)],
                axis=1).astype(BF16)
            picked = jnp.where(target((256, 256), 0, h, sel) == names.astype(jnp.int32), 1.0, 0.0).astype(BF16)
            picked = jnp.dot(values, picked, preferred_element_type=F32)[:1]
            packed = jnp.concatenate(
                [jnp.dot(hit, left, preferred_element_type=F32), jnp.dot(hit, right, preferred_element_type=F32)],
                axis=0).astype(BF16)
            back_out[h, home] = packed
            names_out[home] = picked if h == 0 else names_out[home] + picked
            if sel == 1 and h == 1:
                name_copy(home).start()
            if sel == 0:
                @pl.when(m < 3)
                def _():
                    back_copy(h, home).start()
                    if h == 1:
                        name_copy(home).start()

                @pl.when(m == 3)
                def _():
                    back_in[h, z] = packed
                    if h == 1:
                        names_in[z] = names_out[z]
            else:
                @pl.when(m < 3)
                def _():
                    back_copy(h, home).start()

                @pl.when(m == 3)
                def _():
                    back_relays[h][0]()

    def spread_soft(h):
        rows = await_soft(h)
        pick = jnp.where(iota((256, LINES), 0) // 8 == iota((256, LINES), 1), 1.0, 0.0).astype(BF16)
        return rows, jnp.dot(pick, rows.astype(BF16), preferred_element_type=F32)

    def await_back(h):
        came = back_in.at[h, pl.ds(0, PLANES - 1)]
        pltpu.make_async_copy(came, came, back_recv.at[h]).wait()

        def repack(i, carry):
            two = back_in[h, pl.ds(i * 2, 2)].astype(F32).reshape(2, 2, BACK, half)
            rows = pl.ds(pl.multiple_of((h * 4 + i) * 2 * BACK, 2 * BACK), 2 * BACK)
            combined[rows, :half] = two[:, 0].reshape(2 * BACK, half).astype(BF16)
            combined[rows, half:] = two[:, 1].reshape(2 * BACK, half).astype(BF16)
            return carry

        lax.fori_loop(0, PLANES // 2, repack, 0)

    await_lines(0)
    score_half(0, sharp_ref, me * PLANES + z, inbox, outbox, soft_out, members, results)
    send_lines(0)
    rows, all_soft = spread_soft(0)
    flag_ref[...] = jnp.broadcast_to(jnp.max(rows[:, 64:], axis=(0, 1), keepdims=True), flag_ref.shape)

    def cross(t, carry):
        take(1, t)
        forward(1, t)
        home_pair(0, order(t), carry)
        return carry

    lax.fori_loop(0, 4, cross, all_soft)
    back_relays[0][1]()
    await_lines(1)
    score_half(1, sharp_ref, me * PLANES + z, inbox, outbox, soft_out, members, results)
    send_lines(1)
    _, all_soft = spread_soft(1)

    def last(t, carry):
        home_pair(1, order(t), carry)
        return carry

    lax.fori_loop(0, 4, last, all_soft)
    back_relays[1][1]()

    for r in range(0, count, 256):
        column = as_column(where_ref[0:1, r:r + 256])
        lane = iota((256, 128), 1).astype(F32)
        for s in range(0, combined.shape[0], 128):
            spots[r:r + 256, s:s + 128] = jnp.where(column == lane + float(s), 1.0, 0.0).astype(BF16)
    await_back(0)
    for sem, ref, rows in [(z_send.at[0], rows_out, FRONT), (z_send.at[1], rows_out, CAP - FRONT)]:
        sent = ref.at[pl.ds(0, PLANES - 2), pl.ds(0, rows)]
        pltpu.make_async_copy(sent, sent, sem).wait()
    sent = slots_out.at[pl.ds(0, PLANES - 1)]
    pltpu.make_async_copy(sent, sent, slot_send).wait()
    pltpu.make_async_copy(sent, sent, name_send).wait()
    for h in range(2):
        for ref, sem in ((line_out, line_send), (outbox, back_line_send)):
            sent = blocks(ref, h, 0, 4 * (LINES - 1))
            pltpu.make_async_copy(sent, sent, sem.at[h]).wait()
        sent = soft_out.at[h, pl.ds(0, LINES - 1)]
        pltpu.make_async_copy(sent, sent, soft_send.at[h]).wait()
        sent = back_out.at[h, pl.ds(0, PLANES - 2)]
        pltpu.make_async_copy(sent, sent, back_send.at[h]).wait()
        relays[h][2]()
        back_relays[h][2]()
    await_back(1)
    came = names_in.at[pl.ds(0, PLANES - 1)]
    pltpu.make_async_copy(came, came, name_recv).wait()
    soft = jnp.concatenate([names_in[...].reshape(PLANES, 256), jnp.zeros((8, 256), F32)], axis=0).astype(BF16)
    for r in range(0, count, 256):
        neighbour[r:r + 256, :] = jnp.dot(
            spots[r:r + 256, :], combined[...], preferred_element_type=F32).astype(BF16)
        found = jnp.where(iota((256, 256), 0).astype(F32) == where_ref[1:2, r:r + 256], 1.0, 0.0).astype(BF16)
        found = jnp.dot(soft, found, preferred_element_type=F32)[:PLANES]
        chosen = jnp.where(iota((PLANES, 256), 0).astype(F32) == where_ref[2:3, r:r + 256], found, 0.0)
        soft_max[:, r:r + 256] = jnp.sum(chosen, axis=0, keepdims=True).astype(BF16)


def whole(sharp, ids, x):
    count, features = x.shape
    half = features // 2
    vmem = pl.BlockSpec(memory_space=pltpu.VMEM)
    lines = pltpu.VMEM((2, 4 * LINES * BLOCK, half), BF16)
    rows = pltpu.VMEM((PLANES, CAP, features), BF16)
    names = pltpu.VMEM((PLANES, 1, 256), F32)
    soft = pltpu.VMEM((2, LINES, 1, 128), F32)
    members = pltpu.VMEM((2, 512, features), BF16)
    back = pltpu.VMEM((2, PLANES, 2 * BACK, half), BF16)
    places = 2 * PLANES * BACK
    dma = pltpu.SemaphoreType.DMA
    return pl.pallas_call(
        whole_kernel,
        in_specs=[pl.BlockSpec(memory_space=pltpu.SMEM), vmem, vmem],
        out_specs=[vmem] * 3,
        out_shape=[
            jax.ShapeDtypeStruct((1, count), BF16),
            jax.ShapeDtypeStruct((count, features), BF16),
            jax.ShapeDtypeStruct((8, 128), F32),
        ],
        scratch_shapes=[
            pltpu.VMEM((8, count), F32), pltpu.VMEM((256, count), BF16), rows, rows,
            pltpu.VMEM((2, FRONT // 2, features), BF16), pltpu.VMEM((2, (CAP - FRONT) // 2, features), BF16),
            names, names, lines, lines, members, members, lines, lines, soft, soft, back, back,
            pltpu.VMEM((2, 2 * BACK, half), BF16), names, names,
            pltpu.VMEM((places, features), BF16), pltpu.VMEM((count, places), BF16),
            dma((2,)), dma((2, PLANES)), dma, dma((PLANES,)), dma((2, 4)), dma((2, 2)), dma((2,)), dma((2,)),
            dma((2, 4)), dma((2,)), dma((2,)), dma((2,)), dma((2, 4)), dma((2, 4)), dma((2,)), dma((2,)),
            dma, dma, dma((2, 4)), dma((2, 2)),
        ],
        compiler_params=pltpu.CompilerParams(
            collective_id=2, has_side_effects=True, vmem_limit_bytes=52 * 2**20),
        name="whole",
    )(sharp, ids, x)


def by_all_slots(n, embeddings, cluster_ids, sharp):
    clusters = sharp.shape[0]
    outbox, dest = pack(cluster_ids[None, :], embeddings, clusters * SRC_CAP)
    (arrived,) = exchange(n, 0, outbox)
    results, soft = settle(sharp, arrived, n, clusters // n, 1)
    returned, soft_returned = exchange(n, 1, results, soft)
    return unpack(dest, returned, soft_returned)


def body(n, embeddings, cluster_ids, sharpness):
    sharp = sharpness.astype(F32)
    soft_max, neighbour, flag = whole(sharp, cluster_ids[None, :], embeddings)
    soft_max, neighbour = lax.cond(
        flag[0, 0] > 0.5,
        lambda: tuple(by_all_slots(n, embeddings, cluster_ids, sharp)),
        lambda: (soft_max, neighbour),
    )
    return (soft_max[0], neighbour)


def solution(mesh):
    n = mesh.size
    return jax.shard_map(
        functools.partial(body, n),
        mesh=mesh,
        in_specs=(P(("group", "dev"), None), P(("group", "dev")), P()),
        out_specs=(P(("group", "dev")), P(("group", "dev"), None)),
        check_vma=False,
    )
```

```python
import functools

import jax
import jax.numpy as jnp
from jax import lax
from jax.experimental import pallas as pl
from jax.experimental.pallas import tpu as pltpu
from jax.sharding import PartitionSpec as P

MESH = pl.DeviceIdType.MESH
SRC_CAP = 2
EMPTY = 1024.0
NEGATIVE = -1e30
NT = (((1,), (1,)), ((), ()))
F32 = jnp.float32
BF16 = jnp.bfloat16


def iota(shape, dim):
    return lax.broadcasted_iota(jnp.int32, shape, dim)


def as_column(row, lanes=128):
    return jnp.transpose(jnp.broadcast_to(row, (lanes, row.shape[1])))


def pack_kernel(ids_ref, x_ref, out_ref, dest_ref, normed):
    step = pl.program_id(0)
    count, features = x_ref.shape
    half = features // 2
    slots = out_ref.shape[0] // 2

    @pl.when(step == 0)
    def _():
        ids = ids_ref[...]
        columns = as_column(ids.astype(F32))
        ordinal = jnp.zeros((1, count), F32)
        for r in range(0, count, 128):
            block = jnp.concatenate([columns[r:r + 128]] * (count // 128), axis=1)
            same = block == ids.astype(F32)
            before = iota((128, count), 0) + r < iota((128, count), 1)
            ordinal += jnp.sum(jnp.where(same & before, 1.0, 0.0), axis=0, keepdims=True)
        dest_ref[...] = ids * SRC_CAP + ordinal.astype(jnp.int32)
        for r in range(0, count, 256):
            wide = x_ref[r:r + 256, :].astype(F32)
            scale = lax.rsqrt(jnp.mean(wide * wide, axis=-1, keepdims=True) + 1e-06)
            normed[r:r + 256, :] = (wide * scale).astype(BF16)

    dest = dest_ref[...]
    hit = jnp.where(iota((slots, count), 0) + step * slots == dest, 1.0, 0.0)
    filled = jnp.sum(hit, axis=1, keepdims=True)
    rows = jnp.dot(hit.astype(BF16), normed[...], preferred_element_type=F32)
    first = jnp.where((iota((slots, 128), 1) == 0) & (filled < 0.5), EMPTY, rows[:, :128])
    left = jnp.concatenate([first, rows[:, 128:half]], axis=1).reshape(slots // 8, 1, 8, half)
    right = rows[:, half:].reshape(slots // 8, 1, 8, half)
    both = jnp.concatenate([left, right], axis=1).reshape(slots * 2, half)
    out_ref[...] = both.astype(BF16)


def pack(ids, x, slots_all):
    count, features = x.shape
    steps = 8
    slots = slots_all // steps
    return pl.pallas_call(
        pack_kernel,
        grid=(steps,),
        in_specs=[
            pl.BlockSpec((1, count), lambda i: (0, 0)),
            pl.BlockSpec((count, features), lambda i: (0, 0)),
        ],
        out_specs=[
            pl.BlockSpec((slots * 2, features // 2), lambda i: (i, 0)),
            pl.BlockSpec((1, count), lambda i: (0, 0)),
        ],
        out_shape=[
            jax.ShapeDtypeStruct((slots_all * 2, features // 2), BF16),
            jax.ShapeDtypeStruct((1, count), jnp.int32),
        ],
        scratch_shapes=[pltpu.VMEM((count, features), BF16)],
        compiler_params=pltpu.CompilerParams(vmem_limit_bytes=32 * 2**20),
        name="pack",
    )(ids, x)


def partner(k, g, d):
    q = (k * 101) % 256
    z = (d % 8 + q % 8) % 8
    x = (d // 8 + (q // 8) % 4) % 4
    y = (g // 2 + (q // 32) % 4) % 4
    core = (g % 2 + q // 128) % 2
    return y * 2 + core, x * 8 + z


def exchange_kernel(n, *refs):
    count = (len(refs) - 3) // 2
    sources, targets = refs[:count], refs[count:2 * count]
    send_sem, recv_sem, own_sem = refs[2 * count:]
    g, d = lax.axis_index("group"), lax.axis_index("dev")
    me = g * 32 + d

    def part(ref, start, blocks):
        size = ref.shape[0] // n
        return ref.at[pl.ds(pl.multiple_of(start * size, size), blocks * size)]

    barrier = pltpu.get_barrier_semaphore()

    def greet(k, carry):
        tg, td = partner(k, g, d)
        pl.semaphore_signal(barrier, inc=1, device_id=(tg, td), device_id_type=MESH)
        return carry

    lax.fori_loop(1, n, greet, 0)
    own = [
        pltpu.make_async_copy(part(s, me, 1), part(t, me, 1), own_sem.at[i])
        for i, (s, t) in enumerate(zip(sources, targets))
    ]
    for copy in own:
        copy.start()
    pl.semaphore_wait(barrier, n - 1)

    def send(k, carry):
        tg, td = partner(k, g, d)
        for i, (s, t) in enumerate(zip(sources, targets)):
            pltpu.make_async_remote_copy(
                src_ref=part(s, tg * 32 + td, 1),
                dst_ref=part(t, me, 1),
                send_sem=send_sem.at[i],
                recv_sem=recv_sem.at[i],
                device_id=(tg, td),
                device_id_type=MESH,
            ).start()
        return carry

    lax.fori_loop(1, n, send, 0)
    for i, (s, t) in enumerate(zip(sources, targets)):
        pltpu.make_async_copy(part(s, 0, n - 1), part(s, 0, n - 1), send_sem.at[i]).wait()
        pltpu.make_async_copy(part(t, 0, n - 1), part(t, 0, n - 1), recv_sem.at[i]).wait()
    for copy in own:
        copy.wait()


def exchange(n, collective_id, *arrays):
    return pl.pallas_call(
        functools.partial(exchange_kernel, n),
        in_specs=[pl.BlockSpec(memory_space=pl.ANY)] * len(arrays),
        out_specs=[pl.BlockSpec(memory_space=pl.ANY)] * len(arrays),
        out_shape=[jax.ShapeDtypeStruct(a.shape, a.dtype) for a in arrays],
        scratch_shapes=[pltpu.SemaphoreType.DMA((len(arrays),))] * 3,
        compiler_params=pltpu.CompilerParams(collective_id=collective_id, has_side_effects=True),
        name="exchange",
    )(*arrays)


def settle_kernel(per_line, sharp_ref, in_ref, out_ref, soft_ref, members, results):
    me = lax.axis_index("group") * 32 + lax.axis_index("dev")
    owned, span, features = members.shape
    half = features // 2
    chunk = 16

    def source_row(o):
        return (o % 32) // 2 * 16 + o // 128 * 8 + (o % 128) // 32 * 2 + o % 2

    inward = jnp.where(source_row(iota((256, 256), 0)) == iota((256, 256), 1), 1.0, 0.0).astype(BF16)
    outward = jnp.where(source_row(iota((256, 256), 1)) == iota((256, 256), 0), 1.0, 0.0).astype(BF16)

    def gather(b, carry):
        arrived = in_ref[pl.ds(pl.multiple_of(b * 256, 256), 256), :]
        placed = jnp.dot(inward, arrived, preferred_element_type=F32).astype(BF16)
        rows = pl.ds(pl.multiple_of(b * 32, 32), 32)
        for c in range(owned):
            members[c, rows, :half] = placed[c * 32:(c + 1) * 32]
            members[c, rows, half:] = placed[128 + c * 32:128 + (c + 1) * 32]
        return carry

    lax.fori_loop(0, span // 32, gather, 0, unroll=4)

    off_diagonal = iota((span, span), 0) != iota((span, span), 1)
    first = jnp.where(iota((16, 128), 1) == 0, 1.0, 0.0).astype(BF16)
    source = iota((span, 128), 0) // 2
    lane = iota((span, 128), 1) - source % per_line * 8 - iota((span, 128), 0) % 2
    soft = jnp.zeros((span, 128), F32)
    for c in range(owned):
        sharp = sharp_ref[me * owned + c]
        rows = members[c]
        marks = lax.dot_general(first, rows[:, :128], NT, preferred_element_type=F32)[:1]
        dots = lax.dot_general(rows, rows, NT, preferred_element_type=F32)
        masked = jnp.where(off_diagonal & (marks < EMPTY / 2), dots * (sharp * (1.0 / features)), NEGATIVE)
        highest = jnp.maximum(jnp.max(masked, axis=1, keepdims=True), 0.0)
        weights = jnp.exp(masked - highest)
        total = jnp.exp(-highest) + jnp.sum(weights, axis=1, keepdims=True)
        soft = jnp.where(lane == 2 * c, (highest + jnp.log(total)) / sharp, soft)
        summed = jnp.dot(weights.astype(BF16), rows, preferred_element_type=F32)
        results[c] = (summed * (1.0 / total)).astype(BF16)

    lines = soft_ref.shape[0]
    pick = jnp.where(iota((lines, span), 1) // (2 * per_line) == iota((lines, span), 0), 1.0, 0.0).astype(BF16)
    spread = jnp.dot(pick, soft.astype(BF16), preferred_element_type=F32)
    soft_ref[...] = spread.reshape(soft_ref.shape)

    def scatter(b, carry):
        rows = pl.ds(pl.multiple_of(b * 32, 32), 32)
        placed = jnp.concatenate(
            [results[c, rows, :half] for c in range(owned)] + [results[c, rows, half:] for c in range(owned)],
            axis=0,
        )
        back = jnp.dot(outward, placed, preferred_element_type=F32)
        out_ref[pl.ds(pl.multiple_of(b * 256, 256), 256), :] = back.astype(BF16)
        return carry

    lax.fori_loop(0, span // 32, scatter, 0, unroll=4)


def settle(sharp, arrived, n, owned, per_line):
    rows, half = arrived.shape
    span = n * SRC_CAP
    return pl.pallas_call(
        functools.partial(settle_kernel, per_line),
        in_specs=[pl.BlockSpec(memory_space=pltpu.SMEM), pl.BlockSpec(memory_space=pltpu.VMEM)],
        out_specs=[pl.BlockSpec(memory_space=pltpu.VMEM)] * 2,
        out_shape=[
            jax.ShapeDtypeStruct((rows, half), BF16),
            jax.ShapeDtypeStruct((n // per_line, 1, 128), F32),
        ],
        scratch_shapes=[
            pltpu.VMEM((owned, span, half * 2), BF16),
            pltpu.VMEM((owned, span, half * 2), BF16),
        ],
        compiler_params=pltpu.CompilerParams(vmem_limit_bytes=40 * 2**20),
        name="settle",
    )(sharp, arrived)


def unpack_kernel(dest_ref, in_ref, soft_in_ref, soft_ref, out_ref, combined, soft_all):
    step = pl.program_id(0)
    slots, features = combined.shape
    half = features // 2
    n = soft_in_ref.shape[0]
    rows = out_ref.shape[0]

    @pl.when(step == 0)
    def _():
        def split(b, carry):
            block = in_ref[pl.ds(pl.multiple_of(b * 512, 512), 512), :].astype(F32).reshape(32, 2, 8, half)
            place = pl.ds(pl.multiple_of(b * 256, 256), 256)
            combined[place, :half] = block[:, 0].reshape(256, half).astype(BF16)
            combined[place, half:] = block[:, 1].reshape(256, half).astype(BF16)
            return carry

        lax.fori_loop(0, slots // 256, split, 0)
        soft_all[...] = jnp.transpose(soft_in_ref[...].reshape(n, 128)).astype(BF16)

    dest = dest_ref[...]
    column = as_column(dest.astype(F32))
    lane = iota((rows, 128), 1).astype(F32)
    hit = jnp.concatenate(
        [jnp.where(column == lane + float(s), 1.0, 0.0).astype(BF16) for s in range(0, slots, 128)], axis=1
    )
    out_ref[...] = jnp.dot(hit, combined[...], preferred_element_type=F32).astype(BF16)

    owner = jnp.where(iota((n, rows), 0) == dest // 8, 1.0, 0.0).astype(BF16)
    found = jnp.dot(soft_all[...], owner, preferred_element_type=F32)[:8]
    chosen = jnp.where(iota((8, rows), 0) == dest % 8, found, 0.0)
    soft_ref[...] = jnp.sum(chosen, axis=0, keepdims=True).astype(BF16)


def unpack(dest, returned, soft_returned):
    count = dest.shape[1]
    n = soft_returned.shape[0]
    blocks, half = returned.shape
    slots, features = blocks // 2, half * 2
    rows = 256
    return pl.pallas_call(
        unpack_kernel,
        grid=(count // rows,),
        in_specs=[
            pl.BlockSpec((1, rows), lambda i: (0, i)),
            pl.BlockSpec((blocks, half), lambda i: (0, 0)),
            pl.BlockSpec((n, 1, 128), lambda i: (0, 0, 0)),
        ],
        out_specs=[
            pl.BlockSpec((1, rows), lambda i: (0, i)),
            pl.BlockSpec((rows, features), lambda i: (i, 0)),
        ],
        out_shape=[
            jax.ShapeDtypeStruct((1, count), BF16),
            jax.ShapeDtypeStruct((count, features), BF16),
        ],
        scratch_shapes=[pltpu.VMEM((slots, features), BF16), pltpu.VMEM((128, n), BF16)],
        compiler_params=pltpu.CompilerParams(vmem_limit_bytes=40 * 2**20),
        name="unpack",
    )(dest, returned, soft_returned)


PLANES = 8
LINES = 32
CAP = 160
BLOCK = 16


def blocks(ref, start, count):
    return ref.at[pl.ds(pl.multiple_of(start * BLOCK, BLOCK), count * BLOCK)]


def near_first(k):
    near = k // 2 + 1
    return near + (k % 2) * (PLANES - 2 * near)


def far_first(k):
    near = 4 - (k + 1) // 2
    return near + ((k + 1) % 2) * (PLANES - 2 * near)


def place():
    g, d = lax.axis_index("group"), lax.axis_index("dev")
    return g, d // PLANES, d % PLANES


def other_lines(g, x):
    ys = [(g // 2 + i) % 4 for i in range(4)]
    cores = [(g % 2 + i) % 2 for i in range(2)]
    xs = [(x + i) % 4 for i in range(4)]
    mixed = [(j * 11) % LINES for j in range(1, LINES)]
    return [(ys[q // 2 % 4] * 2 + cores[q % 2], xs[q // 8]) for q in mixed]


def greet_all(g, x, z):
    barrier = pltpu.get_barrier_semaphore()

    def greet_z(k, carry):
        there = (g, x * PLANES + (z + k) % PLANES)
        pl.semaphore_signal(barrier, inc=1, device_id=there, device_id_type=MESH)
        return carry

    lax.fori_loop(1, PLANES, greet_z, 0)
    for tg, tx in other_lines(g, x):
        pl.semaphore_signal(barrier, inc=1, device_id=(tg, tx * PLANES + z), device_id_type=MESH)
    return barrier


def relay_copies(rows_out, relay_in, rows_in, send_sems, recv_sems, g, x, z, source_at):
    def first_leg():
        copies = []
        for way, hop in enumerate((2, PLANES - 2)):
            half = pl.ds(way * (CAP // 2), CAP // 2)
            copies.append(pltpu.make_async_remote_copy(
                src_ref=rows_out.at[(z + 4) % PLANES, half], dst_ref=relay_in.at[way],
                send_sem=send_sems.at[way], recv_sem=recv_sems.at[way],
                device_id=(g, x * PLANES + (z + hop) % PLANES), device_id_type=MESH))
        return copies

    def second_leg():
        copies = []
        for way, hop in enumerate((2, PLANES - 2)):
            half = pl.ds(way * (CAP // 2), CAP // 2)
            source = (z + PLANES - hop) % PLANES
            copies.append(pltpu.make_async_remote_copy(
                src_ref=relay_in.at[way], dst_ref=rows_in.at[source, half],
                send_sem=send_sems.at[2 + way], recv_sem=source_at(source),
                device_id=(g, x * PLANES + (z + hop) % PLANES), device_id_type=MESH))
        return copies

    def pass_on():
        for way, copy in enumerate(second_leg()):
            came = relay_in.at[way]
            pltpu.make_async_copy(came, came, recv_sems.at[way]).wait()
            copy.start()

    def finish():
        for copy in first_leg() + second_leg():
            copy.wait_send()

    return first_leg, pass_on, finish


def collect_kernel(ids_ref, x_any, x_sem, x_ref, inbox, where_ref, slots_in, hits, rows_out, rows_in, relay_in, slots_out, line_out,
                   z_send, z_recv, relay_send, relay_recv, line_send, line_recv, own_sem):
    g, x, z = place()
    lines = other_lines(g, x)
    count, features = x_ref.shape
    half = features // 2
    x_copy = pltpu.make_async_copy(x_any, x_ref, x_sem)
    x_copy.start()
    barrier = greet_all(g, x, z)

    ids = ids_ref[...]
    columns = as_column(ids.astype(F32)).astype(jnp.int32)
    plane = jnp.right_shift(ids, 2) & (PLANES - 1)
    plane_columns = jnp.right_shift(columns, 2) & (PLANES - 1)
    before = iota((128, 128), 0) < iota((128, 128), 1)
    ordinal, position = [], []
    for t in range(0, count, 128):
        same = jnp.zeros((128, 128), F32)
        beside = jnp.zeros((128, 128), F32)
        for r in range(0, t + 128, 128):
            alike = columns[r:r + 128] == ids[:, t:t + 128]
            near = plane_columns[r:r + 128] == plane[:, t:t + 128]
            if r == t:
                alike, near = alike & before, near & before
            same += jnp.where(alike, 1.0, 0.0)
            beside += jnp.where(near, 1.0, 0.0)
        ordinal.append(jnp.sum(same, axis=0, keepdims=True))
        position.append(jnp.sum(beside, axis=0, keepdims=True))
    ordinal, position = jnp.concatenate(ordinal, axis=1), jnp.concatenate(position, axis=1)
    where_ref[...] = jnp.concatenate([plane.astype(F32), position, jnp.zeros((6, count), F32)], axis=0)
    flag = jnp.where(jnp.max(position) > CAP - 0.5, 1.0, 0.0)
    slot = (jnp.right_shift(ids, 5) * 8 + (ids & 3) * SRC_CAP).astype(F32) + ordinal + 1.0
    slot = jnp.broadcast_to(slot, (16, count)).astype(BF16)
    hits[CAP:, :] = jnp.zeros((256 - CAP, count), BF16)
    key = jnp.where(position < CAP - 0.5, position.astype(jnp.int32) * PLANES + plane, -1)

    def compact(there):
        hits[:CAP, :] = jnp.where(iota((CAP, count), 0) * PLANES + there == key, 1.0, 0.0).astype(BF16)
        rows = jnp.dot(hits[:CAP, :], x_ref[...], preferred_element_type=F32).astype(BF16)
        names = lax.dot_general(slot, hits[...], NT, preferred_element_type=F32)[:1]
        return rows, jnp.where(iota((1, 256), 1) == 255, flag, names)

    def z_copy(out, into, i, there):
        return pltpu.make_async_remote_copy(
            src_ref=out.at[there], dst_ref=into.at[z], send_sem=z_send.at[i], recv_sem=z_recv.at[i, z],
            device_id=(g, x * PLANES + there), device_id_type=MESH)

    first_leg, pass_on, finish_relay = relay_copies(
        rows_out, relay_in, rows_in, relay_send, relay_recv, g, x, z, lambda source: z_recv.at[0, source])

    def prepare(there):
        rows, names = compact(there)
        rows_out[there] = rows
        slots_out[there] = names

    def send_z(k, carry):
        there = (z + near_first(k)) % PLANES
        prepare(there)
        z_copy(rows_out, rows_in, 0, there).start()
        z_copy(slots_out, slots_in, 1, there).start()
        return carry

    opposite = (z + 4) % PLANES
    x_copy.wait()
    pl.semaphore_wait(barrier, PLANES + LINES - 2)
    prepare(opposite)
    for copy in first_leg():
        copy.start()
    z_copy(slots_out, slots_in, 1, opposite).start()
    lax.fori_loop(0, PLANES - 2, send_z, 0)
    rows, names = compact(z)
    rows_in[z] = rows
    slots_in[z] = names

    def own_copy(source):
        return pltpu.make_async_copy(
            blocks(line_out, source * LINES + g * 4 + x, 1), blocks(inbox, (g * 4 + x) * PLANES + source, 1),
            own_sem.at[source])

    def forward(source):
        wide = rows_in[source].astype(F32)
        scale = lax.rsqrt(jnp.mean(wide * wide, axis=-1, keepdims=True) + 1e-06)
        names = slots_in[source][:, :CAP].astype(jnp.int32) - 1
        hit = jnp.where(iota((256, CAP), 0) == names, 1.0, 0.0)
        filled = jnp.sum(hit, axis=1, keepdims=True)
        rows = jnp.dot(hit.astype(BF16), (wide * scale).astype(BF16), preferred_element_type=F32)
        first = jnp.where((iota((256, 128), 1) == 0) & (filled < 0.5), EMPTY, rows[:, :128])
        left = jnp.concatenate([first, rows[:, 128:half]], axis=1).reshape(LINES, 1, 8, half)
        right = rows[:, half:].reshape(LINES, 1, 8, half)
        both = jnp.concatenate([left, right], axis=1).reshape(512, half)
        line_out[pl.ds(pl.multiple_of(source * 512, 512), 512), :] = both.astype(BF16)
        own_copy(source).start()

        for tg, tx in lines:
            pltpu.make_async_remote_copy(
                src_ref=blocks(line_out, source * LINES + tg * 4 + tx, 1),
                dst_ref=blocks(inbox, (g * 4 + x) * PLANES + source, 1),
                send_sem=line_send, recv_sem=line_recv,
                device_id=(tg, tx * PLANES + z), device_id_type=MESH).start()

    forward(z)
    pass_on()

    def arrive(k, carry):
        source = (z + PLANES - near_first(k)) % PLANES
        pltpu.make_async_copy(rows_in.at[source], rows_in.at[source], z_recv.at[0, source]).wait()
        pltpu.make_async_copy(slots_in.at[source], slots_in.at[source], z_recv.at[1, source]).wait()
        forward(source)
        return carry

    lax.fori_loop(0, PLANES - 1, arrive, 0)
    others = PLANES * (LINES - 1)
    sent = rows_out.at[pl.ds(0, PLANES - 2)]
    pltpu.make_async_copy(sent, sent, z_send.at[0]).wait()
    sent = slots_out.at[pl.ds(0, PLANES - 1)]
    pltpu.make_async_copy(sent, sent, z_send.at[1]).wait()
    finish_relay()
    pltpu.make_async_copy(blocks(line_out, 0, others), blocks(line_out, 0, others), line_send).wait()
    pltpu.make_async_copy(blocks(inbox, 0, others), blocks(inbox, 0, others), line_recv).wait()

    def finish(source, carry):
        own_copy(source).wait()
        return carry

    lax.fori_loop(0, PLANES, finish, 0)


def restore_kernel(results, soft_ref, slots_ref, rows_back, soft_back, flag_ref, line_in, soft_out, soft_in, rows_out,
                   relay_in, names_out, z_send, z_recv, relay_send, relay_recv, line_send, line_recv, soft_sem, own_sem, meanwhile):
    g, x, z = place()
    lines = other_lines(g, x)
    me = g * 4 + x
    half = results.shape[1]
    flag = jnp.max(jnp.where(iota((PLANES, 1, 256), 2) == 255, slots_ref[...], 0.0))
    soft_out[...] = jnp.where(iota(soft_out.shape, 2) < 64, soft_ref[...], flag)
    soft_in[me] = soft_out[me]

    for tg, tx in lines:
        pltpu.make_async_remote_copy(
            src_ref=soft_out.at[tg * 4 + tx], dst_ref=soft_in.at[me], send_sem=soft_sem.at[0],
            recv_sem=soft_sem.at[1], device_id=(tg, tx * PLANES + z), device_id_type=MESH).start()

    def own_copy(home):
        return pltpu.make_async_copy(
            blocks(results, me * PLANES + home, 1), blocks(line_in, home * LINES + me, 1), own_sem.at[home])

    def home_of(k):
        return (z + far_first(k)) % PLANES

    def send_line(k, carry):
        home = home_of(k)
        own_copy(home).start()

        for tg, tx in lines:
            pltpu.make_async_remote_copy(
                src_ref=blocks(results, (tg * 4 + tx) * PLANES + home, 1),
                dst_ref=blocks(line_in, home * LINES + me, 1),
                send_sem=line_send, recv_sem=line_recv.at[home],
                device_id=(tg, tx * PLANES + z), device_id_type=MESH).start()
        return carry

    lax.fori_loop(0, 3, send_line, 0)
    first = soft_in.at[pl.ds(0, LINES - 1)]
    pltpu.make_async_copy(first, first, soft_sem.at[1]).wait()
    all_soft = soft_in[...].reshape(LINES, 128)
    flag_ref[...] = jnp.broadcast_to(jnp.max(all_soft[:, 64:], axis=(0, 1), keepdims=True), flag_ref.shape)
    spread = jnp.where(iota((256, LINES), 0) // 8 == iota((256, LINES), 1), 1.0, 0.0).astype(BF16)
    all_soft = jnp.dot(spread, all_soft.astype(BF16), preferred_element_type=F32)

    def settle_home(home):
        arrived = blocks(line_in, home * LINES, LINES - 1)
        pltpu.make_async_copy(arrived, arrived, line_recv.at[home]).wait()
        own_copy(home).wait()
        both = line_in[pl.ds(pl.multiple_of(home * 512, 512), 512), :].astype(F32).reshape(LINES, 2, 8, half)
        left, right = both[:, 0].reshape(256, half).astype(BF16), both[:, 1].reshape(256, half).astype(BF16)
        names = slots_ref[home]
        column = as_column(names)[:CAP] - 1.0
        lane = iota((CAP, 128), 1).astype(F32)
        hit = jnp.concatenate(
            [jnp.where(column == lane + float(s), 1.0, 0.0).astype(BF16) for s in (0, 128)], axis=1)
        mine = jnp.where(iota((256, 128), 1) == home * 8 + iota((256, 128), 0) % 8, all_soft, 0.0).astype(BF16)
        values = lax.dot_general(jnp.ones((16, 128), BF16), mine, NT, preferred_element_type=F32)
        picked = jnp.where(iota((256, 256), 0) == names.astype(jnp.int32) - 1, 1.0, 0.0).astype(BF16)
        picked = jnp.dot(values.astype(BF16), picked, preferred_element_type=F32)[:1]
        left = jnp.dot(hit, left, preferred_element_type=F32).astype(BF16)
        right = jnp.dot(hit, right, preferred_element_type=F32).astype(BF16)
        return left, right, picked

    first_leg, pass_on, finish_relay = relay_copies(
        rows_out, relay_in, rows_back, relay_send, relay_recv, g, x, z, lambda source: z_recv.at[0])

    def z_copy(out, into, i, home):
        return pltpu.make_async_remote_copy(
            src_ref=out.at[home], dst_ref=into.at[z], send_sem=z_send.at[i], recv_sem=z_recv.at[i],
            device_id=(g, x * PLANES + home), device_id_type=MESH)

    def send_z(k, carry):
        home = home_of(k)
        left, right, picked = settle_home(home)
        rows_out[home, :, :half] = left
        rows_out[home, :, half:] = right
        names_out[home] = picked
        z_copy(names_out, soft_back, 1, home).start()

        @pl.when(k == 0)
        def _():
            for copy in first_leg():
                copy.start()

        @pl.when(k > 0)
        def _():
            z_copy(rows_out, rows_back, 0, home).start()

        @pl.when(k == 2)
        def _():
            pass_on()

        @pl.when(k < PLANES - 3)
        def _():
            send_line(k + 3, 0)

        return carry

    lax.fori_loop(0, PLANES - 1, send_z, 0)
    left, right, picked = settle_home(z)
    rows_back[z, :, :half] = left
    rows_back[z, :, half:] = right
    soft_back[z] = picked

    meanwhile()
    others = PLANES * (LINES - 1)
    sent = soft_out.at[pl.ds(0, LINES - 1)]
    pltpu.make_async_copy(sent, sent, soft_sem.at[0]).wait()
    pltpu.make_async_copy(blocks(results, 0, others), blocks(results, 0, others), line_send).wait()
    sent = rows_out.at[pl.ds(0, PLANES - 2)]
    pltpu.make_async_copy(sent, sent, z_send.at[0]).wait()
    sent = names_out.at[pl.ds(0, PLANES - 1)]
    pltpu.make_async_copy(sent, sent, z_send.at[1]).wait()
    finish_relay()
    for i, into in enumerate((rows_back, soft_back)):
        came = into.at[pl.ds(0, PLANES - 1)]
        pltpu.make_async_copy(came, came, z_recv.at[i]).wait()


def find_spots(where_ref, spots):
    for r in range(0, spots.shape[0], 256):
        plane, position = where_ref[0:1, r:r + 256], where_ref[1:2, r:r + 256]
        column = as_column(plane * CAP + position)
        lane = iota((256, 128), 1).astype(F32)
        for t in range(0, spots.shape[1], 128):
            spots[r:r + 256, t:t + 128] = jnp.where(column == lane + float(t), 1.0, 0.0).astype(BF16)


def place_kernel(spots, where_ref, in_ref, soft_in_ref, soft_ref, out_ref):
    rows = out_ref.shape[0]
    plane, position = where_ref[0:1, :], where_ref[1:2, :]
    combined = in_ref[...].reshape(PLANES * CAP, in_ref.shape[2])
    out_ref[...] = jnp.dot(spots[...], combined, preferred_element_type=F32).astype(BF16)

    spot = jnp.where(iota((256, rows), 0).astype(F32) == position, 1.0, 0.0).astype(BF16)
    soft = soft_in_ref[...].reshape(PLANES, 256)
    soft = jnp.concatenate([soft, jnp.zeros((8, 256), F32)], axis=0).astype(BF16)
    found = jnp.dot(soft, spot, preferred_element_type=F32)[:PLANES]
    chosen = jnp.where(iota((PLANES, rows), 0).astype(F32) == plane, found, 0.0)
    soft_ref[...] = jnp.sum(chosen, axis=0, keepdims=True).astype(BF16)


def whole_kernel(sharp_ref, ids_ref, x_any, soft_max, neighbour, flag_ref, inbox, where_ref, slots_in, hits,
                 rows_out, rows_in, relay_in, slots_out, line_out, members, results, soft, line_in, soft_out, soft_in,
                 back_out, back_in, relay_back, names_out, names_in, z_send, z_recv, relay_send, relay_recv, line_send,
                 line_recv, own_sem, z_send_b, z_recv_b, relay_send_b, relay_recv_b, line_send_b, line_recv_b, soft_sem,
                 own_sem_b, x_ref, x_sem, spots):
    collect_kernel(ids_ref, x_any, x_sem, x_ref, inbox, where_ref, slots_in, hits, rows_out, rows_in, relay_in, slots_out, line_out,
                   z_send, z_recv, relay_send, relay_recv, line_send, line_recv, own_sem)
    settle_kernel(PLANES, sharp_ref, inbox, line_out, soft, members, results)
    restore_kernel(line_out, soft, slots_in, back_in, names_in, flag_ref, line_in, soft_out, soft_in, back_out,
                   relay_back, names_out, z_send_b, z_recv_b, relay_send_b, relay_recv_b, line_send_b, line_recv_b,
                   soft_sem, own_sem_b, lambda: find_spots(where_ref, spots))
    for r in range(0, neighbour.shape[0], 256):
        rows = pl.ds(r, 256)
        place_kernel(spots.at[rows], where_ref.at[:, rows], back_in, names_in, soft_max.at[:, rows], neighbour.at[rows])


def whole(sharp, ids, x):
    count, features = x.shape
    half = features // 2
    slots = PLANES * LINES * BLOCK
    vmem = pl.BlockSpec(memory_space=pltpu.VMEM)
    lines = pltpu.VMEM((slots, half), BF16)
    rows = pltpu.VMEM((PLANES, CAP, features), BF16)
    halves = pltpu.VMEM((2, CAP // 2, features), BF16)
    names = pltpu.VMEM((PLANES, 1, 256), F32)
    soft = pltpu.VMEM((LINES, 1, 128), F32)
    members = pltpu.VMEM((4, slots // 8, features), BF16)
    dma = pltpu.SemaphoreType.DMA
    return pl.pallas_call(
        whole_kernel,
        in_specs=[pl.BlockSpec(memory_space=pltpu.SMEM), vmem, pl.BlockSpec(memory_space=pl.ANY)],
        out_specs=[vmem] * 3,
        out_shape=[
            jax.ShapeDtypeStruct((1, count), BF16),
            jax.ShapeDtypeStruct((count, features), BF16),
            jax.ShapeDtypeStruct((8, 128), F32),
        ],
        scratch_shapes=[
            lines, pltpu.VMEM((8, count), F32), names, pltpu.VMEM((256, count), BF16),
            rows, rows, halves, names, lines, members, members, soft, lines, soft, soft,
            rows, rows, halves, names, names,
            dma((2,)), dma((2, PLANES)), dma((4,)), dma((2,)), dma, dma, dma((PLANES,)),
            dma((2,)), dma((2,)), dma((4,)), dma((2,)), dma, dma((PLANES,)), dma((2,)), dma((PLANES,)),
            pltpu.VMEM((count, features), BF16), dma, pltpu.VMEM((count, PLANES * CAP), BF16),
        ],
        compiler_params=pltpu.CompilerParams(
            collective_id=2, has_side_effects=True, vmem_limit_bytes=48 * 2**20),
        name="whole",
    )(sharp, ids, x)


def by_all_slots(n, embeddings, cluster_ids, sharp):
    clusters = sharp.shape[0]
    outbox, dest = pack(cluster_ids[None, :], embeddings, clusters * SRC_CAP)
    (arrived,) = exchange(n, 0, outbox)
    results, soft = settle(sharp, arrived, n, clusters // n, 1)
    returned, soft_returned = exchange(n, 1, results, soft)
    return unpack(dest, returned, soft_returned)


def body(n, embeddings, cluster_ids, sharpness):
    sharp = sharpness.astype(F32)
    soft_max, neighbour, flag = whole(sharp, cluster_ids[None, :], embeddings)
    soft_max, neighbour = lax.cond(
        flag[0, 0] > 0.5,
        lambda: tuple(by_all_slots(n, embeddings, cluster_ids, sharp)),
        lambda: (soft_max, neighbour),
    )
    return (soft_max[0], neighbour)


def solution(mesh):
    n = mesh.size
    return jax.shard_map(
        functools.partial(body, n),
        mesh=mesh,
        in_specs=(P(("group", "dev"), None), P(("group", "dev")), P()),
        out_specs=(P(("group", "dev")), P(("group", "dev"), None)),
        check_vma=False,
    )
```

```python
import functools

import jax
import jax.numpy as jnp
from jax import lax
from jax.experimental import pallas as pl
from jax.experimental.pallas import tpu as pltpu
from jax.sharding import PartitionSpec as P

MESH = pl.DeviceIdType.MESH
SRC_CAP = 2
EMPTY = 1024.0
NEGATIVE = -1e30
NT = (((1,), (1,)), ((), ()))
F32 = jnp.float32
BF16 = jnp.bfloat16


def iota(shape, dim):
    return lax.broadcasted_iota(jnp.int32, shape, dim)


def as_column(row, lanes=128):
    return jnp.transpose(jnp.broadcast_to(row, (lanes, row.shape[1])))


def pack_kernel(ids_ref, x_ref, out_ref, dest_ref, normed):
    step = pl.program_id(0)
    count, features = x_ref.shape
    half = features // 2
    slots = out_ref.shape[0] // 2

    @pl.when(step == 0)
    def _():
        ids = ids_ref[...]
        columns = as_column(ids.astype(F32))
        ordinal = jnp.zeros((1, count), F32)
        for r in range(0, count, 128):
            block = jnp.concatenate([columns[r:r + 128]] * (count // 128), axis=1)
            same = block == ids.astype(F32)
            before = iota((128, count), 0) + r < iota((128, count), 1)
            ordinal += jnp.sum(jnp.where(same & before, 1.0, 0.0), axis=0, keepdims=True)
        dest_ref[...] = ids * SRC_CAP + ordinal.astype(jnp.int32)
        for r in range(0, count, 256):
            wide = x_ref[r:r + 256, :].astype(F32)
            scale = lax.rsqrt(jnp.mean(wide * wide, axis=-1, keepdims=True) + 1e-06)
            normed[r:r + 256, :] = (wide * scale).astype(BF16)

    dest = dest_ref[...]
    hit = jnp.where(iota((slots, count), 0) + step * slots == dest, 1.0, 0.0)
    filled = jnp.sum(hit, axis=1, keepdims=True)
    rows = jnp.dot(hit.astype(BF16), normed[...], preferred_element_type=F32)
    first = jnp.where((iota((slots, 128), 1) == 0) & (filled < 0.5), EMPTY, rows[:, :128])
    left = jnp.concatenate([first, rows[:, 128:half]], axis=1).reshape(slots // 8, 1, 8, half)
    right = rows[:, half:].reshape(slots // 8, 1, 8, half)
    both = jnp.concatenate([left, right], axis=1).reshape(slots * 2, half)
    out_ref[...] = both.astype(BF16)


def pack(ids, x, slots_all):
    count, features = x.shape
    steps = 8
    slots = slots_all // steps
    return pl.pallas_call(
        pack_kernel,
        grid=(steps,),
        in_specs=[
            pl.BlockSpec((1, count), lambda i: (0, 0)),
            pl.BlockSpec((count, features), lambda i: (0, 0)),
        ],
        out_specs=[
            pl.BlockSpec((slots * 2, features // 2), lambda i: (i, 0)),
            pl.BlockSpec((1, count), lambda i: (0, 0)),
        ],
        out_shape=[
            jax.ShapeDtypeStruct((slots_all * 2, features // 2), BF16),
            jax.ShapeDtypeStruct((1, count), jnp.int32),
        ],
        scratch_shapes=[pltpu.VMEM((count, features), BF16)],
        compiler_params=pltpu.CompilerParams(vmem_limit_bytes=32 * 2**20),
        name="pack",
    )(ids, x)


def partner(k, g, d):
    q = (k * 101) % 256
    z = (d % 8 + q % 8) % 8
    x = (d // 8 + (q // 8) % 4) % 4
    y = (g // 2 + (q // 32) % 4) % 4
    core = (g % 2 + q // 128) % 2
    return y * 2 + core, x * 8 + z


def exchange_kernel(n, *refs):
    count = (len(refs) - 3) // 2
    sources, targets = refs[:count], refs[count:2 * count]
    send_sem, recv_sem, own_sem = refs[2 * count:]
    g, d = lax.axis_index("group"), lax.axis_index("dev")
    me = g * 32 + d

    def part(ref, start, blocks):
        size = ref.shape[0] // n
        return ref.at[pl.ds(pl.multiple_of(start * size, size), blocks * size)]

    barrier = pltpu.get_barrier_semaphore()

    def greet(k, carry):
        tg, td = partner(k, g, d)
        pl.semaphore_signal(barrier, inc=1, device_id=(tg, td), device_id_type=MESH)
        return carry

    lax.fori_loop(1, n, greet, 0)
    own = [
        pltpu.make_async_copy(part(s, me, 1), part(t, me, 1), own_sem.at[i])
        for i, (s, t) in enumerate(zip(sources, targets))
    ]
    for copy in own:
        copy.start()
    pl.semaphore_wait(barrier, n - 1)

    def send(k, carry):
        tg, td = partner(k, g, d)
        for i, (s, t) in enumerate(zip(sources, targets)):
            pltpu.make_async_remote_copy(
                src_ref=part(s, tg * 32 + td, 1),
                dst_ref=part(t, me, 1),
                send_sem=send_sem.at[i],
                recv_sem=recv_sem.at[i],
                device_id=(tg, td),
                device_id_type=MESH,
            ).start()
        return carry

    lax.fori_loop(1, n, send, 0)
    for i, (s, t) in enumerate(zip(sources, targets)):
        pltpu.make_async_copy(part(s, 0, n - 1), part(s, 0, n - 1), send_sem.at[i]).wait()
        pltpu.make_async_copy(part(t, 0, n - 1), part(t, 0, n - 1), recv_sem.at[i]).wait()
    for copy in own:
        copy.wait()


def exchange(n, collective_id, *arrays):
    return pl.pallas_call(
        functools.partial(exchange_kernel, n),
        in_specs=[pl.BlockSpec(memory_space=pl.ANY)] * len(arrays),
        out_specs=[pl.BlockSpec(memory_space=pl.ANY)] * len(arrays),
        out_shape=[jax.ShapeDtypeStruct(a.shape, a.dtype) for a in arrays],
        scratch_shapes=[pltpu.SemaphoreType.DMA((len(arrays),))] * 3,
        compiler_params=pltpu.CompilerParams(collective_id=collective_id, has_side_effects=True),
        name="exchange",
    )(*arrays)


def settle_parts(sharp_ref, in_ref, out_ref, soft_ref, members, results):
    me = lax.axis_index("group") * 32 + lax.axis_index("dev")
    owned, span, features = members.shape
    half = features // 2
    chunk = 16

    def source_row(o):
        return (o % 32) // 2 * 16 + o // 128 * 8 + (o % 128) // 32 * 2 + o % 2

    inward = jnp.where(source_row(iota((256, 256), 0)) == iota((256, 256), 1), 1.0, 0.0).astype(BF16)
    outward = jnp.where(source_row(iota((256, 256), 1)) == iota((256, 256), 0), 1.0, 0.0).astype(BF16)

    def gather(b, carry):
        arrived = in_ref[pl.ds(pl.multiple_of(b * 256, 256), 256), :]
        placed = jnp.dot(inward, arrived, preferred_element_type=F32).astype(BF16)
        rows = pl.ds(pl.multiple_of(b * 32, 32), 32)
        for c in range(owned):
            members[c, rows, :half] = placed[c * 32:(c + 1) * 32]
            members[c, rows, half:] = placed[128 + c * 32:128 + (c + 1) * 32]
        return carry

    lines = soft_ref.shape[0]

    def score():
        off_diagonal = iota((span, span), 0) != iota((span, span), 1)
        first = jnp.where(iota((16, 128), 1) == 0, 1.0, 0.0).astype(BF16)
        source = iota((span, 128), 0) // 2
        lane = iota((span, 128), 1) - source // lines * 8 - iota((span, 128), 0) % 2
        soft = jnp.zeros((span, 128), F32)
        for c in range(owned):
            soft = score_one(c, soft, off_diagonal, first, lane)
        pick = jnp.where(iota((lines, span), 1) // 2 % lines == iota((lines, span), 0), 1.0, 0.0).astype(BF16)
        spread = jnp.dot(pick, soft.astype(BF16), preferred_element_type=F32)
        soft_ref[...] = spread.reshape(soft_ref.shape)

    def score_one(c, soft, off_diagonal, first, lane):
        sharp = sharp_ref[me * owned + c]
        rows = members[c]
        marks = lax.dot_general(first, rows[:, :128], NT, preferred_element_type=F32)[:1]
        dots = lax.dot_general(rows, rows, NT, preferred_element_type=F32)
        masked = jnp.where(off_diagonal & (marks < EMPTY / 2), dots * (sharp * (1.0 / features)), NEGATIVE)
        highest = jnp.maximum(jnp.max(masked, axis=1, keepdims=True), 0.0)
        weights = jnp.exp(masked - highest)
        total = jnp.exp(-highest) + jnp.sum(weights, axis=1, keepdims=True)
        soft = jnp.where(lane == 2 * c, (highest + jnp.log(total)) / sharp, soft)
        summed = jnp.dot(weights.astype(BF16), rows, preferred_element_type=F32)
        results[c] = (summed * (1.0 / total)).astype(BF16)
        return soft

    def scatter(b, carry):
        rows = pl.ds(pl.multiple_of(b * 32, 32), 32)
        placed = jnp.concatenate(
            [results[c, rows, :half] for c in range(owned)] + [results[c, rows, half:] for c in range(owned)],
            axis=0,
        )
        back = jnp.dot(outward, placed, preferred_element_type=F32)
        out_ref[pl.ds(pl.multiple_of(b * 256, 256), 256), :] = back.astype(BF16)
        return carry

    return gather, score, scatter


def settle_kernel(sharp_ref, in_ref, out_ref, soft_ref, members, results):
    gather, score, scatter = settle_parts(sharp_ref, in_ref, out_ref, soft_ref, members, results)
    steps = members.shape[1] // 32
    lax.fori_loop(0, steps, gather, 0, unroll=4)
    score()
    lax.fori_loop(0, steps, scatter, 0, unroll=4)


def settle(sharp, arrived, n, owned):
    rows, half = arrived.shape
    span = n * SRC_CAP
    return pl.pallas_call(
        settle_kernel,
        in_specs=[pl.BlockSpec(memory_space=pltpu.SMEM), pl.BlockSpec(memory_space=pltpu.VMEM)],
        out_specs=[pl.BlockSpec(memory_space=pltpu.VMEM)] * 2,
        out_shape=[
            jax.ShapeDtypeStruct((rows, half), BF16),
            jax.ShapeDtypeStruct((n, 1, 128), F32),
        ],
        scratch_shapes=[
            pltpu.VMEM((owned, span, half * 2), BF16),
            pltpu.VMEM((owned, span, half * 2), BF16),
        ],
        compiler_params=pltpu.CompilerParams(vmem_limit_bytes=40 * 2**20),
        name="settle",
    )(sharp, arrived)


def unpack_kernel(dest_ref, in_ref, soft_in_ref, soft_ref, out_ref, combined, soft_all):
    step = pl.program_id(0)
    slots, features = combined.shape
    half = features // 2
    n = soft_in_ref.shape[0]
    rows = out_ref.shape[0]

    @pl.when(step == 0)
    def _():
        def split(b, carry):
            block = in_ref[pl.ds(pl.multiple_of(b * 512, 512), 512), :].astype(F32).reshape(32, 2, 8, half)
            place = pl.ds(pl.multiple_of(b * 256, 256), 256)
            combined[place, :half] = block[:, 0].reshape(256, half).astype(BF16)
            combined[place, half:] = block[:, 1].reshape(256, half).astype(BF16)
            return carry

        lax.fori_loop(0, slots // 256, split, 0)
        soft_all[...] = jnp.transpose(soft_in_ref[...].reshape(n, 128)).astype(BF16)

    dest = dest_ref[...]
    column = as_column(dest.astype(F32))
    lane = iota((rows, 128), 1).astype(F32)
    hit = jnp.concatenate(
        [jnp.where(column == lane + float(s), 1.0, 0.0).astype(BF16) for s in range(0, slots, 128)], axis=1
    )
    out_ref[...] = jnp.dot(hit, combined[...], preferred_element_type=F32).astype(BF16)

    owner = jnp.where(iota((n, rows), 0) == dest // 8, 1.0, 0.0).astype(BF16)
    found = jnp.dot(soft_all[...], owner, preferred_element_type=F32)[:8]
    chosen = jnp.where(iota((8, rows), 0) == dest % 8, found, 0.0)
    soft_ref[...] = jnp.sum(chosen, axis=0, keepdims=True).astype(BF16)


def unpack(dest, returned, soft_returned):
    count = dest.shape[1]
    n = soft_returned.shape[0]
    blocks, half = returned.shape
    slots, features = blocks // 2, half * 2
    rows = 256
    return pl.pallas_call(
        unpack_kernel,
        grid=(count // rows,),
        in_specs=[
            pl.BlockSpec((1, rows), lambda i: (0, i)),
            pl.BlockSpec((blocks, half), lambda i: (0, 0)),
            pl.BlockSpec((n, 1, 128), lambda i: (0, 0, 0)),
        ],
        out_specs=[
            pl.BlockSpec((1, rows), lambda i: (0, i)),
            pl.BlockSpec((rows, features), lambda i: (i, 0)),
        ],
        out_shape=[
            jax.ShapeDtypeStruct((1, count), BF16),
            jax.ShapeDtypeStruct((count, features), BF16),
        ],
        scratch_shapes=[pltpu.VMEM((slots, features), BF16), pltpu.VMEM((128, n), BF16)],
        compiler_params=pltpu.CompilerParams(vmem_limit_bytes=40 * 2**20),
        name="unpack",
    )(dest, returned, soft_returned)


PLANES = 8
LINES = 32
CAP = 160
BLOCK = 16


def blocks(ref, start, count):
    return ref.at[pl.ds(pl.multiple_of(start * BLOCK, BLOCK), count * BLOCK)]


def near_first(k):
    near = k // 2 + 1
    return near + (k % 2) * (PLANES - 2 * near)


def far_first(k):
    near = 4 - (k + 1) // 2
    return near + ((k + 1) % 2) * (PLANES - 2 * near)


def place():
    g, d = lax.axis_index("group"), lax.axis_index("dev")
    return g, d // PLANES, d % PLANES


def other_lines(g, x):
    ys = [(g // 2 + i) % 4 for i in range(4)]
    cores = [(g % 2 + i) % 2 for i in range(2)]
    xs = [(x + i) % 4 for i in range(4)]
    mixed = [(j * 11) % LINES for j in range(1, LINES)]
    return [(ys[q // 2 % 4] * 2 + cores[q % 2], xs[q // 8]) for q in mixed]


def greet_all(g, x, z):
    barrier = pltpu.get_barrier_semaphore()

    def greet_z(k, carry):
        there = (g, x * PLANES + (z + k) % PLANES)
        pl.semaphore_signal(barrier, inc=1, device_id=there, device_id_type=MESH)
        return carry

    lax.fori_loop(1, PLANES, greet_z, 0)
    for tg, tx in other_lines(g, x):
        pl.semaphore_signal(barrier, inc=1, device_id=(tg, tx * PLANES + z), device_id_type=MESH)
    return barrier


def relay_copies(rows_out, relay_in, rows_in, send_sems, recv_sems, g, x, z, source_at):
    def first_leg():
        copies = []
        for way, hop in enumerate((2, PLANES - 2)):
            half = pl.ds(way * (CAP // 2), CAP // 2)
            copies.append(pltpu.make_async_remote_copy(
                src_ref=rows_out.at[(z + 4) % PLANES, half], dst_ref=relay_in.at[way],
                send_sem=send_sems.at[way], recv_sem=recv_sems.at[way],
                device_id=(g, x * PLANES + (z + hop) % PLANES), device_id_type=MESH))
        return copies

    def second_leg():
        copies = []
        for way, hop in enumerate((2, PLANES - 2)):
            half = pl.ds(way * (CAP // 2), CAP // 2)
            source = (z + PLANES - hop) % PLANES
            copies.append(pltpu.make_async_remote_copy(
                src_ref=relay_in.at[way], dst_ref=rows_in.at[source, half],
                send_sem=send_sems.at[2 + way], recv_sem=source_at(source),
                device_id=(g, x * PLANES + (z + hop) % PLANES), device_id_type=MESH))
        return copies

    def pass_on():
        for way, copy in enumerate(second_leg()):
            came = relay_in.at[way]
            pltpu.make_async_copy(came, came, recv_sems.at[way]).wait()
            copy.start()

    def finish():
        for copy in first_leg() + second_leg():
            copy.wait_send()

    return first_leg, pass_on, finish


def collect_kernel(ids_ref, x_any, x_sem, x_ref, inbox, where_ref, slots_in, hits, rows_out, rows_in, relay_in, slots_out, line_out,
                   z_send, z_recv, relay_send, relay_recv, line_send, line_recv, own_sem, gather):
    g, x, z = place()
    lines = other_lines(g, x)
    count, features = x_ref.shape
    half = features // 2
    x_copy = pltpu.make_async_copy(x_any, x_ref, x_sem)
    x_copy.start()
    barrier = greet_all(g, x, z)

    ids = ids_ref[...]
    columns = as_column(ids.astype(F32)).astype(jnp.int32)
    plane = jnp.right_shift(ids, 2) & (PLANES - 1)
    plane_columns = jnp.right_shift(columns, 2) & (PLANES - 1)
    before = iota((128, 128), 0) < iota((128, 128), 1)
    ordinal, position = [], []
    for t in range(0, count, 128):
        same = jnp.zeros((128, 128), F32)
        beside = jnp.zeros((128, 128), F32)
        for r in range(0, t + 128, 128):
            alike = columns[r:r + 128] == ids[:, t:t + 128]
            near = plane_columns[r:r + 128] == plane[:, t:t + 128]
            if r == t:
                alike, near = alike & before, near & before
            same += jnp.where(alike, 1.0, 0.0)
            beside += jnp.where(near, 1.0, 0.0)
        ordinal.append(jnp.sum(same, axis=0, keepdims=True))
        position.append(jnp.sum(beside, axis=0, keepdims=True))
    ordinal, position = jnp.concatenate(ordinal, axis=1), jnp.concatenate(position, axis=1)
    where_ref[...] = jnp.concatenate([plane.astype(F32), position, jnp.zeros((6, count), F32)], axis=0)
    flag = jnp.where(jnp.max(position) > CAP - 0.5, 1.0, 0.0)
    slot = (jnp.right_shift(ids, 5) * 8 + (ids & 3) * SRC_CAP).astype(F32) + ordinal + 1.0
    slot = jnp.broadcast_to(slot, (16, count)).astype(BF16)
    hits[CAP:, :] = jnp.zeros((256 - CAP, count), BF16)
    key = jnp.where(position < CAP - 0.5, position.astype(jnp.int32) * PLANES + plane, -1)

    def compact(there):
        hits[:CAP, :] = jnp.where(iota((CAP, count), 0) * PLANES + there == key, 1.0, 0.0).astype(BF16)
        rows = jnp.dot(hits[:CAP, :], x_ref[...], preferred_element_type=F32).astype(BF16)
        names = lax.dot_general(slot, hits[...], NT, preferred_element_type=F32)[:1]
        return rows, jnp.where(iota((1, 256), 1) == 255, flag, names)

    def z_copy(out, into, i, there):
        return pltpu.make_async_remote_copy(
            src_ref=out.at[there], dst_ref=into.at[z], send_sem=z_send.at[i], recv_sem=z_recv.at[i, z],
            device_id=(g, x * PLANES + there), device_id_type=MESH)

    first_leg, pass_on, finish_relay = relay_copies(
        rows_out, relay_in, rows_in, relay_send, relay_recv, g, x, z, lambda source: z_recv.at[0, source])

    def prepare(there):
        rows, names = compact(there)
        rows_out[there] = rows
        slots_out[there] = names

    def send_z(k, carry):
        there = (z + near_first(k)) % PLANES
        prepare(there)
        z_copy(rows_out, rows_in, 0, there).start()
        z_copy(slots_out, slots_in, 1, there).start()
        return carry

    opposite = (z + 4) % PLANES
    x_copy.wait()
    pl.semaphore_wait(barrier, PLANES + LINES - 2)
    prepare(opposite)
    for copy in first_leg():
        copy.start()
    z_copy(slots_out, slots_in, 1, opposite).start()
    lax.fori_loop(0, PLANES - 2, send_z, 0)
    rows, names = compact(z)
    rows_in[z] = rows
    slots_in[z] = names

    def own_copy(source):
        return pltpu.make_async_copy(
            blocks(line_out, source * LINES + g * 4 + x, 1), blocks(inbox, source * LINES + g * 4 + x, 1),
            own_sem.at[source])

    def forward(source):
        wide = rows_in[source].astype(F32)
        scale = lax.rsqrt(jnp.mean(wide * wide, axis=-1, keepdims=True) + 1e-06)
        names = slots_in[source][:, :CAP].astype(jnp.int32) - 1
        hit = jnp.where(iota((256, CAP), 0) == names, 1.0, 0.0)
        filled = jnp.sum(hit, axis=1, keepdims=True)
        rows = jnp.dot(hit.astype(BF16), (wide * scale).astype(BF16), preferred_element_type=F32)
        first = jnp.where((iota((256, 128), 1) == 0) & (filled < 0.5), EMPTY, rows[:, :128])
        left = jnp.concatenate([first, rows[:, 128:half]], axis=1).reshape(LINES, 1, 8, half)
        right = rows[:, half:].reshape(LINES, 1, 8, half)
        both = jnp.concatenate([left, right], axis=1).reshape(512, half)
        line_out[pl.ds(pl.multiple_of(source * 512, 512), 512), :] = both.astype(BF16)
        own_copy(source).start()

        for tg, tx in lines:
            pltpu.make_async_remote_copy(
                src_ref=blocks(line_out, source * LINES + tg * 4 + tx, 1),
                dst_ref=blocks(inbox, source * LINES + g * 4 + x, 1),
                send_sem=line_send, recv_sem=line_recv.at[source],
                device_id=(tg, tx * PLANES + z), device_id_type=MESH).start()

    forward(z)
    pass_on()

    def arrive(k, carry):
        source = (z + PLANES - near_first(k)) % PLANES
        pltpu.make_async_copy(rows_in.at[source], rows_in.at[source], z_recv.at[0, source]).wait()
        pltpu.make_async_copy(slots_in.at[source], slots_in.at[source], z_recv.at[1, source]).wait()
        forward(source)
        return carry

    lax.fori_loop(0, PLANES - 1, arrive, 0)

    def complete(source):
        came = blocks(inbox, source * LINES, LINES - 1)
        pltpu.make_async_copy(came, came, line_recv.at[source]).wait()
        own_copy(source).wait()
        gather(source * 2, 0)
        gather(source * 2 + 1, 0)

    def complete_next(k, carry):
        complete((z + PLANES - near_first(k)) % PLANES)
        return carry

    complete(z)
    lax.fori_loop(0, PLANES - 1, complete_next, 0)
    others = PLANES * (LINES - 1)
    sent = rows_out.at[pl.ds(0, PLANES - 2)]
    pltpu.make_async_copy(sent, sent, z_send.at[0]).wait()
    sent = slots_out.at[pl.ds(0, PLANES - 1)]
    pltpu.make_async_copy(sent, sent, z_send.at[1]).wait()
    finish_relay()
    pltpu.make_async_copy(blocks(line_out, 0, others), blocks(line_out, 0, others), line_send).wait()


def restore_kernel(results, soft_ref, slots_ref, rows_back, soft_back, flag_ref, line_in, soft_out, soft_in, rows_out,
                   relay_in, names_out, z_send, z_recv, relay_send, relay_recv, line_send, line_recv, soft_sem, own_sem, scatter, meanwhile):
    g, x, z = place()
    lines = other_lines(g, x)
    me = g * 4 + x
    half = results.shape[1]
    flag = jnp.max(jnp.where(iota((PLANES, 1, 256), 2) == 255, slots_ref[...], 0.0))
    soft_out[...] = jnp.where(iota(soft_out.shape, 2) < 64, soft_ref[...], flag)
    soft_in[me] = soft_out[me]

    def own_copy(home):
        return pltpu.make_async_copy(
            blocks(results, home * LINES + me, 1), blocks(line_in, home * LINES + me, 1), own_sem.at[home])

    def home_of(k):
        return (z + far_first(k)) % PLANES

    def send_line(k, carry):
        home = home_of(k)
        scatter(home * 2, 0)
        scatter(home * 2 + 1, 0)
        own_copy(home).start()

        for tg, tx in lines:
            pltpu.make_async_remote_copy(
                src_ref=blocks(results, home * LINES + tg * 4 + tx, 1),
                dst_ref=blocks(line_in, home * LINES + me, 1),
                send_sem=line_send, recv_sem=line_recv.at[home],
                device_id=(tg, tx * PLANES + z), device_id_type=MESH).start()
        return carry

    lax.fori_loop(0, 3, send_line, 0)
    for tg, tx in lines:
        pltpu.make_async_remote_copy(
            src_ref=soft_out.at[tg * 4 + tx], dst_ref=soft_in.at[me], send_sem=soft_sem.at[0],
            recv_sem=soft_sem.at[1], device_id=(tg, tx * PLANES + z), device_id_type=MESH).start()
    first = soft_in.at[pl.ds(0, LINES - 1)]
    pltpu.make_async_copy(first, first, soft_sem.at[1]).wait()
    all_soft = soft_in[...].reshape(LINES, 128)
    flag_ref[...] = jnp.broadcast_to(jnp.max(all_soft[:, 64:], axis=(0, 1), keepdims=True), flag_ref.shape)
    spread = jnp.where(iota((256, LINES), 0) // 8 == iota((256, LINES), 1), 1.0, 0.0).astype(BF16)
    all_soft = jnp.dot(spread, all_soft.astype(BF16), preferred_element_type=F32)

    def settle_home(home):
        arrived = blocks(line_in, home * LINES, LINES - 1)
        pltpu.make_async_copy(arrived, arrived, line_recv.at[home]).wait()
        own_copy(home).wait()
        both = line_in[pl.ds(pl.multiple_of(home * 512, 512), 512), :].astype(F32).reshape(LINES, 2, 8, half)
        left, right = both[:, 0].reshape(256, half).astype(BF16), both[:, 1].reshape(256, half).astype(BF16)
        names = slots_ref[home]
        column = as_column(names)[:CAP] - 1.0
        lane = iota((CAP, 128), 1).astype(F32)
        hit = jnp.concatenate(
            [jnp.where(column == lane + float(s), 1.0, 0.0).astype(BF16) for s in (0, 128)], axis=1)
        mine = jnp.where(iota((256, 128), 1) == home * 8 + iota((256, 128), 0) % 8, all_soft, 0.0).astype(BF16)
        values = lax.dot_general(jnp.ones((16, 128), BF16), mine, NT, preferred_element_type=F32)
        picked = jnp.where(iota((256, 256), 0) == names.astype(jnp.int32) - 1, 1.0, 0.0).astype(BF16)
        picked = jnp.dot(values.astype(BF16), picked, preferred_element_type=F32)[:1]
        left = jnp.dot(hit, left, preferred_element_type=F32).astype(BF16)
        right = jnp.dot(hit, right, preferred_element_type=F32).astype(BF16)
        return left, right, picked

    first_leg, pass_on, finish_relay = relay_copies(
        rows_out, relay_in, rows_back, relay_send, relay_recv, g, x, z, lambda source: z_recv.at[0])

    def z_copy(out, into, i, home):
        return pltpu.make_async_remote_copy(
            src_ref=out.at[home], dst_ref=into.at[z], send_sem=z_send.at[i], recv_sem=z_recv.at[i],
            device_id=(g, x * PLANES + home), device_id_type=MESH)

    def send_z(k, carry):
        home = home_of(k)
        left, right, picked = settle_home(home)
        rows_out[home, :, :half] = left
        rows_out[home, :, half:] = right
        names_out[home] = picked
        z_copy(names_out, soft_back, 1, home).start()

        @pl.when(k == 0)
        def _():
            for copy in first_leg():
                copy.start()

        @pl.when(k > 0)
        def _():
            z_copy(rows_out, rows_back, 0, home).start()

        @pl.when(k == 2)
        def _():
            pass_on()

        @pl.when(k < PLANES - 3)
        def _():
            send_line(k + 3, 0)

        return carry

    lax.fori_loop(0, PLANES - 1, send_z, 0)
    left, right, picked = settle_home(z)
    rows_back[z, :, :half] = left
    rows_back[z, :, half:] = right
    soft_back[z] = picked

    meanwhile()
    others = PLANES * (LINES - 1)
    sent = soft_out.at[pl.ds(0, LINES - 1)]
    pltpu.make_async_copy(sent, sent, soft_sem.at[0]).wait()
    pltpu.make_async_copy(blocks(results, 0, others), blocks(results, 0, others), line_send).wait()
    sent = rows_out.at[pl.ds(0, PLANES - 2)]
    pltpu.make_async_copy(sent, sent, z_send.at[0]).wait()
    sent = names_out.at[pl.ds(0, PLANES - 1)]
    pltpu.make_async_copy(sent, sent, z_send.at[1]).wait()
    finish_relay()
    for i, into in enumerate((rows_back, soft_back)):
        came = into.at[pl.ds(0, PLANES - 1)]
        pltpu.make_async_copy(came, came, z_recv.at[i]).wait()


def find_spots(where_ref, spots):
    for r in range(0, spots.shape[0], 256):
        plane, position = where_ref[0:1, r:r + 256], where_ref[1:2, r:r + 256]
        column = as_column(plane * CAP + position)
        lane = iota((256, 128), 1).astype(F32)
        for t in range(0, spots.shape[1], 128):
            spots[r:r + 256, t:t + 128] = jnp.where(column == lane + float(t), 1.0, 0.0).astype(BF16)


def place_kernel(spots, where_ref, in_ref, soft_in_ref, soft_ref, out_ref):
    rows = out_ref.shape[0]
    plane, position = where_ref[0:1, :], where_ref[1:2, :]
    combined = in_ref[...].reshape(PLANES * CAP, in_ref.shape[2])
    out_ref[...] = jnp.dot(spots[...], combined, preferred_element_type=F32).astype(BF16)

    spot = jnp.where(iota((256, rows), 0).astype(F32) == position, 1.0, 0.0).astype(BF16)
    soft = soft_in_ref[...].reshape(PLANES, 256)
    soft = jnp.concatenate([soft, jnp.zeros((8, 256), F32)], axis=0).astype(BF16)
    found = jnp.dot(soft, spot, preferred_element_type=F32)[:PLANES]
    chosen = jnp.where(iota((PLANES, rows), 0).astype(F32) == plane, found, 0.0)
    soft_ref[...] = jnp.sum(chosen, axis=0, keepdims=True).astype(BF16)


def whole_kernel(sharp_ref, ids_ref, x_any, soft_max, neighbour, flag_ref, inbox, where_ref, slots_in, hits,
                 rows_out, rows_in, relay_in, slots_out, line_out, members, results, soft, line_in, soft_out, soft_in,
                 back_out, back_in, relay_back, names_out, names_in, z_send, z_recv, relay_send, relay_recv, line_send,
                 line_recv, own_sem, z_send_b, z_recv_b, relay_send_b, relay_recv_b, line_send_b, line_recv_b, soft_sem,
                 own_sem_b, x_ref, x_sem, spots):
    gather, score, scatter = settle_parts(sharp_ref, inbox, line_out, soft, members, results)
    collect_kernel(ids_ref, x_any, x_sem, x_ref, inbox, where_ref, slots_in, hits, rows_out, rows_in, relay_in, slots_out, line_out,
                   z_send, z_recv, relay_send, relay_recv, line_send, line_recv, own_sem,
                   gather)
    score()
    restore_kernel(line_out, soft, slots_in, back_in, names_in, flag_ref, line_in, soft_out, soft_in, back_out,
                   relay_back, names_out, z_send_b, z_recv_b, relay_send_b, relay_recv_b, line_send_b, line_recv_b,
                   soft_sem, own_sem_b, scatter, lambda: find_spots(where_ref, spots))
    for r in range(0, neighbour.shape[0], 256):
        rows = pl.ds(r, 256)
        place_kernel(spots.at[rows], where_ref.at[:, rows], back_in, names_in, soft_max.at[:, rows], neighbour.at[rows])


def whole(sharp, ids, x):
    count, features = x.shape
    half = features // 2
    slots = PLANES * LINES * BLOCK
    vmem = pl.BlockSpec(memory_space=pltpu.VMEM)
    lines = pltpu.VMEM((slots, half), BF16)
    rows = pltpu.VMEM((PLANES, CAP, features), BF16)
    halves = pltpu.VMEM((2, CAP // 2, features), BF16)
    names = pltpu.VMEM((PLANES, 1, 256), F32)
    soft = pltpu.VMEM((LINES, 1, 128), F32)
    members = pltpu.VMEM((4, slots // 8, features), BF16)
    dma = pltpu.SemaphoreType.DMA
    return pl.pallas_call(
        whole_kernel,
        in_specs=[pl.BlockSpec(memory_space=pltpu.SMEM), vmem, pl.BlockSpec(memory_space=pl.ANY)],
        out_specs=[vmem] * 3,
        out_shape=[
            jax.ShapeDtypeStruct((1, count), BF16),
            jax.ShapeDtypeStruct((count, features), BF16),
            jax.ShapeDtypeStruct((8, 128), F32),
        ],
        scratch_shapes=[
            lines, pltpu.VMEM((8, count), F32), names, pltpu.VMEM((256, count), BF16),
            rows, rows, halves, names, lines, members, members, soft, lines, soft, soft,
            rows, rows, halves, names, names,
            dma((2,)), dma((2, PLANES)), dma((4,)), dma((2,)), dma, dma((PLANES,)), dma((PLANES,)),
            dma((2,)), dma((2,)), dma((4,)), dma((2,)), dma, dma((PLANES,)), dma((2,)), dma((PLANES,)),
            pltpu.VMEM((count, features), BF16), dma, pltpu.VMEM((count, PLANES * CAP), BF16),
        ],
        compiler_params=pltpu.CompilerParams(
            collective_id=2, has_side_effects=True, vmem_limit_bytes=48 * 2**20),
        name="whole",
    )(sharp, ids, x)


def by_all_slots(n, embeddings, cluster_ids, sharp):
    clusters = sharp.shape[0]
    outbox, dest = pack(cluster_ids[None, :], embeddings, clusters * SRC_CAP)
    (arrived,) = exchange(n, 0, outbox)
    results, soft = settle(sharp, arrived, n, clusters // n)
    returned, soft_returned = exchange(n, 1, results, soft)
    return unpack(dest, returned, soft_returned)


def body(n, embeddings, cluster_ids, sharpness):
    sharp = sharpness.astype(F32)
    soft_max, neighbour, flag = whole(sharp, cluster_ids[None, :], embeddings)
    soft_max, neighbour = lax.cond(
        flag[0, 0] > 0.5,
        lambda: tuple(by_all_slots(n, embeddings, cluster_ids, sharp)),
        lambda: (soft_max, neighbour),
    )
    return (soft_max[0], neighbour)


def solution(mesh):
    n = mesh.size
    return jax.shard_map(
        functools.partial(body, n),
        mesh=mesh,
        in_specs=(P(("group", "dev"), None), P(("group", "dev")), P()),
        out_specs=(P(("group", "dev")), P(("group", "dev"), None)),
        check_vma=False,
    )
```
